32 devices in a mesh: section: 2 (over core), dp: 16 (over z, y, x).
Axes of the slice: x: 2, y: 2, z: 4, core: 2. Of those that a mesh axis runs over, the one named last changes fastest.
Arguments:
- section_in: bfloat16 [2, 32768, 512], P('section', 'dp'), may hold values from -6 to 6
- ln1_gain: float32 [2, 512], P('section'), may hold values from 0.5 to 1.5
- ln1_shift: float32 [2, 512], P('section'), may hold values from -2 to 2
- qkv_weight: bfloat16 [2, 512, 1536], P('section'), may hold values from -0.25 to 0.25
- out_weight: bfloat16 [2, 512, 512], P('section'), may hold values from -1.5 to 1.5
- ln2_gain: float32 [2, 512], P('section'), may hold values from 0.5 to 1.5
- ln2_shift: float32 [2, 512], P('section'), may hold values from -2 to 2
- up_weight: bfloat16 [2, 512, 2048], P('section'), may hold values from -0.25 to 0.25
- up_shift: float32 [2, 2048], P('section'), may hold values from -3 to 3
- down_weight: bfloat16 [2, 2048, 512], P('section'), may hold values from -0.125 to 0.125
- final_gain: float32 [2, 512], P('section'), may hold values from 0.5 to 1.5
- final_shift: float32 [2, 512], P('section'), may hold values from -2 to 2
- bridge_weight: bfloat16 [2, 32, 512], P('section'), may hold values from -0.25 to 0.25
- codebook: float32 [32, 8192], P(None, ('section', 'dp')), may hold values from -6 to 6
- codes: int32 [32768], P('dp'), may hold values from 0 to 8191
- doc_lengths: int32 [64, 4], P('dp'), may hold values from 1 to 256, 512 in all within a row
Outputs:
- section_out: bfloat16 [2, 32768, 512], P('section', 'dp')
- grad_ln1_gain: float32 [2, 512], P('section')
- grad_ln1_shift: float32 [2, 512], P('section')
- grad_qkv_weight: float32 [2, 512, 1536], P('section')
- grad_out_weight: float32 [2, 512, 512], P('section')
- grad_ln2_gain: float32 [2, 512], P('section')
- grad_ln2_shift: float32 [2, 512], P('section')
- grad_up_weight: float32 [2, 512, 2048], P('section')
- grad_up_shift: float32 [2, 2048], P('section')
- grad_down_weight: float32 [2, 2048, 512], P('section')
- grad_final_gain: float32 [2, 512], P('section')
- grad_final_shift: float32 [2, 512], P('section')
- grad_bridge_weight: float32 [2, 32, 512], P('section')
- grad_codebook: float32 [32, 8192], P(None, ('section', 'dp'))
The draws below stay inside these ranges and needn't reach their ends.
Inputs may be any that keep to these rules, and one draw needn't show every extreme that they name: `doc_lengths`: each row holds, in order, the lengths of the documents packed into one group of 512 tokens; a row sums to 512.
All inputs are finite; a program needn't handle non-finite values.
Results may differ from the reference program's by a relative error of at most 0.014.
Values may be sent and summed in bfloat16 or wider, within the bound.
No kernel may reach another device: no remote copies, remote signals or barrier semaphores. Data moves between devices by JAX's collectives and lax.ppermute only.
A program may use at most 192 MiB of HBM per device.

```python
import math
import jax
import jax.numpy as jnp
import numpy as np
from jax import lax

D = 512
HEADS = 8
HEAD_DIM = 64
FF = 2048
LATENT = 32
CODES = 8192
MB_TOK = 512
DOCS = 4
TOKENS = 32768
GROUPS = 64


def touch_ends(array, rng, least, high):
    dims = array.shape
    place = [jax.random.randint(jax.random.fold_in(rng, axis), (), 0, dims[axis]) for axis in range(len(dims))]
    array = array.at[tuple(place)].set(least)
    longest = dims.index(max(dims))
    place[longest] = (place[longest] + 1) % dims[longest]
    return array.at[tuple(place)].set(high)


def steps_of(key, shape, cuts, least, top_value):
    loudness = 1.0
    for position, shards_of in cuts:
        steps = jax.random.uniform(jax.random.fold_in(jax.random.fold_in(key, 6), position), (shards_of,), jnp.float32, least / len(cuts), top_value / len(cuts))
        loudness = loudness * jnp.repeat(jnp.exp(steps), shape[position] // shards_of).reshape((-1,) + (1,) * (len(shape) - 1 - position))
    return loudness


def split_up(count, total, reach, skew):
    portions = [(1 << 20) // math.isqrt(standing ** skew) + 1 for standing in range(2, count + 1)]
    rest, counts = total - reach - (count - 1), [1] * (count - 1)
    while rest > 0:
        candidates = [i for i in range(count - 1) if counts[i] < reach]
        mass, remaining = sum([portions[i] for i in candidates]), rest
        for i in candidates:
            addition = min(reach - counts[i], max(1, remaining * portions[i] // mass), rest)
            counts[i] = counts[i] + addition
            rest = rest - addition
    return np.array([reach] + counts)


def ragged_sizes(key, amount, total, reach, slope):
    if amount == 2:
        one = jax.random.randint(key, (), max(1, total - reach), min(reach, total - 1) + 1)
        return jnp.stack([one, total - one])
    sizes = jnp.asarray(split_up(amount, total, reach, slope), jnp.int32)
    twos = (amount - 1) // 2
    donor, sink = sizes[1:1 + 2 * twos:2], sizes[2:2 + 2 * twos:2]
    margin = jnp.minimum(donor - 1, reach - sink)
    shifted = jax.random.randint(jax.random.fold_in(key, 1), (twos,), 0, 1 << 20) % (margin + 1)
    sizes = sizes.at[1:1 + 2 * twos:2].set(donor - shifted).at[2:2 + 2 * twos:2].set(sink + shifted)
    return sizes[jax.random.permutation(jax.random.fold_in(key, 2), amount)]


def gaussian(own_key, extent, deviation, limit, cuts=(), held_as=jnp.bfloat16):
    values = jax.random.normal(own_key, extent, jnp.float32) * deviation
    if len(cuts) > 0:
        values = steps_of(own_key, extent, cuts, -0.22, 0.18) * values
    return jnp.clip(values, min=-limit, max=limit).astype(held_as)


def setup_inputs(seed: int = 0) -> dict:
    splits = jax.random.split(jax.random.key(seed), 17)
    return {
        "section_in": gaussian(splits[0], (2, TOKENS, D), 1.0, 6.0, ((0, 2), (1, 16))),
        "ln1_gain": jnp.clip(1.0 + 0.1 * jax.random.normal(splits[1], (2, D), jnp.float32), 0.5, 1.5),
        "ln1_shift": gaussian(splits[2], (2, D), 0.3, 2.0, ((0, 2),), jnp.float32),
        "qkv_weight": gaussian(splits[3], (2, D, 3 * D), D ** -0.5, 0.25, ((0, 2),)),
        "out_weight": gaussian(splits[4], (2, D, D), (D // 32) ** -0.5, 1.5, ((0, 2),)),
        "ln2_gain": jnp.clip(1.0 + 0.1 * jax.random.normal(splits[5], (2, D), jnp.float32), 0.5, 1.5),
        "ln2_shift": gaussian(splits[6], (2, D), 0.3, 2.0, ((0, 2),), jnp.float32),
        "up_weight": gaussian(splits[7], (2, D, FF), D ** -0.5, 0.25, ((0, 2),)),
        "up_shift": gaussian(splits[8], (2, FF), 0.5, 3.0, ((0, 2),), jnp.float32),
        "down_weight": gaussian(splits[9], (2, FF, D), FF ** -0.5, 0.125, ((0, 2),)),
        "final_gain": jnp.clip(1.0 + 0.1 * jax.random.normal(splits[10], (2, D), jnp.float32), 0.5, 1.5),
        "final_shift": gaussian(splits[11], (2, D), 0.3, 2.0, ((0, 2),), jnp.float32),
        "bridge_weight": gaussian(splits[12], (2, LATENT, D), D ** -0.5, 0.25, ((0, 2),)),
        "codebook": gaussian(splits[13], (LATENT, CODES), 1.0, 6.0, ((1, 32),), jnp.float32),
        "codes": touch_ends(jax.random.randint(splits[14], (TOKENS,), 0, CODES), jax.random.fold_in(splits[14], 1), 0, CODES - 1).astype(jnp.int32),
        "doc_lengths": jax.vmap(lambda own: ragged_sizes(own, DOCS, MB_TOK, MB_TOK // 2, 2))(jax.random.split(splits[15], GROUPS)).reshape((GROUPS, DOCS)).astype(jnp.int32),
    }


@jax.custom_vjp
def low(v):
    return lax.optimization_barrier(v.astype(jnp.bfloat16)).astype(jnp.float32)

@jax.custom_vjp
def low_back(v):
    return v

def low_keep(v):
    return (low(v), None)

def low_pass(kept, grad):
    return (grad,)

def back_keep(v):
    return (v, None)

def back_low(kept, grad):
    return (low(grad),)
low.defvjp(low_keep, low_pass)
low_back.defvjp(back_keep, back_low)
norm_epsilon = 1e-06

def matmul(left, right):
    return jnp.dot(left, right, precision=lax.Precision.HIGHEST, preferred_element_type=jnp.float32)

def layer_norm(inputs, gain, shift):
    centred = inputs - lax.optimization_barrier(jnp.mean(inputs, axis=-1, keepdims=True))
    scaled = centred * lax.rsqrt(lax.optimization_barrier(jnp.mean(centred * centred, axis=-1, keepdims=True)) + norm_epsilon)
    return scaled * gain + shift

def unit_rows(inputs):
    return inputs * lax.rsqrt(lax.optimization_barrier(jnp.sum(inputs * inputs, axis=-1, keepdims=True)) + norm_epsilon)

def same_segment(lengths, row_count):
    bounds = jnp.cumsum(lengths, dtype=jnp.int32)
    places = jnp.arange(row_count, dtype=jnp.int32)
    labels = lax.optimization_barrier(jnp.sum((places[:, None] >= bounds[None, :]).astype(jnp.int32), axis=1, dtype=jnp.int32))
    return labels[:, None] == labels[None, :]

def block(inputs, params, section_side, same_doc):
    ln1_gain, ln1_shift, qkv_weight, out_weight, ln2_gain, ln2_shift, up_weight, up_shift, down_weight = [member[section_side] for member in params[:9]]
    row_count = inputs.shape[0]
    normed = low(layer_norm(inputs, ln1_gain, ln1_shift))
    projected = low_back(low(matmul(normed, qkv_weight)))
    queries = projected[:, :D].reshape(row_count, HEADS, HEAD_DIM)
    key_heads = projected[:, D:2 * D].reshape(row_count, HEADS, HEAD_DIM)
    value_heads = projected[:, 2 * D:].reshape(row_count, HEADS, HEAD_DIM)
    scores = jnp.einsum('thd,shd->hts', queries, key_heads, precision=lax.Precision.HIGHEST) * HEAD_DIM ** (-0.5)
    scores = low_back(jnp.where(same_doc[None], scores, -1000000000.0))
    row_peak = lax.optimization_barrier(jnp.max(scores, axis=-1, keepdims=True))
    exp_scores = jnp.exp(scores - row_peak)
    attention = low(exp_scores / lax.optimization_barrier(jnp.sum(exp_scores, axis=-1, keepdims=True)))
    mixed_heads = jnp.einsum('hts,shd->thd', attention, value_heads, precision=lax.Precision.HIGHEST)
    mixed_heads = low_back(low(mixed_heads.reshape(row_count, D)))
    middle = inputs + low_back(matmul(mixed_heads, out_weight))
    normed_two = low(layer_norm(middle, ln2_gain, ln2_shift))
    hidden = low_back(matmul(normed_two, up_weight) + up_shift)
    active = low(jax.nn.gelu(hidden, approximate=True))
    return middle + low_back(matmul(active, down_weight))

def encode(patch, params, same_doc):
    encoded = block(patch, params, 0, same_doc)
    feature = low(layer_norm(encoded, params[9][0], params[10][0]))
    projection = low_back(matmul(feature, params[11][0].T))
    return unit_rows(projection)

def code_rows(table, code_ids):
    return unit_rows(jnp.take(table, code_ids, axis=1).T)

def group_terms(params, patch, cotangent, code_ids, lengths, latent_fixed, code_fixed):
    same_doc = same_segment(lengths, patch.shape[0])
    latent = encode(patch, params, same_doc)
    code_vec = code_rows(params[12], code_ids)
    quant = low_back(low(latent + (code_fixed - latent_fixed)))
    lifted = low_back(matmul(quant, params[11][1]))
    decoded = block(lifted, params, 1, same_doc)
    final = layer_norm(decoded, params[9][1], params[10][1])
    objective = jnp.sum(cotangent * final)
    objective = objective + jnp.sum(jnp.square(latent_fixed - code_vec))
    return (objective, final)

def reference(section_in, ln1_gain, ln1_shift, qkv_weight, out_weight, ln2_gain, ln2_shift, up_weight, up_shift, down_weight, final_gain, final_shift, bridge_weight, codebook, codes, doc_lengths):
    params = tuple((member.astype(jnp.float32) for member in (ln1_gain, ln1_shift, qkv_weight, out_weight, ln2_gain, ln2_shift, up_weight, up_shift, down_weight, final_gain, final_shift, bridge_weight, codebook)))
    groups = doc_lengths.shape[0]
    row_count = section_in.shape[1] // groups
    width = section_in.shape[2]
    patches = section_in[0].astype(jnp.float32).reshape(groups, row_count, width)
    cotangents = section_in[1].astype(jnp.float32).reshape(groups, row_count, width)
    code_groups = codes.reshape(groups, row_count)

    def fixed_terms(entry):
        patch, code_ids, lengths = entry
        return (encode(patch, params, same_segment(lengths, row_count)), code_rows(params[12], code_ids))
    latent_fixed, code_fixed = lax.map(fixed_terms, (patches, code_groups, doc_lengths))

    def total(weights, patch_all):

        def one_group(entry):
            patch, cotangent, code_ids, lengths, latent_one, code_one = entry
            return group_terms(weights, patch, cotangent, code_ids, lengths, latent_one, code_one)
        objectives, finals = lax.map(jax.checkpoint(one_group), (patch_all, cotangents, code_groups, doc_lengths, latent_fixed, code_fixed))
        return (jnp.sum(objectives), finals)
    objective, pullback, finals = jax.vjp(total, params, patches, has_aux=True)
    grad_params, grad_patches = pullback(jnp.ones_like(objective))
    section_out = jnp.stack([grad_patches.reshape(-1, width), finals.reshape(-1, width)]).astype(jnp.bfloat16)
    return (section_out, grad_params[0], grad_params[1], grad_params[2], grad_params[3], grad_params[4], grad_params[5], grad_params[6], grad_params[7], grad_params[8], grad_params[9], grad_params[10], grad_params[11], grad_params[12])
```

```python
import functools

import jax
import jax.numpy as jnp
from jax import lax
from jax.experimental import pallas as pl
from jax.experimental.pallas import tpu as pltpu
from jax.sharding import PartitionSpec as P

HEADS = 8
PAIRS = HEADS // 2
LANES = 128
EPS = 1e-06
GELU_FACTOR = 0.7978845608028654
GELU_CUBIC = 0.044715
BLOCKED = -1000000000.0
FULL = jnp.float32
HALF = jnp.bfloat16
VMEM_BYTES = 60 * 1024 * 1024


def low(value):
    return value.astype(HALF)


def mm(left, right):
    return lax.dot_general(left, right, (((1,), (0,)), ((), ())), preferred_element_type=FULL)


def mm_nt(left, right):
    return lax.dot_general(left, right, (((1,), (1,)), ((), ())), preferred_element_type=FULL)


def mm_tn(left, right):
    return lax.dot_general(left, right, (((0,), (0,)), ((), ())), preferred_element_type=FULL)


def norm_forward(inputs, gain, shift):
    centred = inputs - jnp.mean(inputs, axis=-1, keepdims=True)
    scaling = lax.rsqrt(jnp.mean(centred * centred, axis=-1, keepdims=True) + EPS)
    normal = centred * scaling
    return normal * gain + shift, normal, scaling


def norm_backward(upstream, normal, scaling, gain):
    scaled = upstream * gain
    inner = scaled - jnp.mean(scaled, axis=-1, keepdims=True)
    inner = inner - normal * jnp.mean(scaled * normal, axis=-1, keepdims=True)
    return (
        scaling * inner,
        jnp.sum(upstream * normal, axis=0, keepdims=True),
        jnp.sum(upstream, axis=0, keepdims=True),
    )


def write_bias(lengths_ref, group, bias_ref):
    rows = bias_ref.shape[0]
    down = lax.broadcasted_iota(jnp.int32, (rows, rows), 0)
    across = lax.broadcasted_iota(jnp.int32, (rows, rows), 1)
    row_label = jnp.zeros((rows, rows), jnp.int32)
    column_label = jnp.zeros((rows, rows), jnp.int32)
    bound = jnp.int32(0)
    for doc in range(lengths_ref.shape[1]):
        bound = bound + lengths_ref[group, doc]
        row_label = row_label + (down >= bound).astype(jnp.int32)
        column_label = column_label + (across >= bound).astype(jnp.int32)
    bias_ref[...] = jnp.where(row_label == column_label, 0.0, BLOCKED)


def half_mask(rows, side):
    lane = lax.broadcasted_iota(jnp.int32, (rows, LANES), 1)
    return lane < LANES // 2 if side == 0 else lane >= LANES // 2


def attention_forward(qkv_ref, bias_ref, mixed_ref, lse_ref, lse_scratch):
    rows = qkv_ref.shape[1]
    scale = (LANES // 2) ** (-0.5)
    lane = lax.broadcasted_iota(jnp.int32, (rows, LANES), 1)
    lse_scratch[...] = jnp.zeros_like(lse_scratch)

    def pair_step(pair, carry):
        queries = qkv_ref[pair] * jnp.asarray(scale, HALF)
        keys = qkv_ref[PAIRS + pair]
        values = qkv_ref[2 * PAIRS + pair]
        mixed = jnp.zeros((rows, LANES), FULL)
        for side in range(2):
            inside = half_mask(rows, side)
            zero = jnp.zeros((), HALF)
            scores = mm_nt(jnp.where(inside, queries, zero), keys) + bias_ref[...]
            peak = jnp.max(scores, axis=-1, keepdims=True)
            weight = jnp.exp(scores - peak)
            total = jnp.sum(weight, axis=-1, keepdims=True)
            part = mm(low(weight), jnp.where(inside, values, zero))
            mixed = mixed + part * (1.0 / total)
            log_total = peak + jnp.log(total)
            lse_scratch[...] = jnp.where(lane == 2 * pair + side, log_total, lse_scratch[...])
        mixed_ref[pair] = low(mixed)
        return carry

    lax.fori_loop(0, PAIRS, pair_step, 0)
    lse_ref[...] = jnp.transpose(lse_scratch[...])[:HEADS]


def heads_joined(mixed_ref):
    return jnp.concatenate([mixed_ref[pair] for pair in range(PAIRS)], axis=1)


def block_forward(
    x, weights, bias_ref, qkv_ref, mixed_ref, lse_ref, lse_scratch, slope_ref, active_ref, total_ref
):
    ln1_gain, ln1_shift, qkv_w, out_w, ln2_gain, ln2_shift, up_w, up_shift, down_w = weights
    width = x.shape[1]
    hidden_width = up_w.shape[1]
    normed = low(norm_forward(x, ln1_gain[...], ln1_shift[...])[0])
    for part in range(3):
        projected = low(mm(normed, qkv_w[:, part * width : (part + 1) * width]))
        for pair in range(PAIRS):
            qkv_ref[part * PAIRS + pair] = projected[:, pair * LANES : (pair + 1) * LANES]
    attention_forward(qkv_ref, bias_ref, mixed_ref, lse_ref, lse_scratch)
    middle = x + mm(heads_joined(mixed_ref), out_w[...])
    normed_two = low(norm_forward(middle, ln2_gain[...], ln2_shift[...])[0])
    total_ref[...] = middle
    tile = width

    def hidden_step(step, carry):
        place = pl.ds(pl.multiple_of(step * tile, tile), tile)
        hidden = mm(normed_two, up_w[:, place]) + up_shift[:, place]
        square = hidden * hidden
        tangent = jnp.tanh(GELU_FACTOR * (hidden * (1.0 + GELU_CUBIC * square)))
        gate = 0.5 * (1.0 + tangent)
        active = low(hidden * gate)
        slope = gate + (0.5 * GELU_FACTOR) * hidden * (1.0 - tangent * tangent) * (
            1.0 + (3.0 * GELU_CUBIC) * square
        )
        active_ref[:, place] = active
        slope_ref[:, place] = low(slope)
        total_ref[...] = total_ref[...] + mm(active, down_w[place, :])
        return carry

    lax.fori_loop(0, hidden_width // tile, hidden_step, 0)
    return middle, normed_two


def feed_backward(
    upstream, middle, weights, slope_ref, active_ref, normed_ref, total_ref, down_out, up_out, up_shift_out
):
    ln1_gain, ln1_shift, qkv_w, out_w, ln2_gain, ln2_shift, up_w, up_shift, down_w = weights
    width = upstream.shape[1]
    hidden_width = up_w.shape[1]
    normed_two, normal, scaling = norm_forward(middle, ln2_gain[...], ln2_shift[...])
    normed_ref[...] = low(normed_two)
    branch = low(upstream)
    total_ref[...] = jnp.zeros_like(total_ref)
    tile = width

    def hidden_step(step, carry):
        place = pl.ds(pl.multiple_of(step * tile, tile), tile)
        down_out[place, :] = down_out[place, :] + mm_tn(active_ref[:, place], branch)
        grad_hidden = mm_nt(branch, down_w[place, :]) * slope_ref[:, place].astype(FULL)
        up_shift_out[:, place] = up_shift_out[:, place] + jnp.sum(grad_hidden, axis=0, keepdims=True)
        grad_low = low(grad_hidden)
        up_out[:, place] = up_out[:, place] + mm_tn(normed_ref[...], grad_low)
        total_ref[...] = total_ref[...] + mm_nt(grad_low, up_w[:, place])
        return carry

    lax.fori_loop(0, hidden_width // tile, hidden_step, 0)
    grad_norm, grad_gain, grad_shift = norm_backward(total_ref[...], normal, scaling, ln2_gain[...])
    return upstream + grad_norm, grad_gain, grad_shift


def attention_backward(qkv_ref, grad_mixed_ref, bias_ref, lse_ref, grad_qkv_ref):
    rows = qkv_ref.shape[1]
    scale = (LANES // 2) ** (-0.5)

    def pair_step(pair, carry):
        queries = qkv_ref[pair] * jnp.asarray(scale, HALF)
        keys = qkv_ref[PAIRS + pair]
        values = qkv_ref[2 * PAIRS + pair]
        grads = grad_mixed_ref[pair]
        grad_queries = jnp.zeros((rows, LANES), FULL)
        grad_keys = jnp.zeros((rows, LANES), FULL)
        grad_values = jnp.zeros((rows, LANES), FULL)
        for side in range(2):
            inside = half_mask(rows, side)
            zero = jnp.zeros((), HALF)
            side_queries = jnp.where(inside, queries, zero)
            side_grads = jnp.where(inside, grads, zero)
            scores = mm_nt(keys, side_queries) + bias_ref[...]
            attention = jnp.exp(scores - lse_ref[pl.ds(2 * pair + side, 1), :])
            grad_values = grad_values + mm(low(attention), side_grads)
            grad_attention = mm_nt(values, side_grads)
            delta = jnp.sum(attention * grad_attention, axis=0, keepdims=True)
            grad_scores = low(attention * (grad_attention - delta))
            grad_keys = grad_keys + mm(grad_scores, side_queries)
            grad_queries = grad_queries + mm_tn(grad_scores, jnp.where(inside, keys, zero))
        grad_qkv_ref[pair] = low(grad_queries * scale)
        grad_qkv_ref[PAIRS + pair] = low(grad_keys)
        grad_qkv_ref[2 * PAIRS + pair] = low(grad_values)
        return carry

    lax.fori_loop(0, PAIRS, pair_step, 0)


def block_attention_backward(
    x,
    grad_middle,
    weights,
    bias_ref,
    qkv_ref,
    mixed_ref,
    lse_ref,
    grad_mixed_ref,
    grad_qkv_ref,
    qkv_out,
    out_out,
):
    ln1_gain, ln1_shift, qkv_w, out_w = weights[:4]
    width = x.shape[1]
    grad_low = low(grad_middle)
    out_out[...] = out_out[...] + mm_tn(heads_joined(mixed_ref), grad_low)
    grad_mixed = low(mm_nt(grad_low, out_w[...]))
    for pair in range(PAIRS):
        grad_mixed_ref[pair] = grad_mixed[:, pair * LANES : (pair + 1) * LANES]
    attention_backward(qkv_ref, grad_mixed_ref, bias_ref, lse_ref, grad_qkv_ref)
    normed, normal, scaling = norm_forward(x, ln1_gain[...], ln1_shift[...])
    normed_low = low(normed)
    grad_normed = jnp.zeros_like(x)
    for part in range(3):
        grad_part = jnp.concatenate(
            [grad_qkv_ref[part * PAIRS + pair] for pair in range(PAIRS)], axis=1
        )
        place = slice(part * width, (part + 1) * width)
        qkv_out[:, place] = qkv_out[:, place] + mm_tn(normed_low, grad_part)
        grad_normed = grad_normed + mm_nt(grad_part, qkv_w[:, place])
    grad_norm, grad_gain, grad_shift = norm_backward(grad_normed, normal, scaling, ln1_gain[...])
    return grad_middle + grad_norm, grad_gain, grad_shift


def unit_rows(rows):
    inverse = lax.rsqrt(jnp.sum(rows * rows, axis=-1, keepdims=True) + EPS)
    return rows * inverse, inverse


def start_totals(*refs):
    @pl.when(pl.program_id(0) == 0)
    def _():
        for ref in refs:
            ref[...] = jnp.zeros_like(ref)


def encoder_forward_kernel(
    lengths,
    patch,
    ln1_gain,
    ln1_shift,
    qkv_w,
    out_w,
    ln2_gain,
    ln2_shift,
    up_w,
    up_shift,
    down_w,
    final_gain,
    final_shift,
    bridge,
    qkv_ref,
    lse_ref,
    mixed_ref,
    middle_ref,
    slope_ref,
    active_ref,
    result_ref,
    latent_ref,
    bias_ref,
    lse_scratch,
):
    weights = (ln1_gain, ln1_shift, qkv_w, out_w, ln2_gain, ln2_shift, up_w, up_shift, down_w)
    write_bias(lengths, pl.program_id(0), bias_ref)
    x = patch[...].astype(FULL)
    middle, _ = block_forward(
        x, weights, bias_ref, qkv_ref, mixed_ref, lse_ref, lse_scratch, slope_ref, active_ref, result_ref
    )
    middle_ref[...] = middle
    feature = low(norm_forward(result_ref[...], final_gain[...], final_shift[...])[0])
    latent_ref[...] = unit_rows(mm_nt(feature, bridge[...]))[0]


def quant_kernel(per_device, codes, codes_column, latent, table, quant_ref, book_ref, gathered, spread):
    count = gathered.shape[0]
    quarter = per_device // 4
    shift_all, shift_quarter = per_device.bit_length() - 1, quarter.bit_length() - 1

    def row_of(code):
        return (code >> shift_all) * quarter + (code & (quarter - 1))

    def gather(index, carry):
        gathered[pl.ds(index, 1), :] = table[pl.ds(row_of(codes[index]), 1), :]
        return carry

    lax.fori_loop(0, count, gather, 0, unroll=8)
    block = (codes_column[...] >> shift_quarter) & 3
    lane = lax.broadcasted_iota(jnp.int32, (count, LANES), 1)
    width = LANES // 4
    rows = gathered[...]
    code = jnp.where(block == 0, rows, 0.0)
    for place in range(1, 4):
        code = code + jnp.where(block == place, pltpu.roll(rows, LANES - width * place, 1), 0.0)
    code = jnp.where(lane < width, code, 0.0)
    held = latent[...]
    quant_ref[...] = low(held + (code - held))
    grad = 2.0 * (code - held)
    placed = jnp.where(block == 0, grad, 0.0)
    for place in range(1, 4):
        placed = placed + jnp.where(block == place, pltpu.roll(grad, width * place, 1), 0.0)
    spread[...] = placed
    book_ref[...] = jnp.zeros_like(book_ref)

    def scatter(index, carry):
        place = pl.ds(row_of(codes[index]), 1)
        book_ref[place, :] = book_ref[place, :] + spread[pl.ds(index, 1), :]
        return carry

    lax.fori_loop(0, count, scatter, 0, unroll=8)


def decoder_feed_kernel(
    lengths,
    quant,
    cotangent,
    ln1_gain,
    ln1_shift,
    qkv_w,
    out_w,
    ln2_gain,
    ln2_shift,
    up_w,
    up_shift,
    down_w,
    final_gain,
    final_shift,
    bridge,
    final_ref,
    qkv_ref,
    lse_ref,
    mixed_ref,
    grad_middle_ref,
    down_out,
    up_out,
    up_shift_out,
    ln2_out,
    final_out,
    bias_ref,
    lse_scratch,
    slope_ref,
    active_ref,
    normed_ref,
    result_ref,
    total_ref,
):
    weights = (ln1_gain, ln1_shift, qkv_w, out_w, ln2_gain, ln2_shift, up_w, up_shift, down_w)
    start_totals(down_out, up_out, up_shift_out, ln2_out, final_out)
    write_bias(lengths, pl.program_id(0), bias_ref)
    x = mm(quant[...], bridge[...])
    middle, _ = block_forward(
        x, weights, bias_ref, qkv_ref, mixed_ref, lse_ref, lse_scratch, slope_ref, active_ref, result_ref
    )
    grad_middle_ref[...] = middle
    final, normal, scaling = norm_forward(result_ref[...], final_gain[...], final_shift[...])
    final_ref[...] = low(final)
    upstream, grad_gain, grad_shift = norm_backward(
        cotangent[...].astype(FULL), normal, scaling, final_gain[...]
    )
    final_out[0:1, :] = final_out[0:1, :] + grad_gain
    final_out[1:2, :] = final_out[1:2, :] + grad_shift
    grad_middle, grad_gain, grad_shift = feed_backward(
        upstream,
        grad_middle_ref[...],
        weights,
        slope_ref,
        active_ref,
        normed_ref,
        total_ref,
        down_out,
        up_out,
        up_shift_out,
    )
    ln2_out[0:1, :] = ln2_out[0:1, :] + grad_gain
    ln2_out[1:2, :] = ln2_out[1:2, :] + grad_shift
    grad_middle_ref[...] = grad_middle


def decoder_attention_kernel(
    lengths,
    quant,
    grad_middle,
    qkv_ref,
    lse_ref,
    mixed_ref,
    ln1_gain,
    ln1_shift,
    qkv_w,
    out_w,
    bridge,
    grad_quant_ref,
    qkv_out,
    out_out,
    ln1_out,
    bridge_out,
    bias_ref,
    grad_mixed_ref,
    grad_qkv_ref,
):
    start_totals(qkv_out, out_out, ln1_out, bridge_out)
    write_bias(lengths, pl.program_id(0), bias_ref)
    grad_input, grad_gain, grad_shift = block_attention_backward(
        mm(quant[...], bridge[...]),
        grad_middle[...],
        (ln1_gain, ln1_shift, qkv_w, out_w),
        bias_ref,
        qkv_ref,
        mixed_ref,
        lse_ref,
        grad_mixed_ref,
        grad_qkv_ref,
        qkv_out,
        out_out,
    )
    ln1_out[0:1, :] = ln1_out[0:1, :] + grad_gain
    ln1_out[1:2, :] = ln1_out[1:2, :] + grad_shift
    grad_lift = low(grad_input)
    bridge_out[...] = bridge_out[...] + mm_tn(quant[...], grad_lift)
    grad_quant_ref[...] = low(mm_nt(grad_lift, bridge[...]))


def encoder_feed_kernel(
    grad_quant,
    middle,
    result,
    slope_ref,
    active_ref,
    ln1_gain,
    ln1_shift,
    qkv_w,
    out_w,
    ln2_gain,
    ln2_shift,
    up_w,
    up_shift,
    down_w,
    final_gain,
    final_shift,
    bridge,
    grad_middle_ref,
    down_out,
    up_out,
    up_shift_out,
    ln2_out,
    final_out,
    bridge_out,
    normed_ref,
    total_ref,
):
    weights = (ln1_gain, ln1_shift, qkv_w, out_w, ln2_gain, ln2_shift, up_w, up_shift, down_w)
    start_totals(down_out, up_out, up_shift_out, ln2_out, final_out, bridge_out)
    feature, normal, scaling = norm_forward(result[...], final_gain[...], final_shift[...])
    feature_low = low(feature)
    latent, inverse = unit_rows(mm_nt(feature_low, bridge[...]))
    grad_latent = grad_quant[...].astype(FULL)
    grad_projection = low(
        inverse * (grad_latent - latent * jnp.sum(latent * grad_latent, axis=1, keepdims=True))
    )
    bridge_out[...] = bridge_out[...] + mm_tn(grad_projection, feature_low)
    upstream, grad_gain, grad_shift = norm_backward(
        mm(grad_projection, bridge[...]), normal, scaling, final_gain[...]
    )
    final_out[0:1, :] = final_out[0:1, :] + grad_gain
    final_out[1:2, :] = final_out[1:2, :] + grad_shift
    grad_middle, grad_gain, grad_shift = feed_backward(
        upstream,
        middle[...],
        weights,
        slope_ref,
        active_ref,
        normed_ref,
        total_ref,
        down_out,
        up_out,
        up_shift_out,
    )
    ln2_out[0:1, :] = ln2_out[0:1, :] + grad_gain
    ln2_out[1:2, :] = ln2_out[1:2, :] + grad_shift
    grad_middle_ref[...] = grad_middle


def encoder_attention_kernel(
    lengths,
    patch,
    grad_middle,
    qkv_ref,
    lse_ref,
    mixed_ref,
    ln1_gain,
    ln1_shift,
    qkv_w,
    out_w,
    grad_patch_ref,
    qkv_out,
    out_out,
    ln1_out,
    bias_ref,
    grad_mixed_ref,
    grad_qkv_ref,
):
    start_totals(qkv_out, out_out, ln1_out)
    write_bias(lengths, pl.program_id(0), bias_ref)
    grad_input, grad_gain, grad_shift = block_attention_backward(
        patch[...].astype(FULL),
        grad_middle[...],
        (ln1_gain, ln1_shift, qkv_w, out_w),
        bias_ref,
        qkv_ref,
        mixed_ref,
        lse_ref,
        grad_mixed_ref,
        grad_qkv_ref,
        qkv_out,
        out_out,
    )
    ln1_out[0:1, :] = ln1_out[0:1, :] + grad_gain
    ln1_out[1:2, :] = ln1_out[1:2, :] + grad_shift
    grad_patch_ref[...] = low(grad_input)


class Token:
    def __init__(self, shape, dtype):
        self.shape, self.dtype = shape, dtype

    def struct(self, groups):
        return jax.ShapeDtypeStruct((groups,) + self.shape, self.dtype)

    def spec(self):
        tail = (0,) * len(self.shape)
        return pl.BlockSpec((None,) + self.shape, lambda group: (group,) + tail)


class Whole:
    def __init__(self, shape, dtype):
        self.shape, self.dtype = shape, dtype

    def struct(self, groups):
        return jax.ShapeDtypeStruct(self.shape, self.dtype)

    def spec(self):
        zeros = (0,) * len(self.shape)
        return pl.BlockSpec(self.shape, lambda group: zeros)


def run_groups(kernel, name, groups, lengths, tokens, wholes, outs, scratch):
    specs = [pl.BlockSpec(memory_space=pltpu.SMEM)] if lengths is not None else []
    specs += [Token(array.shape[1:], array.dtype).spec() for array in tokens]
    specs += [Whole(array.shape, array.dtype).spec() for array in wholes]
    given = ([lengths] if lengths is not None else []) + list(tokens) + list(wholes)
    return pl.pallas_call(
        kernel,
        grid=(groups,),
        in_specs=specs,
        out_specs=[out.spec() for out in outs],
        out_shape=[out.struct(groups) for out in outs],
        scratch_shapes=scratch,
        compiler_params=pltpu.CompilerParams(vmem_limit_bytes=VMEM_BYTES),
        name=name,
    )(*given)


def from_section(block):
    return lax.ppermute(block, "section", [(0, 1), (1, 0)])


def on_device(
    section_in,
    ln1_gain,
    ln1_shift,
    qkv_weight,
    out_weight,
    ln2_gain,
    ln2_shift,
    up_weight,
    up_shift,
    down_weight,
    final_gain,
    final_shift,
    bridge_weight,
    codebook,
    codes,
    doc_lengths,
):
    section = lax.axis_index("section")
    encoder_side = section == 0
    micro = doc_lengths.shape[0]
    groups = micro // 2
    rows = section_in.shape[1] // micro
    width = section_in.shape[2]
    hidden_width = up_weight.shape[2]
    latent_width = bridge_weight.shape[1]
    per_device = codebook.shape[1]

    vectors = jnp.concatenate(
        [ln1_gain, ln1_shift, ln2_gain, ln2_shift, final_gain, final_shift, up_shift.reshape(-1, width)],
        axis=0,
    )
    bridge = jnp.pad(bridge_weight[0], ((0, LANES - latent_width), (0, 0)))
    own = (vectors, qkv_weight[0], out_weight[0], up_weight[0], down_weight[0], bridge)
    other = tuple(from_section(member) for member in own)

    def split(member, received):
        return (
            jnp.where(encoder_side, member, received),
            jnp.where(encoder_side, received, member),
        )

    pairs = [split(member, received) for member, received in zip(own, other)]

    def weights_of(side):
        vector, qkv_w, out_w, up_w, down_w, bridge_w = [pair[side] for pair in pairs]
        return dict(
            ln1_gain=vector[0:1],
            ln1_shift=vector[1:2],
            qkv_w=qkv_w,
            out_w=out_w,
            ln2_gain=vector[2:3],
            ln2_shift=vector[3:4],
            up_w=up_w,
            up_shift=vector[6:].reshape(1, hidden_width),
            down_w=down_w,
            final_gain=vector[4:5],
            final_shift=vector[5:6],
            bridge=bridge_w,
        )

    encoder, decoder = weights_of(0), weights_of(1)

    halves = section_in[0].reshape(2, groups, rows, width)
    mine = lax.dynamic_index_in_dim(halves, section, 0, keepdims=False)
    theirs = from_section(lax.dynamic_index_in_dim(halves, 1 - section, 0, keepdims=False))
    patch = jnp.where(encoder_side, mine, theirs)
    cotangent = jnp.where(encoder_side, theirs, mine)
    lengths = lax.dynamic_slice_in_dim(doc_lengths, section * groups, groups, 0)
    own_codes = lax.dynamic_slice_in_dim(codes, section * groups * rows, groups * rows, 0)

    inverse = lax.rsqrt(jnp.sum(codebook * codebook, axis=0, keepdims=True) + EPS)
    unit_codes = codebook * inverse
    quarter = per_device // 4
    packed = (
        unit_codes.reshape(latent_width, 4, quarter).transpose(2, 1, 0).reshape(quarter, 4 * latent_width)
    )
    table = lax.all_gather(packed, ("section", "dp"), axis=0, tiled=True)

    names = (
        "ln1_gain ln1_shift qkv_w out_w ln2_gain ln2_shift up_w up_shift down_w final_gain final_shift bridge"
    ).split()
    short = "ln1_gain ln1_shift qkv_w out_w".split()
    saved_qkv = Token((3 * PAIRS, rows, LANES), HALF)
    saved_lse = Token((HEADS, rows), FULL)
    saved_mixed = Token((PAIRS, rows, LANES), HALF)
    wide = Token((rows, width), FULL)
    hidden = Token((rows, hidden_width), HALF)
    bias_scratch = pltpu.VMEM((rows, rows), FULL)
    lse_scratch = pltpu.VMEM((rows, LANES), FULL)

    qkv_e, lse_e, mixed_e, middle_e, slope_e, active_e, result_e, latent = run_groups(
        encoder_forward_kernel,
        "encoder_forward",
        groups,
        lengths,
        [patch],
        [encoder[name] for name in names],
        [saved_qkv, saved_lse, saved_mixed, wide, hidden, hidden, wide, Token((rows, LANES), FULL)],
        [bias_scratch, lse_scratch],
    )

    count = groups * rows
    vmem = pl.BlockSpec(memory_space=pltpu.VMEM)
    quant, book = pl.pallas_call(
        functools.partial(quant_kernel, per_device),
        in_specs=[pl.BlockSpec(memory_space=pltpu.SMEM), vmem, vmem, vmem],
        out_specs=[vmem, vmem],
        out_shape=[
            jax.ShapeDtypeStruct((count, LANES), HALF),
            jax.ShapeDtypeStruct(table.shape, FULL),
        ],
        scratch_shapes=[pltpu.VMEM((count, LANES), FULL), pltpu.VMEM((count, LANES), FULL)],
        compiler_params=pltpu.CompilerParams(vmem_limit_bytes=VMEM_BYTES),
        name="quantize",
    )(own_codes, own_codes.reshape(count, 1), latent.reshape(count, LANES), table)
    quant = quant.reshape(groups, rows, LANES)

    down_grad = Whole((hidden_width, width), FULL)
    up_grad = Whole((width, hidden_width), FULL)
    hidden_vector = Whole((1, hidden_width), FULL)
    two_vectors = Whole((2, width), FULL)
    qkv_grad = Whole((width, 3 * width), FULL)
    out_grad = Whole((width, width), FULL)
    bridge_grad = Whole((LANES, width), FULL)
    feed_scratch = [pltpu.VMEM((rows, width), HALF), pltpu.VMEM((rows, width), FULL)]
    final, qkv_d, lse_d, mixed_d, middle_d, down_d, up_d, up_shift_d, ln2_d, final_d = run_groups(
        decoder_feed_kernel,
        "decoder_forward_feed_backward",
        groups,
        lengths,
        [quant, cotangent],
        [decoder[name] for name in names],
        [
            Token((rows, width), HALF),
            saved_qkv,
            saved_lse,
            saved_mixed,
            wide,
            down_grad,
            up_grad,
            hidden_vector,
            two_vectors,
            two_vectors,
        ],
        [bias_scratch, lse_scratch]
        + [pltpu.VMEM((rows, hidden_width), HALF)] * 2
        + [feed_scratch[0], feed_scratch[1], feed_scratch[1]],
    )
    attention_scratch = [
        bias_scratch,
        pltpu.VMEM((PAIRS, rows, LANES), HALF),
        pltpu.VMEM((3 * PAIRS, rows, LANES), HALF),
    ]
    grad_quant, qkv_wd, out_d, ln1_d, bridge_d = run_groups(
        decoder_attention_kernel,
        "decoder_attention_backward",
        groups,
        lengths,
        [quant, middle_d, qkv_d, lse_d, mixed_d],
        [decoder[name] for name in short] + [decoder["bridge"]],
        [Token((rows, LANES), HALF), qkv_grad, out_grad, two_vectors, bridge_grad],
        attention_scratch,
    )
    middle_grad, down_e, up_e, up_shift_e, ln2_e, final_e, bridge_e = run_groups(
        encoder_feed_kernel,
        "encoder_feed_backward",
        groups,
        None,
        [grad_quant, middle_e, result_e, slope_e, active_e],
        [encoder[name] for name in names],
        [wide, down_grad, up_grad, hidden_vector, two_vectors, two_vectors, bridge_grad],
        feed_scratch,
    )
    grad_patch, qkv_we, out_e, ln1_e = run_groups(
        encoder_attention_kernel,
        "encoder_attention_backward",
        groups,
        lengths,
        [patch, middle_grad, qkv_e, lse_e, mixed_e],
        [encoder[name] for name in short],
        [Token((rows, width), HALF), qkv_grad, out_grad, two_vectors],
        attention_scratch,
    )

    def flat(ln1, ln2, final_norm, up_shift_grad, bridge_part):
        return jnp.concatenate(
            [ln1, ln2, final_norm, up_shift_grad.reshape(-1, width), bridge_part[:latent_width]], axis=0
        )

    small_e = flat(ln1_e, ln2_e, final_e, up_shift_e, bridge_e)
    small_d = flat(ln1_d, ln2_d, final_d, up_shift_d, bridge_d)

    def summed(encoder_grad, decoder_grad):
        keep = jnp.where(encoder_side, encoder_grad, decoder_grad)
        send = low(jnp.where(encoder_side, decoder_grad, encoder_grad))
        return lax.psum(low(keep + from_section(send).astype(FULL)), "dp").astype(FULL)

    small = summed(small_e, small_d)
    qkv_total = summed(qkv_we, qkv_wd)
    out_total = summed(out_e, out_d)
    up_total = summed(up_e, up_d)
    down_total = summed(down_e, down_d)

    book_own = lax.psum_scatter(book, ("section", "dp"), scatter_dimension=0, tiled=True)
    book_grad = (
        book_own.reshape(quarter, 4, latent_width).transpose(2, 1, 0).reshape(latent_width, per_device)
    )
    book_grad = inverse * (
        book_grad - unit_codes * jnp.sum(unit_codes * book_grad, axis=0, keepdims=True)
    )

    sent = jnp.where(encoder_side, final, grad_patch)
    kept = jnp.where(encoder_side, grad_patch, final)
    got = from_section(sent)
    section_out = jnp.where(
        encoder_side, jnp.concatenate([kept, got], axis=0), jnp.concatenate([got, kept], axis=0)
    ).reshape(1, micro * rows, width)
    vectors_end = 6 + hidden_width // width
    return (
        section_out,
        small[0:1],
        small[1:2],
        qkv_total[None],
        out_total[None],
        small[2:3],
        small[3:4],
        up_total[None],
        small[6:vectors_end].reshape(1, hidden_width),
        down_total[None],
        small[4:5],
        small[5:6],
        small[vectors_end:][None],
        book_grad,
    )


def solution(mesh):
    placed = (
        P("section", "dp", None),
        P("section", None),
        P("section", None),
        P("section", None, None),
        P("section", None, None),
        P("section", None),
        P("section", None),
        P("section", None, None),
        P("section", None),
        P("section", None, None),
        P("section", None),
        P("section", None),
        P("section", None, None),
        P(None, ("section", "dp")),
        P("dp"),
        P("dp", None),
    )
    return jax.shard_map(
        on_device,
        mesh=mesh,
        in_specs=placed,
        out_specs=(
            P("section", "dp", None),
            P("section", None),
            P("section", None),
            P("section", None, None),
            P("section", None, None),
            P("section", None),
            P("section", None),
            P("section", None, None),
            P("section", None),
            P("section", None, None),
            P("section", None),
            P("section", None),
            P("section", None, None),
            P(None, ("section", "dp")),
        ),
        check_vma=False,
    )
```

```python
import functools

import jax
import jax.numpy as jnp
from jax import lax
from jax.experimental import pallas as pl
from jax.experimental.pallas import tpu as pltpu
from jax.sharding import PartitionSpec as P

HEADS = 8
PAIRS = HEADS // 2
LANES = 128
EPS = 1e-06
GELU_FACTOR = 0.7978845608028654
GELU_CUBIC = 0.044715
BLOCKED = -1000000000.0
CHUNKS = 16
FULL = jnp.float32
HALF = jnp.bfloat16
VMEM_BYTES = 60 * 1024 * 1024


def low(value):
    return value.astype(HALF)


def mm(left, right):
    return lax.dot_general(left, right, (((1,), (0,)), ((), ())), preferred_element_type=FULL)


def mm_nt(left, right):
    return lax.dot_general(left, right, (((1,), (1,)), ((), ())), preferred_element_type=FULL)


def mm_tn(left, right):
    return lax.dot_general(left, right, (((0,), (0,)), ((), ())), preferred_element_type=FULL)


def norm_forward(inputs, gain, shift):
    centred = inputs - jnp.mean(inputs, axis=-1, keepdims=True)
    scaling = lax.rsqrt(jnp.mean(centred * centred, axis=-1, keepdims=True) + EPS)
    normal = centred * scaling
    return normal * gain + shift, normal, scaling


def norm_backward(upstream, normal, scaling, gain):
    scaled = upstream * gain
    inner = scaled - jnp.mean(scaled, axis=-1, keepdims=True)
    inner = inner - normal * jnp.mean(scaled * normal, axis=-1, keepdims=True)
    return (
        scaling * inner,
        jnp.sum(upstream * normal, axis=0, keepdims=True),
        jnp.sum(upstream, axis=0, keepdims=True),
    )


def write_bias(lengths_ref, group, bias_ref):
    rows = bias_ref.shape[0]
    down = lax.broadcasted_iota(jnp.int32, (rows, rows), 0)
    across = lax.broadcasted_iota(jnp.int32, (rows, rows), 1)
    row_label = jnp.zeros((rows, rows), jnp.int32)
    column_label = jnp.zeros((rows, rows), jnp.int32)
    bound = jnp.int32(0)
    for doc in range(lengths_ref.shape[1]):
        bound = bound + lengths_ref[group, doc]
        row_label = row_label + (down >= bound).astype(jnp.int32)
        column_label = column_label + (across >= bound).astype(jnp.int32)
    bias_ref[...] = jnp.where(row_label == column_label, 0.0, BLOCKED)


def half_mask(rows, side):
    lane = lax.broadcasted_iota(jnp.int32, (rows, LANES), 1)
    return lane < LANES // 2 if side == 0 else lane >= LANES // 2


def attention_forward(qkv_ref, bias_ref, mixed_ref, lse_ref, lse_scratch):
    rows = qkv_ref.shape[1]
    scale = (LANES // 2) ** (-0.5)
    lane = lax.broadcasted_iota(jnp.int32, (rows, LANES), 1)
    lse_scratch[...] = jnp.zeros_like(lse_scratch)

    def pair_step(pair, carry):
        queries = qkv_ref[pair] * jnp.asarray(scale, HALF)
        keys = qkv_ref[PAIRS + pair]
        values = qkv_ref[2 * PAIRS + pair]
        mixed = jnp.zeros((rows, LANES), FULL)
        for side in range(2):
            inside = half_mask(rows, side)
            zero = jnp.zeros((), HALF)
            scores = mm_nt(jnp.where(inside, queries, zero), keys) + bias_ref[...]
            peak = jnp.max(scores, axis=-1, keepdims=True)
            weight = jnp.exp(scores - peak)
            total = jnp.sum(weight, axis=-1, keepdims=True)
            part = mm(low(weight), jnp.where(inside, values, zero))
            mixed = mixed + part * (1.0 / total)
            log_total = peak + jnp.log(total)
            lse_scratch[...] = jnp.where(lane == 2 * pair + side, log_total, lse_scratch[...])
        mixed_ref[pair] = low(mixed)
        return carry

    lax.fori_loop(0, PAIRS, pair_step, 0)
    lse_ref[...] = jnp.transpose(lse_scratch[...])[:HEADS]


def heads_joined(mixed_ref):
    return jnp.concatenate([mixed_ref[pair] for pair in range(PAIRS)], axis=1)


def block_forward(
    x, weights, bias_ref, qkv_ref, mixed_ref, lse_ref, lse_scratch, slope_ref, active_ref, total_ref
):
    ln1_gain, ln1_shift, qkv_w, out_w, ln2_gain, ln2_shift, up_w, up_shift, down_w = weights
    width = x.shape[1]
    hidden_width = up_w.shape[1]
    normed = low(norm_forward(x, ln1_gain[...], ln1_shift[...])[0])
    for part in range(3):
        projected = low(mm(normed, qkv_w[:, part * width : (part + 1) * width]))
        for pair in range(PAIRS):
            qkv_ref[part * PAIRS + pair] = projected[:, pair * LANES : (pair + 1) * LANES]
    attention_forward(qkv_ref, bias_ref, mixed_ref, lse_ref, lse_scratch)
    middle = x + mm(heads_joined(mixed_ref), out_w[...])
    normed_two = low(norm_forward(middle, ln2_gain[...], ln2_shift[...])[0])
    total_ref[...] = middle
    tile = width

    def hidden_step(step, carry):
        place = pl.ds(pl.multiple_of(step * tile, tile), tile)
        hidden = mm(normed_two, up_w[:, place]) + up_shift[:, place]
        square = hidden * hidden
        tangent = jnp.tanh(GELU_FACTOR * (hidden * (1.0 + GELU_CUBIC * square)))
        gate = 0.5 * (1.0 + tangent)
        active = low(hidden * gate)
        slope = gate + (0.5 * GELU_FACTOR) * hidden * (1.0 - tangent * tangent) * (
            1.0 + (3.0 * GELU_CUBIC) * square
        )
        active_ref[:, place] = active
        slope_ref[:, place] = low(slope)
        total_ref[...] = total_ref[...] + mm(active, down_w[place, :])
        return carry

    lax.fori_loop(0, hidden_width // tile, hidden_step, 0)
    return middle, normed_two


def feed_backward(
    upstream, middle, weights, slope_ref, active_ref, normed_ref, total_ref, down_out, up_out, up_shift_out
):
    ln1_gain, ln1_shift, qkv_w, out_w, ln2_gain, ln2_shift, up_w, up_shift, down_w = weights
    width = upstream.shape[1]
    hidden_width = up_w.shape[1]
    normed_two, normal, scaling = norm_forward(middle, ln2_gain[...], ln2_shift[...])
    normed_ref[...] = low(normed_two)
    branch = low(upstream)
    total_ref[...] = jnp.zeros_like(total_ref)
    tile = width

    def hidden_step(step, carry):
        place = pl.ds(pl.multiple_of(step * tile, tile), tile)
        down_out[place, :] = down_out[place, :] + mm_tn(active_ref[:, place], branch)
        grad_hidden = mm_nt(branch, down_w[place, :]) * slope_ref[:, place].astype(FULL)
        up_shift_out[:, place] = up_shift_out[:, place] + jnp.sum(grad_hidden, axis=0, keepdims=True)
        grad_low = low(grad_hidden)
        up_out[:, place] = up_out[:, place] + mm_tn(normed_ref[...], grad_low)
        total_ref[...] = total_ref[...] + mm_nt(grad_low, up_w[:, place])
        return carry

    lax.fori_loop(0, hidden_width // tile, hidden_step, 0)
    grad_norm, grad_gain, grad_shift = norm_backward(total_ref[...], normal, scaling, ln2_gain[...])
    return upstream + grad_norm, grad_gain, grad_shift


def attention_backward(qkv_ref, grad_mixed_ref, bias_ref, lse_ref, grad_qkv_ref):
    rows = qkv_ref.shape[1]
    scale = (LANES // 2) ** (-0.5)

    def pair_step(pair, carry):
        queries = qkv_ref[pair] * jnp.asarray(scale, HALF)
        keys = qkv_ref[PAIRS + pair]
        values = qkv_ref[2 * PAIRS + pair]
        grads = grad_mixed_ref[pair]
        grad_queries = jnp.zeros((rows, LANES), FULL)
        grad_keys = jnp.zeros((rows, LANES), FULL)
        grad_values = jnp.zeros((rows, LANES), FULL)
        for side in range(2):
            inside = half_mask(rows, side)
            zero = jnp.zeros((), HALF)
            side_queries = jnp.where(inside, queries, zero)
            side_grads = jnp.where(inside, grads, zero)
            scores = mm_nt(keys, side_queries) + bias_ref[...]
            attention = jnp.exp(scores - lse_ref[pl.ds(2 * pair + side, 1), :])
            grad_values = grad_values + mm(low(attention), side_grads)
            grad_attention = mm_nt(values, side_grads)
            delta = jnp.sum(attention * grad_attention, axis=0, keepdims=True)
            grad_scores = low(attention * (grad_attention - delta))
            grad_keys = grad_keys + mm(grad_scores, side_queries)
            grad_queries = grad_queries + mm_tn(grad_scores, jnp.where(inside, keys, zero))
        grad_qkv_ref[pair] = low(grad_queries * scale)
        grad_qkv_ref[PAIRS + pair] = low(grad_keys)
        grad_qkv_ref[2 * PAIRS + pair] = low(grad_values)
        return carry

    lax.fori_loop(0, PAIRS, pair_step, 0)


def attention_gradients(
    grad_middle, out_w, bias_ref, qkv_ref, mixed_ref, lse_ref, grad_mixed_ref, grad_qkv_ref, out_out
):
    grad_low = low(grad_middle)
    out_out[...] = out_out[...] + mm_tn(heads_joined(mixed_ref), grad_low)
    grad_mixed = low(mm_nt(grad_low, out_w[...]))
    for pair in range(PAIRS):
        grad_mixed_ref[pair] = grad_mixed[:, pair * LANES : (pair + 1) * LANES]
    attention_backward(qkv_ref, grad_mixed_ref, bias_ref, lse_ref, grad_qkv_ref)


def projection_gradients(x, grad_middle, ln1_gain, ln1_shift, qkv_w, grad_qkv_ref, qkv_out):
    width = x.shape[1]
    normed, normal, scaling = norm_forward(x, ln1_gain[...], ln1_shift[...])
    normed_low = low(normed)
    grad_normed = jnp.zeros_like(x)
    for part in range(3):
        grad_part = jnp.concatenate(
            [grad_qkv_ref[part * PAIRS + pair] for pair in range(PAIRS)], axis=1
        )
        place = slice(part * width, (part + 1) * width)
        qkv_out[:, place] = qkv_out[:, place] + mm_tn(normed_low, grad_part)
        grad_normed = grad_normed + mm_nt(grad_part, qkv_w[:, place])
    grad_norm, grad_gain, grad_shift = norm_backward(grad_normed, normal, scaling, ln1_gain[...])
    return grad_middle + grad_norm, grad_gain, grad_shift


def unit_rows(rows):
    inverse = lax.rsqrt(jnp.sum(rows * rows, axis=-1, keepdims=True) + EPS)
    return rows * inverse, inverse


def start_totals(*refs):
    @pl.when(pl.program_id(0) == 0)
    def _():
        for ref in refs:
            ref[...] = jnp.zeros_like(ref)


def encoder_forward_kernel(
    lengths,
    patch,
    ln1_gain,
    ln1_shift,
    qkv_w,
    out_w,
    ln2_gain,
    ln2_shift,
    up_w,
    up_shift,
    down_w,
    final_gain,
    final_shift,
    bridge,
    qkv_ref,
    lse_ref,
    mixed_ref,
    middle_ref,
    slope_ref,
    active_ref,
    result_ref,
    latent_ref,
    bias_ref,
    lse_scratch,
):
    weights = (ln1_gain, ln1_shift, qkv_w, out_w, ln2_gain, ln2_shift, up_w, up_shift, down_w)
    write_bias(lengths, pl.program_id(0), bias_ref)
    x = patch[...].astype(FULL)
    middle, _ = block_forward(
        x, weights, bias_ref, qkv_ref, mixed_ref, lse_ref, lse_scratch, slope_ref, active_ref, result_ref
    )
    middle_ref[...] = middle
    feature = low(norm_forward(result_ref[...], final_gain[...], final_shift[...])[0])
    latent_ref[...] = unit_rows(mm_nt(feature, bridge[...]))[0]


def quant_kernel(per_device, codes, codes_column, latent, table, quant_ref, book_ref, gathered, spread):
    count = gathered.shape[0]
    quarter = per_device // 4
    shift_all, shift_quarter = per_device.bit_length() - 1, quarter.bit_length() - 1

    def row_of(code):
        return (code >> shift_all) * quarter + (code & (quarter - 1))

    def gather(index, carry):
        gathered[pl.ds(index, 1), :] = table[pl.ds(row_of(codes[index]), 1), :]
        return carry

    lax.fori_loop(0, count, gather, 0, unroll=8)
    block = (codes_column[...] >> shift_quarter) & 3
    lane = lax.broadcasted_iota(jnp.int32, (count, LANES), 1)
    width = LANES // 4
    rows = gathered[...]
    code = jnp.where(block == 0, rows, 0.0)
    for place in range(1, 4):
        code = code + jnp.where(block == place, pltpu.roll(rows, LANES - width * place, 1), 0.0)
    code = jnp.where(lane < width, code, 0.0)
    held = latent[...]
    quant_ref[...] = low(held + (code - held))
    grad = 2.0 * (code - held)
    placed = jnp.where(block == 0, grad, 0.0)
    for place in range(1, 4):
        placed = placed + jnp.where(block == place, pltpu.roll(grad, width * place, 1), 0.0)
    spread[...] = placed
    book_ref[...] = jnp.zeros_like(book_ref)

    def scatter(index, carry):
        place = pl.ds(row_of(codes[index]), 1)
        book_ref[place, :] = book_ref[place, :] + spread[pl.ds(index, 1), :]
        return carry

    lax.fori_loop(0, count, scatter, 0, unroll=8)


def add_row(ref, row, value):
    ref[row : row + 1, :] = ref[row : row + 1, :] + value


def feed_vectors(vector_out, up_shift_acc):
    width = vector_out.shape[1]
    for part in range(up_shift_acc.shape[1] // width):
        vector_out[4 + part : 5 + part, :] = up_shift_acc[:, part * width : (part + 1) * width]


def last_group():
    return pl.program_id(0) == pl.num_programs(0) - 1


def decoder_feed_kernel(
    lengths,
    where,
    quant,
    cotangent,
    ln1_gain,
    ln1_shift,
    qkv_w,
    out_w,
    ln2_gain,
    ln2_shift,
    up_w,
    up_shift,
    down_w,
    final_gain,
    final_shift,
    bridge,
    final_ref,
    qkv_ref,
    lse_ref,
    mixed_ref,
    grad_middle_ref,
    keep_ref,
    send_ref,
    vector_out,
    bias_ref,
    lse_scratch,
    slope_ref,
    active_ref,
    normed_ref,
    result_ref,
    total_ref,
    down_acc,
    up_acc,
    up_shift_acc,
):
    weights = (ln1_gain, ln1_shift, qkv_w, out_w, ln2_gain, ln2_shift, up_w, up_shift, down_w)
    start_totals(down_acc, up_acc, up_shift_acc, vector_out)
    write_bias(lengths, pl.program_id(0), bias_ref)
    x = mm(quant[...], bridge[...])
    middle, _ = block_forward(
        x, weights, bias_ref, qkv_ref, mixed_ref, lse_ref, lse_scratch, slope_ref, active_ref, result_ref
    )
    grad_middle_ref[...] = middle
    final, normal, scaling = norm_forward(result_ref[...], final_gain[...], final_shift[...])
    final_ref[...] = low(final)
    upstream, grad_gain, grad_shift = norm_backward(
        cotangent[...].astype(FULL), normal, scaling, final_gain[...]
    )
    add_row(vector_out, 2, grad_gain)
    add_row(vector_out, 3, grad_shift)
    grad_middle, grad_gain, grad_shift = feed_backward(
        upstream,
        grad_middle_ref[...],
        weights,
        slope_ref,
        active_ref,
        normed_ref,
        total_ref,
        down_acc,
        up_acc,
        up_shift_acc,
    )
    add_row(vector_out, 0, grad_gain)
    add_row(vector_out, 1, grad_shift)
    grad_middle_ref[...] = grad_middle

    @pl.when(last_group())
    def _():
        feed_vectors(vector_out, up_shift_acc)
        pieces = [rows_of(down_acc)] + column_parts(up_acc, x.shape[1])
        store_blocks(where, keep_ref, send_ref, pieces)


def decoder_attention_kernel(
    lengths,
    where,
    quant,
    grad_middle,
    qkv_ref,
    lse_ref,
    mixed_ref,
    ln1_gain,
    ln1_shift,
    qkv_w,
    out_w,
    bridge,
    book,
    grad_quant_ref,
    keep_ref,
    send_ref,
    vector_out,
    bridge_out,
    bias_ref,
    grad_mixed_ref,
    grad_qkv_ref,
    qkv_acc,
    out_acc,
    *,
    owners,
    per_owner,
):
    start_totals(qkv_acc, out_acc, vector_out, bridge_out)
    write_bias(lengths, pl.program_id(0), bias_ref)
    attention_gradients(
        grad_middle[...], out_w, bias_ref, qkv_ref, mixed_ref, lse_ref, grad_mixed_ref, grad_qkv_ref, out_acc
    )
    grad_input, grad_gain, grad_shift = projection_gradients(
        mm(quant[...], bridge[...]), grad_middle[...], ln1_gain, ln1_shift, qkv_w, grad_qkv_ref, qkv_acc
    )
    add_row(vector_out, 0, grad_gain)
    add_row(vector_out, 1, grad_shift)
    grad_lift = low(grad_input)
    bridge_out[...] = bridge_out[...] + mm_tn(quant[...], grad_lift)
    grad_quant_ref[...] = low(mm_nt(grad_lift, bridge[...]))

    @pl.when(last_group())
    def _():
        pieces = [rows_of(out_acc)] + column_parts(qkv_acc, grad_input.shape[1])
        pieces = pieces + [codebook_rows(book, per_owner, owners)]
        store_blocks(where, keep_ref, send_ref, pieces)


def encoder_feed_kernel(
    where,
    grad_quant,
    middle,
    result,
    slope_ref,
    active_ref,
    ln1_gain,
    ln1_shift,
    qkv_w,
    out_w,
    ln2_gain,
    ln2_shift,
    up_w,
    up_shift,
    down_w,
    final_gain,
    final_shift,
    bridge,
    grad_middle_ref,
    keep_ref,
    send_ref,
    vector_out,
    bridge_out,
    normed_ref,
    total_ref,
    down_acc,
    up_acc,
    up_shift_acc,
):
    weights = (ln1_gain, ln1_shift, qkv_w, out_w, ln2_gain, ln2_shift, up_w, up_shift, down_w)
    start_totals(down_acc, up_acc, up_shift_acc, vector_out, bridge_out)
    feature, normal, scaling = norm_forward(result[...], final_gain[...], final_shift[...])
    feature_low = low(feature)
    latent, inverse = unit_rows(mm_nt(feature_low, bridge[...]))
    grad_latent = grad_quant[...].astype(FULL)
    grad_projection = low(
        inverse * (grad_latent - latent * jnp.sum(latent * grad_latent, axis=1, keepdims=True))
    )
    bridge_out[...] = bridge_out[...] + mm_tn(grad_projection, feature_low)
    upstream, grad_gain, grad_shift = norm_backward(
        mm(grad_projection, bridge[...]), normal, scaling, final_gain[...]
    )
    add_row(vector_out, 2, grad_gain)
    add_row(vector_out, 3, grad_shift)
    grad_middle, grad_gain, grad_shift = feed_backward(
        upstream,
        middle[...],
        weights,
        slope_ref,
        active_ref,
        normed_ref,
        total_ref,
        down_acc,
        up_acc,
        up_shift_acc,
    )
    add_row(vector_out, 0, grad_gain)
    add_row(vector_out, 1, grad_shift)
    grad_middle_ref[...] = grad_middle

    @pl.when(last_group())
    def _():
        feed_vectors(vector_out, up_shift_acc)
        store_blocks(where, keep_ref, send_ref, [rows_of(down_acc)] + column_parts(up_acc, upstream.shape[1]))


def encoder_attention_kernel(
    lengths,
    grad_middle,
    qkv_ref,
    lse_ref,
    mixed_ref,
    out_w,
    grad_qkv_ref,
    out_acc,
    bias_ref,
    grad_mixed_ref,
):
    start_totals(out_acc)
    write_bias(lengths, pl.program_id(0), bias_ref)
    attention_gradients(
        grad_middle[...], out_w, bias_ref, qkv_ref, mixed_ref, lse_ref, grad_mixed_ref, grad_qkv_ref, out_acc
    )


def encoder_input_kernel(
    where,
    patch,
    grad_middle,
    grad_qkv_ref,
    ln1_gain,
    ln1_shift,
    qkv_w,
    out_sum,
    grad_patch_ref,
    keep_ref,
    send_ref,
    vector_out,
    qkv_acc,
):
    start_totals(qkv_acc, vector_out)
    grad_input, grad_gain, grad_shift = projection_gradients(
        patch[...].astype(FULL), grad_middle[...], ln1_gain, ln1_shift, qkv_w, grad_qkv_ref, qkv_acc
    )
    add_row(vector_out, 0, grad_gain)
    add_row(vector_out, 1, grad_shift)
    grad_patch_ref[...] = low(grad_input)

    @pl.when(last_group())
    def _():
        pieces = [rows_of(out_sum)] + column_parts(qkv_acc, grad_input.shape[1])
        store_blocks(where, keep_ref, send_ref, pieces)


def store_blocks(where, keep_ref, send_ref, pieces):
    def step(index, carry):
        chunk = jnp.bitwise_xor(index, where[1])
        for side, ref in ((0, keep_ref), (1, send_ref)):
            block = 2 * chunk + jnp.bitwise_xor(where[0], side)
            offset = 0
            for piece in pieces:
                values = piece(block)
                count = values.shape[0]
                ref[index, offset : offset + count, :] = low(values)
                offset += count
        return carry

    lax.fori_loop(0, CHUNKS, step, 0)


def rows_of(ref, part=None):
    count = ref.shape[0] // (2 * CHUNKS)

    def piece(block):
        place = pl.ds(pl.multiple_of(block * count, count), count)
        if part is None:
            return ref[place, :]
        return ref[place, part]

    return piece


def column_parts(ref, width):
    return [rows_of(ref, slice(start, start + width)) for start in range(0, ref.shape[1], width)]


def codebook_rows(book_ref, per_owner, owners):
    def piece(block):
        side, chunk = block & 1, block >> 1
        rows = []
        for high in range(owners // CHUNKS):
            owner = side * owners + high * CHUNKS + chunk
            rows.append(book_ref[pl.ds(pl.multiple_of(owner * per_owner, per_owner), per_owner), :])
        joined = jnp.concatenate(rows, axis=0) if len(rows) > 1 else rows[0]
        count = joined.shape[0] // 4
        return jnp.concatenate([joined[part * count : (part + 1) * count] for part in range(4)], axis=1)

    return piece


class Token:
    def __init__(self, shape, dtype):
        self.shape, self.dtype = shape, dtype

    def struct(self, groups):
        return jax.ShapeDtypeStruct((groups,) + self.shape, self.dtype)

    def spec(self):
        tail = (0,) * len(self.shape)
        return pl.BlockSpec((None,) + self.shape, lambda group: (group,) + tail)


class Whole:
    def __init__(self, shape, dtype):
        self.shape, self.dtype = shape, dtype

    def struct(self, groups):
        return jax.ShapeDtypeStruct(self.shape, self.dtype)

    def spec(self):
        zeros = (0,) * len(self.shape)
        return pl.BlockSpec(self.shape, lambda group: zeros)


def run_groups(kernel, name, groups, lengths, tokens, wholes, outs, scratch, flops):
    specs = [pl.BlockSpec(memory_space=pltpu.SMEM)] * len(lengths)
    specs += [Token(array.shape[1:], array.dtype).spec() for array in tokens]
    specs += [Whole(array.shape, array.dtype).spec() for array in wholes]
    given = list(lengths) + list(tokens) + list(wholes)
    return pl.pallas_call(
        kernel,
        grid=(groups,),
        in_specs=specs,
        out_specs=[out.spec() for out in outs],
        out_shape=[out.struct(groups) for out in outs],
        scratch_shapes=scratch,
        compiler_params=pltpu.CompilerParams(vmem_limit_bytes=VMEM_BYTES),
        cost_estimate=pl.CostEstimate(flops=flops, bytes_accessed=0, transcendentals=0),
        name=name,
    )(*given)


def from_section(block):
    return lax.ppermute(block, "section", [(0, 1), (1, 0)])


def from_dp(block, mask):
    count = lax.axis_size("dp")
    return lax.ppermute(block, "dp", [(place, place ^ mask) for place in range(count)])


def from_dp_of(block, mask, side):
    count = lax.axis_size("dp")
    first = side * count
    route = [(first + place, first + (place ^ mask)) for place in range(count)]
    return lax.ppermute(block, ("section", "dp"), route)


def small_call(kernel, name, outs, *given):
    vmem = pl.BlockSpec(memory_space=pltpu.VMEM)
    size = sum(member.size * member.dtype.itemsize for member in given)
    return pl.pallas_call(
        kernel,
        in_specs=[vmem] * len(given),
        out_specs=[vmem] * len(outs),
        out_shape=[jax.ShapeDtypeStruct(shape, HALF) for shape in outs],
        compiler_params=pltpu.CompilerParams(vmem_limit_bytes=VMEM_BYTES),
        cost_estimate=pl.CostEstimate(flops=0, bytes_accessed=2 * size, transcendentals=0),
        name=name,
    )(*given)


def total_of(*values):
    total = values[0].astype(FULL)
    for value in values[1:]:
        total = total + value.astype(FULL)
    return low(total)


PLANE, DEPTH = (1, 2, 3), (4, 8, 12)


def groups_of(masks):
    count = lax.axis_size("dp")
    return [[place ^ mask for mask in (0,) + masks] for place in range(count) if place & masks[2] == 0]


def exchange(blocks, masks):
    return [blocks[0]] + [from_dp(block, mask) for block, mask in zip(blocks[1:], masks)]


def add_cores(name, batches):
    rows = sum(kept.shape[1] for kept, _ in batches)
    width = batches[0][0].shape[2]

    def kernel(*refs):
        outs = refs[-4:]
        for chunk in range(CHUNKS):
            start = 0
            for number in range(len(batches)):
                value = total_of(refs[2 * number][chunk], refs[2 * number + 1][chunk])
                outs[chunk % 4][chunk // 4, start : start + value.shape[0], :] = value
                start += value.shape[0]

    flat = [member for batch in batches for member in batch]
    return small_call(kernel, name + "_cores", [(CHUNKS // 4, rows, width)] * 4, *flat)


def add_plane(name, members):
    def kernel(*refs):
        for place in range(4):
            refs[4 + place][...] = total_of(*[ref[place] for ref in refs[:4]])

    return small_call(kernel, name + "_plane", [members[0].shape[1:]] * 4, *members)


def add_depth(name, *batches):
    rows = sum(batch[0].shape[0] for batch in batches)

    def kernel(*refs):
        start = 0
        for number in range(len(batches)):
            value = total_of(*[ref[...] for ref in refs[4 * number : 4 * number + 4]])
            refs[-1][start : start + value.shape[0], :] = value
            start += value.shape[0]

    flat = [member for batch in batches for member in batch]
    return small_call(kernel, name + "_depth", [(rows, flat[0].shape[1])], *flat)[0]


def add_far(chunk):
    bit = CHUNKS
    while bit < lax.axis_size("dp"):
        chunk = total_of(chunk, from_dp(chunk, bit))
        bit = 2 * bit
    return chunk


def gather_depth_for(chunk, side):
    own = jnp.stack([chunk, from_section(chunk)])
    return jnp.stack([own] + [from_dp_of(own, mask, side) for mask in DEPTH])


def gather_plane_for(deep, side):
    return [deep] + [from_dp_of(deep, mask, side) for mask in PLANE]


def gather_depth(chunk):
    return jnp.stack([chunk] + [from_dp(chunk, mask) for mask in DEPTH])


def gather_plane(deep):
    depths, rows, width = deep.shape
    half = lax.all_gather(
        deep.reshape(depths * rows, width), "dp", axis=0, tiled=True, axis_index_groups=groups_of(PLANE)
    )
    return half.reshape(4, depths, rows, width)


def store_segments(outs, segments, block, piece, start, end):
    for offset, size, target, column in segments:
        first, last = max(start, offset), min(end, offset + size)
        if first < last:
            place = pl.ds(pl.multiple_of(block * size + (first - offset), 16), last - first)
            values = piece[first - start : last - start, :]
            outs[target][place, column : column + values.shape[1]] = values.astype(FULL)


def unpack_kernel(segments, where, *refs):
    encoder, decoder, outs = refs[:4], refs[4:6], refs[6:]
    rows = encoder[0].shape[2]

    @pl.when(where[0] == 0)
    def _():
        def step(deep, carry):
            for flat in range(4):
                chunk = jnp.bitwise_xor(4 * deep + flat, where[1])
                for side in range(2):
                    block = 2 * chunk + jnp.bitwise_xor(where[0], side)
                    store_segments(outs, segments, block, encoder[flat].at[deep, side], 0, rows)
            return carry

        lax.fori_loop(0, 4, step, 0)

    @pl.when(where[0] != 0)
    def _():
        def step(deep, carry):
            for flat in range(4):
                for side in range(2):
                    chunk = jnp.bitwise_xor(4 * deep, where[1] & 12) + flat
                    block = 2 * chunk + jnp.bitwise_xor(where[0], side)
                    store_segments(outs, segments, block, decoder[side].at[flat, deep], 0, rows)
            return carry

        lax.fori_loop(0, 4, step, 0)


def after(value, *others):
    return lax.optimization_barrier((value, others))[0]


def on_device(
    section_in,
    ln1_gain,
    ln1_shift,
    qkv_weight,
    out_weight,
    ln2_gain,
    ln2_shift,
    up_weight,
    up_shift,
    down_weight,
    final_gain,
    final_shift,
    bridge_weight,
    codebook,
    codes,
    doc_lengths,
):
    section = lax.axis_index("section")
    encoder_side = section == 0
    micro = doc_lengths.shape[0]
    groups = micro // 2
    rows = section_in.shape[1] // micro
    width = section_in.shape[2]
    hidden_width = up_weight.shape[2]
    latent_width = bridge_weight.shape[1]
    per_device = codebook.shape[1]

    vectors = jnp.concatenate(
        [ln1_gain, ln1_shift, ln2_gain, ln2_shift, final_gain, final_shift, up_shift.reshape(-1, width)],
        axis=0,
    )
    bridge = jnp.pad(bridge_weight[0], ((0, LANES - latent_width), (0, 0)))
    own = (vectors, qkv_weight[0], out_weight[0], up_weight[0], down_weight[0], bridge)
    other = tuple(from_section(member) for member in own)

    def split(member, received):
        return (
            jnp.where(encoder_side, member, received),
            jnp.where(encoder_side, received, member),
        )

    pairs = [split(member, received) for member, received in zip(own, other)]

    def weights_of(side):
        vector, qkv_w, out_w, up_w, down_w, bridge_w = [pair[side] for pair in pairs]
        return dict(
            ln1_gain=vector[0:1],
            ln1_shift=vector[1:2],
            qkv_w=qkv_w,
            out_w=out_w,
            ln2_gain=vector[2:3],
            ln2_shift=vector[3:4],
            up_w=up_w,
            up_shift=vector[6:].reshape(1, hidden_width),
            down_w=down_w,
            final_gain=vector[4:5],
            final_shift=vector[5:6],
            bridge=bridge_w,
        )

    encoder, decoder = weights_of(0), weights_of(1)

    halves = section_in[0].reshape(2, groups, rows, width)
    mine = lax.dynamic_index_in_dim(halves, section, 0, keepdims=False)
    theirs = from_section(lax.dynamic_index_in_dim(halves, 1 - section, 0, keepdims=False))
    patch = jnp.where(encoder_side, mine, theirs)
    cotangent = jnp.where(encoder_side, theirs, mine)
    lengths = lax.dynamic_slice_in_dim(doc_lengths, section * groups, groups, 0)
    own_codes = lax.dynamic_slice_in_dim(codes, section * groups * rows, groups * rows, 0)

    inverse = lax.rsqrt(jnp.sum(codebook * codebook, axis=0, keepdims=True) + EPS)
    unit_codes = codebook * inverse
    quarter = per_device // 4
    packed = (
        unit_codes.reshape(latent_width, 4, quarter).transpose(2, 1, 0).reshape(quarter, 4 * latent_width)
    )
    table = lax.all_gather(packed, ("section", "dp"), axis=0, tiled=True)

    short = ["ln1_gain", "ln1_shift", "qkv_w", "out_w"]
    names = short + ["ln2_gain", "ln2_shift", "up_w", "up_shift", "down_w", "final_gain", "final_shift", "bridge"]
    where = jnp.stack([section, lax.axis_index("dp") & (CHUNKS - 1)]).astype(jnp.int32)
    saved_qkv = Token((3 * PAIRS, rows, LANES), HALF)
    saved_lse = Token((HEADS, rows), FULL)
    saved_mixed = Token((PAIRS, rows, LANES), HALF)
    wide = Token((rows, width), FULL)
    hidden = Token((rows, hidden_width), HALF)
    bias_scratch = pltpu.VMEM((rows, rows), FULL)
    lse_scratch = pltpu.VMEM((rows, LANES), FULL)

    qkv_e, lse_e, mixed_e, middle_e, slope_e, active_e, result_e, latent = run_groups(
        encoder_forward_kernel,
        "encoder_forward",
        groups,
        [lengths],
        [patch],
        [encoder[name] for name in names],
        [saved_qkv, saved_lse, saved_mixed, wide, hidden, hidden, wide, Token((rows, LANES), FULL)],
        [bias_scratch, lse_scratch],
        24 << 30,
    )

    count = groups * rows
    vmem = pl.BlockSpec(memory_space=pltpu.VMEM)
    quant, book = pl.pallas_call(
        functools.partial(quant_kernel, per_device),
        in_specs=[pl.BlockSpec(memory_space=pltpu.SMEM), vmem, vmem, vmem],
        out_specs=[vmem, vmem],
        out_shape=[
            jax.ShapeDtypeStruct((count, LANES), HALF),
            jax.ShapeDtypeStruct(table.shape, FULL),
        ],
        scratch_shapes=[pltpu.VMEM((count, LANES), FULL), pltpu.VMEM((count, LANES), FULL)],
        compiler_params=pltpu.CompilerParams(vmem_limit_bytes=VMEM_BYTES),
        cost_estimate=pl.CostEstimate(flops=8 << 30, bytes_accessed=0, transcendentals=0),
        name="quantize",
    )(own_codes, own_codes.reshape(count, 1), latent.reshape(count, LANES), table)
    quant = quant.reshape(groups, rows, LANES)

    blocks = 2 * CHUNKS
    down_rows = hidden_width // blocks
    thin_rows = width // blocks
    up_parts = hidden_width // width
    feed_rows = down_rows + up_parts * thin_rows
    attention_rows = 4 * thin_rows
    book_rows = 4 * latent_width * (lax.axis_size("dp") // CHUNKS) * quarter // width
    vector_rows = 4 + up_parts
    feed_sums = [pltpu.VMEM((hidden_width, width), FULL), pltpu.VMEM((width, hidden_width), FULL)]
    feed_sums += [pltpu.VMEM((1, hidden_width), FULL)]
    attention_sums = [pltpu.VMEM((width, 3 * width), FULL), pltpu.VMEM((width, width), FULL)]
    feed_blocks = Whole((CHUNKS, feed_rows, width), HALF)
    two_vectors = Whole((2, width), FULL)
    feed_vector = Whole((vector_rows, width), FULL)
    bridge_grad = Whole((LANES, width), FULL)
    feed_scratch = [pltpu.VMEM((rows, width), HALF), pltpu.VMEM((rows, width), FULL)]
    final, qkv_d, lse_d, mixed_d, middle_d, keep_1, send_1, vectors_1 = run_groups(
        decoder_feed_kernel,
        "decoder_forward_feed_backward",
        groups,
        [lengths, where],
        [quant, cotangent],
        [decoder[name] for name in names],
        [
            Token((rows, width), HALF),
            saved_qkv,
            saved_lse,
            saved_mixed,
            wide,
            feed_blocks,
            feed_blocks,
            feed_vector,
        ],
        [bias_scratch, lse_scratch]
        + [pltpu.VMEM((rows, hidden_width), HALF)] * 2
        + [feed_scratch[0], feed_scratch[1], feed_scratch[1]]
        + feed_sums,
        36 << 30,
    )
    attention_scratch = [
        bias_scratch,
        pltpu.VMEM((PAIRS, rows, LANES), HALF),
        pltpu.VMEM((3 * PAIRS, rows, LANES), HALF),
    ] + attention_sums
    grad_quant, keep_2, send_2, vectors_2, bridge_d = run_groups(
        functools.partial(decoder_attention_kernel, owners=lax.axis_size("dp"), per_owner=quarter),
        "decoder_attention_backward",
        groups,
        [lengths, where],
        [quant, middle_d, qkv_d, lse_d, mixed_d],
        [decoder[name] for name in short] + [decoder["bridge"], book],
        [Token((rows, LANES), HALF)]
        + [Whole((CHUNKS, attention_rows + book_rows, width), HALF)] * 2
        + [two_vectors, bridge_grad],
        attention_scratch,
        20 << 30,
    )
    got_1, got_2 = from_section(send_1), from_section(send_2)
    middle_grad, keep_3, send_3, vectors_3, bridge_e = run_groups(
        encoder_feed_kernel,
        "encoder_feed_backward",
        groups,
        [where],
        [grad_quant, middle_e, result_e, slope_e, active_e],
        [encoder[name] for name in names],
        [wide, feed_blocks, feed_blocks, feed_vector, bridge_grad],
        feed_scratch + feed_sums,
        20 << 30,
    )
    plane_d = add_cores("decoder", [(keep_1, got_1), (keep_2, got_2)])
    got_3 = from_section(send_3)
    grad_qkv, out_sum = run_groups(
        encoder_attention_kernel,
        "encoder_attention_backward",
        groups,
        [lengths],
        [after(middle_grad, plane_d), qkv_e, lse_e, mixed_e],
        [encoder["out_w"]],
        [saved_qkv, Whole((width, width), FULL)],
        attention_scratch[:2],
        20 << 30,
    )
    depth_d = add_plane("decoder", after(exchange(plane_d, PLANE), grad_qkv))
    plane_3 = add_cores("encoder_feed", [(keep_3, after(got_3, grad_qkv))])
    grad_patch, keep_4, send_4, vectors_4 = run_groups(
        encoder_input_kernel,
        "encoder_input_backward",
        groups,
        [where],
        [patch, middle_grad, after(grad_qkv, depth_d, plane_3)],
        [encoder[name] for name in short[:3]] + [out_sum],
        [Token((rows, width), HALF)]
        + [Whole((CHUNKS, attention_rows, width), HALF)] * 2
        + [two_vectors],
        attention_sums[:1],
        8 << 30,
    )
    def flat(attention_vectors, feed_vectors_, bridge_part):
        return jnp.concatenate([attention_vectors, feed_vectors_, bridge_part[:latent_width]], axis=0)

    small_e = flat(vectors_4, vectors_3, bridge_e)
    small_d = flat(vectors_2, vectors_1, bridge_d)
    small_rows = -(-small_e.shape[0] // 16) * 16
    grown = ((0, small_rows - small_e.shape[0]), (0, 0))
    small = jnp.pad(jnp.where(encoder_side, small_e, small_d), grown)
    small_got = from_section(jnp.pad(low(jnp.where(encoder_side, small_d, small_e)), grown))

    depth_3 = add_plane("encoder_feed", after(exchange(plane_3, PLANE), grad_patch))
    got_4 = after(from_section(send_4), depth_3)
    plane_4 = add_cores("encoder_attention", [(keep_4, got_4)])
    small = total_of(small, after(small_got, plane_4))
    small_plane = exchange([small] * 4, PLANE)
    chunk_d = add_far(add_depth("decoder", after(exchange(depth_d, DEPTH), plane_4, small)))
    decoder_rows = feed_rows + attention_rows
    deep_d = gather_depth(chunk_d[:decoder_rows])
    depth_4 = add_plane("encoder_attention", after(exchange(plane_4, PLANE), chunk_d))
    small = total_of(*after(small_plane, depth_4))
    small_depth = exchange([small] * 4, DEPTH)
    half_d = gather_plane(after(deep_d, depth_4))
    chunk_e = add_far(
        add_depth("encoder", after(exchange(depth_3, DEPTH), depth_4), after(exchange(depth_4, DEPTH), deep_d))
    )
    deep_e = gather_depth_for(chunk_e, 0)
    small = total_of(*after(small_depth, deep_e))
    bit = CHUNKS
    while bit < lax.axis_size("dp"):
        small = total_of(small, from_dp(small, bit))
        bit = 2 * bit
    small = small.astype(FULL)
    gathered = gather_plane_for(deep_e, 0)
    half_d = after(half_d, deep_e)
    halves_d = (half_d, lax.ppermute(half_d, "section", [(0, 1)]))

    feed_segments = [(0, down_rows, 0, 0)] + [
        (down_rows + part * thin_rows, thin_rows, 1, part * width) for part in range(up_parts)
    ]
    attention_segments = [(0, thin_rows, 3, 0)] + [
        ((part + 1) * thin_rows, thin_rows, 2, part * width) for part in range(3)
    ]
    segments = feed_segments + [
        (feed_rows + offset, size, target, column) for offset, size, target, column in attention_segments
    ]
    given = gathered + list(halves_d)
    down_total, up_total, qkv_total, out_total = pl.pallas_call(
        functools.partial(unpack_kernel, segments),
        in_specs=[pl.BlockSpec(memory_space=pltpu.SMEM)] + [vmem] * len(given),
        out_specs=[vmem] * 4,
        out_shape=[
            jax.ShapeDtypeStruct(shape, FULL)
            for shape in (
                (hidden_width, width),
                (width, hidden_width),
                (width, 3 * width),
                (width, width),
            )
        ],
        compiler_params=pltpu.CompilerParams(vmem_limit_bytes=VMEM_BYTES),
        name="unpack",
    )(where, *given)

    book_sum = chunk_d[decoder_rows:].astype(FULL)
    book_sum = book_sum.reshape(book_rows, 4, LANES).transpose(1, 0, 2).reshape(-1, quarter, LANES)
    book_own = lax.dynamic_index_in_dim(book_sum, lax.axis_index("dp") // CHUNKS, 0, keepdims=False)
    book_grad = (
        book_own.reshape(quarter, 4, latent_width).transpose(2, 1, 0).reshape(latent_width, per_device)
    )
    book_grad = inverse * (
        book_grad - unit_codes * jnp.sum(unit_codes * book_grad, axis=0, keepdims=True)
    )

    sent = jnp.where(encoder_side, final, grad_patch)
    kept = jnp.where(encoder_side, grad_patch, final)
    got = from_section(sent)
    section_out = jnp.where(
        encoder_side, jnp.concatenate([kept, got], axis=0), jnp.concatenate([got, kept], axis=0)
    ).reshape(1, micro * rows, width)
    first_vector = 2
    hidden_vector = first_vector + 4
    return (
        section_out,
        small[0:1],
        small[1:2],
        qkv_total[None],
        out_total[None],
        small[2:3],
        small[3:4],
        up_total[None],
        small[hidden_vector : hidden_vector + up_parts].reshape(1, hidden_width),
        down_total[None],
        small[4:5],
        small[5:6],
        small[hidden_vector + up_parts : hidden_vector + up_parts + latent_width][None],
        book_grad,
    )


def solution(mesh):
    placed = (
        P("section", "dp", None),
        P("section", None),
        P("section", None),
        P("section", None, None),
        P("section", None, None),
        P("section", None),
        P("section", None),
        P("section", None, None),
        P("section", None),
        P("section", None, None),
        P("section", None),
        P("section", None),
        P("section", None, None),
        P(None, ("section", "dp")),
        P("dp"),
        P("dp", None),
    )
    return jax.shard_map(
        on_device,
        mesh=mesh,
        in_specs=placed,
        out_specs=(
            P("section", "dp", None),
            P("section", None),
            P("section", None),
            P("section", None, None),
            P("section", None, None),
            P("section", None),
            P("section", None),
            P("section", None, None),
            P("section", None),
            P("section", None, None),
            P("section", None),
            P("section", None),
            P("section", None, None),
            P(None, ("section", "dp")),
        ),
        check_vma=False,
    )
```

```python
import functools

import jax
import jax.numpy as jnp
from jax import lax
from jax.experimental import pallas as pl
from jax.experimental.pallas import tpu as pltpu
from jax.sharding import PartitionSpec as P

HEADS = 8
PAIRS = HEADS // 2
LANES = 128
EPS = 1e-06
GELU_FACTOR = 0.7978845608028654
GELU_CUBIC = 0.044715
BLOCKED = -1000000000.0
CHUNKS = 16
FULL = jnp.float32
HALF = jnp.bfloat16
VMEM_BYTES = 12 * 1024 * 1024


def low(value):
    return value.astype(HALF)


def mm(left, right):
    return lax.dot_general(left, right, (((1,), (0,)), ((), ())), preferred_element_type=FULL)


def mm_nt(left, right):
    return lax.dot_general(left, right, (((1,), (1,)), ((), ())), preferred_element_type=FULL)


def mm_tn(left, right):
    return lax.dot_general(left, right, (((0,), (0,)), ((), ())), preferred_element_type=FULL)


def norm_forward(inputs, gain, shift):
    centred = inputs - jnp.mean(inputs, axis=-1, keepdims=True)
    scaling = lax.rsqrt(jnp.mean(centred * centred, axis=-1, keepdims=True) + EPS)
    normal = centred * scaling
    return normal * gain + shift, normal, scaling


def row_chunks(rows, size=64):
    return [slice(start, start + size) for start in range(0, rows, size)]


def norm_rows(source, target, gain, shift):
    for part in row_chunks(source.shape[0]):
        target[part, :] = low(norm_forward(source[part, :].astype(FULL), gain[...], shift[...])[0])


def write_bias(lengths_ref, group, bias_ref):
    rows = bias_ref.shape[0]
    down = lax.broadcasted_iota(jnp.int32, (rows, rows), 0)
    across = lax.broadcasted_iota(jnp.int32, (rows, rows), 1)
    row_label = jnp.zeros((rows, rows), jnp.int32)
    column_label = jnp.zeros((rows, rows), jnp.int32)
    bound = jnp.int32(0)
    for doc in range(lengths_ref.shape[1]):
        bound = bound + lengths_ref[group, doc]
        row_label = row_label + (down >= bound).astype(jnp.int32)
        column_label = column_label + (across >= bound).astype(jnp.int32)
    bias_ref[...] = jnp.where(row_label == column_label, 0.0, BLOCKED)


def half_mask(rows, side):
    lane = lax.broadcasted_iota(jnp.int32, (rows, LANES), 1)
    return lane < LANES // 2 if side == 0 else lane >= LANES // 2


def attention_forward(qkv_ref, bias_ref, mixed_ref, lse_ref, lse_scratch):
    rows = qkv_ref.shape[1]
    scale = (LANES // 2) ** (-0.5)
    lane = lax.broadcasted_iota(jnp.int32, (rows, LANES), 1)
    lse_scratch[...] = jnp.zeros_like(lse_scratch)

    def pair_step(pair, carry):
        queries = qkv_ref[pair] * jnp.asarray(scale, HALF)
        keys = qkv_ref[PAIRS + pair]
        values = qkv_ref[2 * PAIRS + pair]
        mixed = jnp.zeros((rows, LANES), FULL)
        for side in range(2):
            inside = half_mask(rows, side)
            zero = jnp.zeros((), HALF)
            scores = mm_nt(jnp.where(inside, queries, zero), keys) + bias_ref[...]
            peak = jnp.max(scores, axis=-1, keepdims=True)
            weight = jnp.exp(scores - peak)
            total = jnp.sum(weight, axis=-1, keepdims=True)
            part = mm(low(weight), jnp.where(inside, values, zero))
            mixed = mixed + part * (1.0 / total)
            log_total = peak + jnp.log(total)
            lse_scratch[...] = jnp.where(lane == 2 * pair + side, log_total, lse_scratch[...])
        mixed_ref[pair] = low(mixed)
        return carry

    lax.fori_loop(0, PAIRS, pair_step, 0, unroll=4)
    lse_ref[...] = jnp.transpose(lse_scratch[...])[:HEADS]


def heads_joined(mixed_ref):
    return jnp.concatenate([mixed_ref[pair] for pair in range(PAIRS)], axis=1)


def mix_forward(
    source, weights, bias_ref, qkv_ref, mixed_ref, lse_ref, lse_scratch, normed_ref, middle_ref
):
    ln1_gain, ln1_shift, qkv_w, out_w = weights
    width = source.shape[1]
    norm_rows(source, normed_ref, ln1_gain, ln1_shift)
    for part in range(3):
        projected = low(mm(normed_ref[...], qkv_w[:, part * width : (part + 1) * width]))
        for pair in range(PAIRS):
            qkv_ref[part * PAIRS + pair] = projected[:, pair * LANES : (pair + 1) * LANES]
    attention_forward(qkv_ref, bias_ref, mixed_ref, lse_ref, lse_scratch)
    middle_ref[...] = source[...].astype(FULL) + mm(heads_joined(mixed_ref), out_w[...])


def feed_forward(middle_ref, weights, normed_ref, slope_ref, active_ref, total_ref):
    ln2_gain, ln2_shift, up_w, up_shift, down_w = weights
    hidden_width = up_w.shape[1]
    norm_rows(middle_ref, normed_ref, ln2_gain, ln2_shift)
    tile = middle_ref.shape[1]
    for step in range(hidden_width // tile):
        place = slice(step * tile, (step + 1) * tile)
        hidden = mm(normed_ref[...], up_w[:, place]) + up_shift[:, place]
        square = hidden * hidden
        tangent = jnp.tanh(hidden * ((GELU_FACTOR * GELU_CUBIC) * square + GELU_FACTOR))
        gate = 0.5 * tangent + 0.5
        active = low(hidden * gate)
        bend = hidden * ((1.5 * GELU_FACTOR * GELU_CUBIC) * square + 0.5 * GELU_FACTOR)
        active_ref[:, place] = active
        slope_ref[:, place] = low(gate + bend * (1.0 - tangent * tangent))
        before = middle_ref[...] if step == 0 else total_ref[...]
        total_ref[...] = before + mm(active, down_w[place, :])


def feed_backward(
    upstream_ref,
    middle_ref,
    weights,
    slope_ref,
    active_ref,
    normed_ref,
    branch_ref,
    total_ref,
    down_out,
    up_out,
    up_shift_out,
    grad_middle_ref,
    vector_out,
):
    ln2_gain, ln2_shift, up_w, down_w = weights
    width = upstream_ref.shape[1]
    hidden_width = up_w.shape[1]
    norm_rows(middle_ref, normed_ref, ln2_gain, ln2_shift)
    tile = width

    def hidden_step(step, carry):
        place = pl.ds(step * tile, tile)
        branch = branch_ref[...]
        down_out[place, :] = down_out[place, :] + mm_tn(active_ref[:, place], branch)
        grad_hidden = mm_nt(branch, down_w[place, :]) * slope_ref[:, place].astype(FULL)
        up_shift_out[:, place] = up_shift_out[:, place] + jnp.sum(grad_hidden, axis=0, keepdims=True)
        grad_low = low(grad_hidden)
        up_out[:, place] = up_out[:, place] + mm_tn(normed_ref[...], grad_low)
        share = mm_nt(grad_low, up_w[:, place])
        total_ref[...] = share if step == 0 else total_ref[...] + share
        return carry

    for step in range(hidden_width // tile):
        hidden_step(step, 0)
    norm_backward_rows(
        total_ref, middle_ref, ln2_gain, ln2_shift, vector_out, 0, upstream_ref, grad_middle_ref
    )


def norm_backward_rows(grad_ref, source, gain, shift, vector_out, row, added_ref, *targets):
    width = source.shape[1]
    grad_gain = jnp.zeros((8, width), FULL)
    grad_shift = jnp.zeros((8, width), FULL)
    for part in row_chunks(source.shape[0]):
        _, normal, scaling = norm_forward(source[part, :].astype(FULL), gain[...], shift[...])
        upstream = grad_ref[part, :].astype(FULL)
        scaled = upstream * gain[...]
        inner = scaled - jnp.mean(scaled, axis=-1, keepdims=True)
        inner = inner - normal * jnp.mean(scaled * normal, axis=-1, keepdims=True)
        grad = scaling * inner
        if added_ref is not None:
            grad = grad + added_ref[part, :]
        for target in targets:
            target[part, :] = grad.astype(target.dtype)
        folded = (upstream.shape[0] // 8, 8, width)
        grad_gain = grad_gain + jnp.sum((upstream * normal).reshape(folded), axis=0)
        grad_shift = grad_shift + jnp.sum(upstream.reshape(folded), axis=0)
    add_row(vector_out, row, jnp.sum(grad_gain, axis=0, keepdims=True))
    add_row(vector_out, row + 1, jnp.sum(grad_shift, axis=0, keepdims=True))


def attention_backward(qkv_ref, grad_mixed_ref, bias_ref, lse_ref, grad_qkv_ref):
    rows = qkv_ref.shape[1]
    scale = (LANES // 2) ** (-0.5)

    def pair_step(pair, carry):
        queries = qkv_ref[pair] * jnp.asarray(scale, HALF)
        keys = qkv_ref[PAIRS + pair]
        values = qkv_ref[2 * PAIRS + pair]
        grads = grad_mixed_ref[pair]
        grad_queries = jnp.zeros((rows, LANES), FULL)
        grad_keys = jnp.zeros((rows, LANES), FULL)
        grad_values = jnp.zeros((rows, LANES), FULL)
        for side in range(2):
            inside = half_mask(rows, side)
            zero = jnp.zeros((), HALF)
            side_queries = jnp.where(inside, queries, zero)
            side_grads = jnp.where(inside, grads, zero)
            scores = mm_nt(keys, side_queries) + bias_ref[...]
            attention = jnp.exp(scores - lse_ref[pl.ds(2 * pair + side, 1), :])
            grad_values = grad_values + mm(low(attention), side_grads)
            grad_attention = mm_nt(values, side_grads)
            delta = jnp.sum(attention * grad_attention, axis=0, keepdims=True)
            grad_scores = low(attention * (grad_attention - delta))
            grad_keys = grad_keys + mm(grad_scores, side_queries)
            grad_queries = grad_queries + mm_tn(grad_scores, jnp.where(inside, keys, zero))
        grad_qkv_ref[pair] = low(grad_queries * scale)
        grad_qkv_ref[PAIRS + pair] = low(grad_keys)
        grad_qkv_ref[2 * PAIRS + pair] = low(grad_values)
        return carry

    lax.fori_loop(0, PAIRS, pair_step, 0, unroll=4)


def attention_gradients(
    grad_middle, out_w, bias_ref, qkv_ref, mixed_ref, lse_ref, grad_mixed_ref, grad_qkv_ref, out_out
):
    grad_low = low(grad_middle)
    out_out[...] = out_out[...] + mm_tn(heads_joined(mixed_ref), grad_low)
    grad_mixed = low(mm_nt(grad_low, out_w[...]))
    for pair in range(PAIRS):
        grad_mixed_ref[pair] = grad_mixed[:, pair * LANES : (pair + 1) * LANES]
    attention_backward(qkv_ref, grad_mixed_ref, bias_ref, lse_ref, grad_qkv_ref)


def projection_gradients(
    source, grad_middle_ref, ln1_gain, ln1_shift, qkv_w, grad_qkv_ref, qkv_out, normed_ref, total_ref, vector_out, target
):
    width = source.shape[1]
    norm_rows(source, normed_ref, ln1_gain, ln1_shift)
    for part in range(3):
        grad_part = jnp.concatenate(
            [grad_qkv_ref[part * PAIRS + pair] for pair in range(PAIRS)], axis=1
        )
        place = slice(part * width, (part + 1) * width)
        qkv_out[:, place] = qkv_out[:, place] + mm_tn(normed_ref[...], grad_part)
        share = mm_nt(grad_part, qkv_w[:, place])
        total_ref[...] = share if part == 0 else total_ref[...] + share
    norm_backward_rows(total_ref, source, ln1_gain, ln1_shift, vector_out, 0, grad_middle_ref, target)


def unit_rows(rows):
    inverse = lax.rsqrt(jnp.sum(rows * rows, axis=-1, keepdims=True) + EPS)
    return rows * inverse, inverse


def start_totals(*refs):
    @pl.when(pl.program_id(0) == 0)
    def _():
        for ref in refs:
            ref[...] = jnp.zeros_like(ref)


def encoder_mix_kernel(
    lengths,
    patch,
    ln1_gain,
    ln1_shift,
    qkv_w,
    out_w,
    qkv_ref,
    lse_ref,
    mixed_ref,
    middle_ref,
    bias_ref,
    lse_scratch,
    normed_ref,
):
    write_bias(lengths, pl.program_id(0), bias_ref)
    mix_forward(
        patch,
        (ln1_gain, ln1_shift, qkv_w, out_w),
        bias_ref,
        qkv_ref,
        mixed_ref,
        lse_ref,
        lse_scratch,
        normed_ref,
        middle_ref,
    )


def encoder_latent_kernel(
    middle,
    ln2_gain,
    ln2_shift,
    up_w,
    up_shift,
    down_w,
    final_gain,
    final_shift,
    bridge,
    slope_ref,
    active_ref,
    result_ref,
    latent_ref,
    normed_ref,
):
    weights = (ln2_gain, ln2_shift, up_w, up_shift, down_w)
    feed_forward(middle, weights, normed_ref, slope_ref, active_ref, result_ref)
    norm_rows(result_ref, normed_ref, final_gain, final_shift)
    latent_ref[...] = unit_rows(mm_nt(normed_ref[...], bridge[...]))[0]


def quant_kernel(places, block_column, latent, *refs):
    pieces, (quant_ref, book_ref, table, gathered, spread, semaphore) = refs[:-6], refs[-6:]
    count = gathered.shape[0]
    size = pieces[0].shape[0]
    copies = [
        pltpu.make_async_copy(piece, table.at[pl.ds(number * size, size)], semaphore.at[number])
        for number, piece in enumerate(pieces)
    ]
    for copy in copies:
        copy.start()
    for copy in copies:
        copy.wait()

    def gather(index, carry):
        gathered[pl.ds(index, 1), :] = table[pl.ds(places[index], 1), :]
        return carry

    lax.fori_loop(0, count, gather, 0, unroll=16)
    block = block_column[...]
    lane = lax.broadcasted_iota(jnp.int32, (count, LANES), 1)
    width = LANES // 4
    rows = gathered[...]
    code = jnp.where(block == 0, rows, 0.0)
    for place in range(1, 4):
        code = code + jnp.where(block == place, pltpu.roll(rows, LANES - width * place, 1), 0.0)
    code = jnp.where(lane < width, code, 0.0)
    held = latent[...]
    quant_ref[...] = low(held + (code - held))
    grad = 2.0 * (code - held)
    placed = jnp.where(block == 0, grad, 0.0)
    for place in range(1, 4):
        placed = placed + jnp.where(block == place, pltpu.roll(grad, width * place, 1), 0.0)
    spread[...] = placed
    book_ref[...] = jnp.zeros_like(book_ref)

    def scatter(index, carry):
        place = pl.ds(places[index], 1)
        book_ref[place, :] = book_ref[place, :] + spread[pl.ds(index, 1), :]
        return carry

    lax.fori_loop(0, count, scatter, 0, unroll=8)


def add_row(ref, row, value):
    ref[row : row + 1, :] = ref[row : row + 1, :] + value


def feed_vectors(vector_out, up_shift_acc):
    width = vector_out.shape[1]
    for part in range(up_shift_acc.shape[1] // width):
        vector_out[4 + part : 5 + part, :] = up_shift_acc[:, part * width : (part + 1) * width]


def last_group():
    return pl.program_id(0) == pl.num_programs(0) - 1


def decoder_feed_kernel(
    lengths,
    where,
    quant,
    cotangent,
    ln1_gain,
    ln1_shift,
    qkv_w,
    out_w,
    ln2_gain,
    ln2_shift,
    up_w,
    up_shift,
    down_w,
    final_gain,
    final_shift,
    bridge,
    final_ref,
    qkv_ref,
    lse_ref,
    mixed_ref,
    grad_middle_ref,
    keep_ref,
    send_ref,
    vector_out,
    bias_ref,
    lse_scratch,
    slope_ref,
    active_ref,
    normed_ref,
    branch_ref,
    source_ref,
    middle_ref,
    result_ref,
    upstream_ref,
    down_acc,
    up_acc,
    up_shift_acc,
):
    start_totals(down_acc, up_acc, up_shift_acc, vector_out)
    write_bias(lengths, pl.program_id(0), bias_ref)
    source_ref[...] = mm(quant[...], bridge[...])
    mix_forward(
        source_ref,
        (ln1_gain, ln1_shift, qkv_w, out_w),
        bias_ref,
        qkv_ref,
        mixed_ref,
        lse_ref,
        lse_scratch,
        normed_ref,
        middle_ref,
    )
    weights = (ln2_gain, ln2_shift, up_w, up_shift, down_w)
    feed_forward(middle_ref, weights, normed_ref, slope_ref, active_ref, result_ref)
    norm_rows(result_ref, final_ref, final_gain, final_shift)
    norm_backward_rows(
        cotangent, result_ref, final_gain, final_shift, vector_out, 2, None, upstream_ref, branch_ref
    )
    feed_backward(
        upstream_ref,
        middle_ref,
        (ln2_gain, ln2_shift, up_w, down_w),
        slope_ref,
        active_ref,
        normed_ref,
        branch_ref,
        result_ref,
        down_acc,
        up_acc,
        up_shift_acc,
        grad_middle_ref,
        vector_out,
    )

    @pl.when(last_group())
    def _():
        feed_vectors(vector_out, up_shift_acc)
        pieces = [rows_of(down_acc)] + column_parts(up_acc, middle_ref.shape[1])
        store_blocks(where, keep_ref, send_ref, pieces)


def decoder_input_kernel(
    where,
    quant,
    grad_middle,
    grad_qkv_ref,
    ln1_gain,
    ln1_shift,
    qkv_w,
    bridge,
    book,
    out_sum,
    feed_vector,
    grad_quant_ref,
    keep_ref,
    send_ref,
    vector_out,
    bridge_out,
    qkv_acc,
    normed_ref,
    source_ref,
    total_ref,
    grad_lift_ref,
    small_ref,
    *,
    owners,
    per_owner,
    latent,
):
    start_totals(qkv_acc, vector_out, bridge_out)
    source_ref[...] = mm(quant[...], bridge[...])
    projection_gradients(
        source_ref,
        grad_middle,
        ln1_gain,
        ln1_shift,
        qkv_w,
        grad_qkv_ref,
        qkv_acc,
        normed_ref,
        total_ref,
        vector_out,
        grad_lift_ref,
    )
    bridge_out[...] = bridge_out[...] + mm_tn(quant[...], grad_lift_ref[...])
    grad_quant_ref[...] = low(mm_nt(grad_lift_ref[...], bridge[...]))

    @pl.when(last_group())
    def _():
        pieces = [rows_of(out_sum)] + column_parts(qkv_acc, source_ref.shape[1])
        spread_rows(small_ref, (vector_out, 2), (feed_vector, feed_vector.shape[0]), (bridge_out, latent))
        pieces = pieces + [lambda block: small_ref[block], codebook_rows(where, book, per_owner, owners)]
        store_blocks(where, keep_ref, send_ref, pieces, relative=False)


def encoder_feed_kernel(
    where,
    grad_quant,
    middle,
    result,
    slope_ref,
    active_ref,
    ln2_gain,
    ln2_shift,
    up_w,
    down_w,
    final_gain,
    final_shift,
    bridge,
    grad_middle_ref,
    keep_ref,
    send_ref,
    vector_out,
    bridge_out,
    normed_ref,
    branch_ref,
    grad_ref,
    upstream_ref,
    down_acc,
    up_acc,
    up_shift_acc,
):
    start_totals(down_acc, up_acc, up_shift_acc, vector_out, bridge_out)
    norm_rows(result, normed_ref, final_gain, final_shift)
    feature = normed_ref[...]
    latent, inverse = unit_rows(mm_nt(feature, bridge[...]))
    grad_latent = grad_quant[...].astype(FULL)
    grad_projection = low(
        inverse * (grad_latent - latent * jnp.sum(latent * grad_latent, axis=1, keepdims=True))
    )
    bridge_out[...] = bridge_out[...] + mm_tn(grad_projection, feature)
    grad_ref[...] = mm(grad_projection, bridge[...])
    norm_backward_rows(
        grad_ref, result, final_gain, final_shift, vector_out, 2, None, upstream_ref, branch_ref
    )
    feed_backward(
        upstream_ref,
        middle,
        (ln2_gain, ln2_shift, up_w, down_w),
        slope_ref,
        active_ref,
        normed_ref,
        branch_ref,
        grad_ref,
        down_acc,
        up_acc,
        up_shift_acc,
        grad_middle_ref,
        vector_out,
    )

    @pl.when(last_group())
    def _():
        feed_vectors(vector_out, up_shift_acc)
        pieces = [rows_of(down_acc)] + column_parts(up_acc, middle.shape[1])
        store_blocks(where, keep_ref, send_ref, pieces)


def attention_backward_kernel(
    lengths,
    grad_middle,
    qkv_ref,
    lse_ref,
    mixed_ref,
    out_w,
    grad_qkv_ref,
    out_acc,
    bias_ref,
    grad_mixed_ref,
):
    start_totals(out_acc)
    write_bias(lengths, pl.program_id(0), bias_ref)
    attention_gradients(
        grad_middle[...], out_w, bias_ref, qkv_ref, mixed_ref, lse_ref, grad_mixed_ref, grad_qkv_ref, out_acc
    )


def encoder_input_kernel(
    where,
    patch,
    grad_middle,
    grad_qkv_ref,
    ln1_gain,
    ln1_shift,
    qkv_w,
    out_sum,
    feed_vector,
    bridge_sum,
    grad_patch_ref,
    keep_ref,
    send_ref,
    vector_out,
    qkv_acc,
    normed_ref,
    total_ref,
    small_ref,
    *,
    latent,
):
    start_totals(qkv_acc, vector_out)
    projection_gradients(
        patch,
        grad_middle,
        ln1_gain,
        ln1_shift,
        qkv_w,
        grad_qkv_ref,
        qkv_acc,
        normed_ref,
        total_ref,
        vector_out,
        grad_patch_ref,
    )

    @pl.when(last_group())
    def _():
        spread_rows(small_ref, (vector_out, 2), (feed_vector, feed_vector.shape[0]), (bridge_sum, latent))
        pieces = [rows_of(out_sum)] + column_parts(qkv_acc, patch.shape[1])
        store_blocks(where, keep_ref, send_ref, pieces + [lambda block: small_ref[block]])


def store_blocks(where, keep_ref, send_ref, pieces, relative=True):
    def step(index, carry):
        if relative:
            chunk = jnp.bitwise_xor(index, where[1])
        else:
            chunk = 4 * jnp.bitwise_xor(index & 3, where[1] >> 2) + (index >> 2)
        for side, ref in ((0, keep_ref), (1, send_ref)):
            block = 2 * chunk + jnp.bitwise_xor(where[0], side)
            offset = 0
            for piece in pieces:
                values = piece(block)
                count = values.shape[0]
                ref[index, offset : offset + count, :] = low(values)
                offset += count
        return carry

    lax.fori_loop(0, CHUNKS, step, 0)


def rows_of(ref, part=None):
    count = ref.shape[0] // (2 * CHUNKS)

    def piece(block):
        place = pl.ds(pl.multiple_of(block * count, count), count)
        if part is None:
            return ref[place, :]
        return ref[place, part]

    return piece


def column_parts(ref, width):
    return [rows_of(ref, slice(start, start + width)) for start in range(0, ref.shape[1], width)]


def codebook_rows(where, book_ref, per_owner, owners):
    def piece(block):
        side = jnp.bitwise_xor(block & 1, where[0])
        chunk = jnp.bitwise_xor(block >> 1, where[1])
        near = 4 * (chunk & 3) + (chunk >> 2)
        rows = []
        for high in range(owners // CHUNKS):
            far = jnp.bitwise_xor(high, where[2]) if owners > CHUNKS else 0
            owner = side * owners + far * CHUNKS + near
            rows.append(book_ref[pl.ds(pl.multiple_of(owner * per_owner, per_owner), per_owner), :])
        joined = jnp.concatenate(rows, axis=0) if len(rows) > 1 else rows[0]
        count = joined.shape[0] // 4
        return jnp.concatenate([joined[part * count : (part + 1) * count] for part in range(4)], axis=1)

    return piece


def spread_rows(target, *sources):
    target[...] = jnp.zeros_like(target)
    rows = [(ref, row) for ref, count in sources for row in range(count)]
    each = -(-len(rows) // target.shape[0])
    for number, (ref, row) in enumerate(rows):
        block, place = number // each, number % each
        target[block, place : place + 1, :] = ref[row : row + 1, :]


class Token:
    def __init__(self, shape, dtype):
        self.shape, self.dtype = shape, dtype

    def struct(self, groups):
        return jax.ShapeDtypeStruct((groups,) + self.shape, self.dtype)


    def spec(self):
        tail = (0,) * len(self.shape)
        return pl.BlockSpec((None,) + self.shape, lambda group: (group,) + tail)


class Parked(Token):
    def struct(self, groups):
        return pltpu.HBM((groups,) + self.shape, self.dtype)


class Whole:
    def __init__(self, shape, dtype):
        self.shape, self.dtype = shape, dtype

    def struct(self, groups):
        return jax.ShapeDtypeStruct(self.shape, self.dtype)

    def spec(self):
        zeros = (0,) * len(self.shape)
        return pl.BlockSpec(self.shape, lambda group: zeros, pipeline_mode=pl.Buffered(1))


class Loaded:
    def __init__(self, where, side, own, other, held, semaphore):
        self.shape = held.shape
        self.copies = [pltpu.make_async_copy(source, held, semaphore) for source in (own, other)]
        self.where, self.side, self.held, self.waited = where, side, held, False

    def start(self):
        @pl.when(self.where[0] == self.side)
        def _():
            self.copies[0].start()

        @pl.when(self.where[0] != self.side)
        def _():
            self.copies[1].start()

    def __getitem__(self, place):
        if not self.waited:
            self.waited = True

            @pl.when(pl.program_id(0) == 0)
            def _():
                self.copies[0].wait()

        return self.held[place]


def run_groups(
    kernel, name, groups, scalars, tokens, wholes, outs, scratch, flops, vmem, where=None, side=None
):
    in_place = pl.BlockSpec(memory_space=pltpu.HBM)
    pairs = [member for member in wholes if isinstance(member, tuple)]
    if pairs:
        scalars = [where] + list(scalars)
    specs = [pl.BlockSpec(memory_space=pltpu.SMEM)] * len(scalars)
    specs += [Token(array.shape[1:], array.dtype).spec() for array in tokens]
    given = list(scalars) + list(tokens)
    for member in wholes:
        if isinstance(member, tuple):
            specs += [in_place] * 2
            given += list(member)
        else:
            specs.append(Whole(member.shape, member.dtype).spec())
            given.append(member)
    held = [pltpu.VMEM(own.shape, own.dtype) for own, _ in pairs]
    semaphores = [pltpu.SemaphoreType.DMA((len(pairs),))] if pairs else []

    def body(*refs):
        if not pairs:
            return kernel(*refs)
        place, refs = refs[0], list(refs[1:])
        semaphore, refs = refs[-1], refs[:-1]
        holders, refs = refs[len(refs) - len(pairs) :], refs[: len(refs) - len(pairs)]
        first = len(scalars) - 1 + len(tokens)
        arguments, rest = refs[:first], refs[first:]
        weights = []
        for member in wholes:
            if isinstance(member, tuple):
                number = len(weights)
                weights.append(
                    Loaded(place, side, rest[0], rest[1], holders[number], semaphore.at[number])
                )
                arguments.append(weights[-1])
                rest = rest[2:]
            else:
                arguments.append(rest[0])
                rest = rest[1:]

        @pl.when(pl.program_id(0) == 0)
        def _():
            for weight in weights:
                weight.start()

        return kernel(*arguments, *rest)

    return pl.pallas_call(
        body,
        grid=(groups,),
        in_specs=specs,
        out_specs=[out.spec() for out in outs],
        out_shape=[out.struct(groups) for out in outs],
        scratch_shapes=list(scratch) + held + semaphores,
        compiler_params=pltpu.CompilerParams(vmem_limit_bytes=vmem << 20),
        cost_estimate=pl.CostEstimate(flops=flops, bytes_accessed=0, transcendentals=0),
        name=name,
    )(*given)


def from_section(block):
    return lax.ppermute(block, "section", [(0, 1), (1, 0)])


def from_dp(block, mask):
    count = lax.axis_size("dp")
    return lax.ppermute(block, "dp", [(place, place ^ mask) for place in range(count)])


def from_dp_of(block, mask, side):
    count = lax.axis_size("dp")
    first = side * count
    route = [(first + place, first + (place ^ mask)) for place in range(count)]
    return lax.ppermute(block, ("section", "dp"), route)


def small_call(kernel, name, outs, *given):
    vmem = pl.BlockSpec(memory_space=pltpu.VMEM)
    size = sum(member.size * member.dtype.itemsize for member in given)
    return pl.pallas_call(
        kernel,
        in_specs=[vmem] * len(given),
        out_specs=[vmem] * len(outs),
        out_shape=[jax.ShapeDtypeStruct(shape, HALF) for shape in outs],
        compiler_params=pltpu.CompilerParams(vmem_limit_bytes=VMEM_BYTES),
        cost_estimate=pl.CostEstimate(flops=0, bytes_accessed=2 * size, transcendentals=0),
        name=name,
    )(*given)


def total_of(*values):
    total = values[0].astype(FULL)
    for value in values[1:]:
        total = total + value.astype(FULL)
    return low(total)


PLANE, DEPTH = (1, 2, 3), (4, 8, 12)


def groups_of(masks):
    count = lax.axis_size("dp")
    return [[place ^ mask for mask in (0,) + masks] for place in range(count) if place & masks[2] == 0]


def exchange(blocks, masks):
    return [blocks[0]] + [from_dp(block, mask) for block, mask in zip(blocks[1:], masks)]


def add_cores(name, batches):
    rows = sum(kept.shape[1] for kept, _ in batches)
    width = batches[0][0].shape[2]

    def kernel(*refs):
        outs = refs[-4:]
        for chunk in range(CHUNKS):
            start = 0
            for number in range(len(batches)):
                value = total_of(refs[2 * number][chunk], refs[2 * number + 1][chunk])
                outs[chunk % 4][chunk // 4, start : start + value.shape[0], :] = value
                start += value.shape[0]

    flat = [member for batch in batches for member in batch]
    return small_call(kernel, name + "_cores", [(CHUNKS // 4, rows, width)] * 4, *flat)


def add_plane(name, members, joined=None):
    rows = members[0].shape[1]
    shape = (rows + (joined.shape[1] if joined is not None else 0), members[0].shape[2])

    def kernel(*refs):
        for place in range(4):
            out = refs[-4 + place]
            out[:rows, :] = total_of(*[ref[place] for ref in refs[:4]])
            if joined is not None:
                out[rows:, :] = refs[4][place]

    given = list(members) + ([joined] if joined is not None else [])
    return small_call(kernel, name + "_plane", [shape] * 4, *given)


def add_depth(name, *batches):
    rows = sum(batch[0].shape[0] for batch in batches)

    def kernel(*refs):
        start = 0
        for number in range(len(batches)):
            value = total_of(*[ref[...] for ref in refs[4 * number : 4 * number + 4]])
            refs[-1][start : start + value.shape[0], :] = value
            start += value.shape[0]

    flat = [member for batch in batches for member in batch]
    return small_call(kernel, name + "_depth", [(rows, flat[0].shape[1])], *flat)[0]


def add_far(chunk):
    bit = CHUNKS
    while bit < lax.axis_size("dp"):
        chunk = total_of(chunk, from_dp(chunk, bit))
        bit = 2 * bit
    return chunk


def gather_depth_for(chunk, side):
    own = jnp.stack([chunk, from_section(chunk)])
    return jnp.stack([own] + [from_dp_of(own, mask, side) for mask in DEPTH])


def gather_plane_for(deep, side):
    return [deep] + [from_dp_of(deep, mask, side) for mask in PLANE]


def join_cores(name, batches):
    rows = sum(kept.shape[1] for kept, _ in batches)
    width = batches[0][0].shape[2]

    def kernel(*refs):
        def step(chunk, carry):
            start = 0
            for number in range(len(batches)):
                value = total_of(refs[2 * number][chunk], refs[2 * number + 1][chunk])
                refs[-1][chunk, start : start + value.shape[0], :] = value
                start += value.shape[0]
            return carry

        lax.fori_loop(0, CHUNKS, step, 0, unroll=2)

    flat = [member for batch in batches for member in batch]
    return small_call(kernel, name + "_cores", [(CHUNKS, rows, width)], *flat)[0]


def scatter_group(blocks, masks):
    total = lax.psum_scatter(
        blocks.reshape(-1, blocks.shape[-1]),
        "dp",
        scatter_dimension=0,
        tiled=True,
        axis_index_groups=groups_of(masks),
    )
    return total.reshape(blocks.shape[1:])


def gather_group(block, masks):
    joined = lax.all_gather(
        block.reshape(-1, block.shape[-1]),
        "dp",
        axis=0,
        tiled=True,
        axis_index_groups=groups_of(masks),
    )
    return joined.reshape((4,) + block.shape)


def store_segments(outs, segments, block, piece, start, end):
    for offset, size, target, column in segments:
        first, last = max(start, offset), min(end, offset + size)
        if first < last:
            place = pl.ds(pl.multiple_of(block * size + (first - offset), 16), last - first)
            values = piece[first - start : last - start, :]
            outs[target][place, column : column + values.shape[1]] = values.astype(FULL)


def unpack_kernel(feed_segments, attention_segments, segments, where, *refs):
    encoder, decoder, outs, small_out = refs[:4], refs[4:8], refs[8:-1], refs[-1]
    few = small_out.shape[1]
    rows = feed_segments[-1][0] + feed_segments[-1][1] + attention_segments[-1][0] + attention_segments[-1][1]
    attention_rows = rows - decoder[0].shape[2]

    @pl.when(where[0] == 0)
    def _():
        def step(deep, carry):
            for flat in range(4):
                chunk = jnp.bitwise_xor(4 * deep + flat, where[1])
                for side in range(2):
                    block = 2 * chunk + jnp.bitwise_xor(where[0], side)
                    piece = encoder[flat].at[deep, side]
                    store_segments(outs, segments, block, piece, 0, rows)
                    small_out[block] = piece[rows : rows + few, :].astype(FULL)
            return carry

        lax.fori_loop(0, 4, step, 0)

    @pl.when(where[0] != 0)
    def _():
        def step(deep, carry):
            for flat in range(4):
                for side in range(2):
                    chunk = jnp.bitwise_xor(4 * deep, where[1] & 12) + flat
                    block = 2 * chunk + jnp.bitwise_xor(where[0], side)
                    piece = decoder[2 * side].at[flat, deep]
                    store_segments(outs, feed_segments, block, piece, 0, piece.shape[0])
                    chunk = jnp.bitwise_xor(4 * deep + flat, where[1])
                    block = 2 * chunk + jnp.bitwise_xor(where[0], side)
                    piece = decoder[2 * side + 1].at[flat, deep]
                    store_segments(outs, attention_segments, block, piece, 0, attention_rows)
                    small_out[block] = piece[attention_rows : attention_rows + few, :].astype(FULL)
            return carry

        lax.fori_loop(0, 4, step, 0)


def after(value, *others):
    return lax.optimization_barrier((value, others))[0]


FEED = ["ln1_gain", "ln1_shift", "qkv_w", "out_w", "ln2_gain", "ln2_shift", "up_w", "up_shift", "down_w"]
ENDS = ["final_gain", "final_shift", "bridge"]


def picked(weights, names):
    return [weights[name] for name in names]


class Sizes:
    def __init__(self, width, hidden, groups, rows):
        self.groups, self.rows, self.width, self.hidden = groups, rows, width, hidden
        blocks = 2 * CHUNKS
        self.down_rows = self.hidden // blocks
        self.thin_rows = self.width // blocks
        self.up_parts = self.hidden // self.width
        self.feed_rows = self.down_rows + self.up_parts * self.thin_rows
        self.attention_rows = 4 * self.thin_rows
        self.small_rows = 16
        rows, width = self.rows, self.width
        self.qkv = Token((3 * PAIRS, rows, LANES), HALF)
        self.lse = Token((HEADS, rows), FULL)
        self.mixed = Token((PAIRS, rows, LANES), HALF)
        self.wide = Token((rows, width), FULL)
        self.wide_low = Token((rows, width), HALF)
        self.hidden_low = Token((rows, self.hidden), HALF)
        self.parked_qkv = Parked((3 * PAIRS, rows, LANES), HALF)
        self.parked_mixed = Parked((PAIRS, rows, LANES), HALF)
        self.parked_wide = Parked((rows, width), FULL)
        self.parked_hidden = Parked((rows, self.hidden), HALF)
        self.latent = Token((rows, LANES), FULL)
        self.latent_low = Token((rows, LANES), HALF)
        self.feed_blocks = Whole((CHUNKS, self.feed_rows, width), HALF)
        self.two_vectors = Whole((2, width), FULL)
        self.feed_vector = Whole((4 + self.up_parts, width), FULL)
        self.bridge = Whole((LANES, width), FULL)
        self.bias_scratch = pltpu.VMEM((rows, rows), FULL)
        self.lse_scratch = pltpu.VMEM((rows, LANES), FULL)
        self.wide_scratch = pltpu.VMEM((rows, width), FULL)
        self.low_scratch = pltpu.VMEM((rows, width), HALF)
        self.mixed_scratch = pltpu.VMEM((PAIRS, rows, LANES), HALF)
        self.qkv_scratch = pltpu.VMEM((3 * PAIRS, rows, LANES), HALF)
        self.hidden_scratch = pltpu.VMEM((rows, self.hidden), HALF)
        self.feed_sums = [
            pltpu.VMEM((self.hidden, width), FULL),
            pltpu.VMEM((width, self.hidden), FULL),
            pltpu.VMEM((1, self.hidden), FULL),
        ]
        self.qkv_sum = pltpu.VMEM((width, 3 * width), FULL)
        self.out_sum = pltpu.VMEM((width, width), FULL)
        self.small_sum = pltpu.VMEM((blocks, self.small_rows, width), FULL)

    def blocks(self, rows):
        return [Whole((CHUNKS, rows, self.width), HALF)] * 2


def encoder_mix(z, lengths, where, patch, weights):
    return run_groups(
        encoder_mix_kernel,
        "encoder_mix",
        z.groups,
        [lengths],
        [patch],
        picked(weights, FEED[:4]),
        [z.parked_qkv, z.lse, z.parked_mixed, z.wide],
        [z.bias_scratch, z.lse_scratch, z.low_scratch],
        10 << 30,
        24,
        where,
        0,
    )


def encoder_latent(z, where, middle, weights):
    return run_groups(
        encoder_latent_kernel,
        "encoder_latent",
        z.groups,
        [],
        [middle],
        picked(weights, FEED[4:] + ENDS),
        [z.parked_hidden, z.parked_hidden, z.parked_wide, z.latent],
        [z.low_scratch],
        12 << 30,
        30,
        where,
        0,
    )


def quantize(z, places, block, latent, pieces):
    count = z.groups * z.rows
    vmem = pl.BlockSpec(memory_space=pltpu.VMEM)
    rows = len(pieces) * pieces[0].shape[0]
    quant, book = pl.pallas_call(
        quant_kernel,
        in_specs=[pl.BlockSpec(memory_space=pltpu.SMEM), vmem, vmem]
        + [pl.BlockSpec(memory_space=pl.ANY)] * len(pieces),
        out_specs=[vmem, vmem],
        out_shape=[
            jax.ShapeDtypeStruct((count, LANES), HALF),
            jax.ShapeDtypeStruct((rows, LANES), FULL),
        ],
        scratch_shapes=[
            pltpu.VMEM((rows, LANES), FULL),
            pltpu.VMEM((count, LANES), FULL),
            pltpu.VMEM((count, LANES), FULL),
            pltpu.SemaphoreType.DMA((len(pieces),)),
        ],
        compiler_params=pltpu.CompilerParams(vmem_limit_bytes=VMEM_BYTES),
        cost_estimate=pl.CostEstimate(flops=8 << 30, bytes_accessed=0, transcendentals=0),
        name="quantize",
    )(places, block.reshape(count, 1), latent.reshape(count, LANES), *pieces)
    return quant.reshape(z.groups, z.rows, LANES), book


def decoder_forward_feed(z, lengths, where, quant, cotangent, weights):
    return run_groups(
        decoder_feed_kernel,
        "decoder_forward_feed_backward",
        z.groups,
        [lengths, where],
        [quant, cotangent],
        picked(weights, FEED + ENDS),
        [z.wide_low, z.qkv, z.lse, z.mixed, z.wide, z.feed_blocks, z.feed_blocks, z.feed_vector],
        [z.bias_scratch, z.lse_scratch, z.hidden_scratch, z.hidden_scratch, z.low_scratch, z.low_scratch]
        + [z.wide_scratch] * 4
        + z.feed_sums,
        36 << 30,
        40,
        where,
        1,
    )


def decoder_input(z, where, quant, grad_middle, grad_qkv, sums, weights, book, book_rows, latent, owners, per_owner):
    return run_groups(
        functools.partial(decoder_input_kernel, owners=owners, per_owner=per_owner, latent=latent),
        "decoder_input_backward",
        z.groups,
        [where],
        [quant, grad_middle, grad_qkv],
        picked(weights, FEED[:3] + ENDS[2:]) + [book] + sums,
        [z.latent_low]
        + z.blocks(z.attention_rows + z.small_rows + book_rows)
        + [z.two_vectors, z.bridge],
        [z.qkv_sum, z.low_scratch, z.wide_scratch, z.wide_scratch, z.low_scratch, z.small_sum],
        8 << 30,
        24,
        where,
        1,
    )


def encoder_feed(z, where, grad_quant, middle, result, slope, active, weights):
    return run_groups(
        encoder_feed_kernel,
        "encoder_feed_backward",
        z.groups,
        [where],
        [grad_quant, middle, result, slope, active],
        picked(weights, FEED[4:7] + FEED[8:] + ENDS),
        [z.wide, z.feed_blocks, z.feed_blocks, z.feed_vector, z.bridge],
        [z.low_scratch, z.low_scratch, z.wide_scratch, z.wide_scratch] + z.feed_sums,
        20 << 30,
        30,
        where,
        0,
    )


def attention_gradient(z, name, side, lengths, where, grad_middle, saved, weights):
    return run_groups(
        attention_backward_kernel,
        name,
        z.groups,
        [lengths],
        [grad_middle] + list(saved),
        picked(weights, ["out_w"]),
        [z.qkv, Whole((z.width, z.width), FULL)],
        [z.bias_scratch, z.mixed_scratch],
        20 << 30,
        18,
        where,
        side,
    )


def encoder_input(z, where, patch, grad_middle, grad_qkv, sums, weights, latent):
    return run_groups(
        functools.partial(encoder_input_kernel, latent=latent),
        "encoder_input_backward",
        z.groups,
        [where],
        [patch, grad_middle, grad_qkv],
        picked(weights, FEED[:3]) + sums,
        [z.wide_low] + z.blocks(z.attention_rows + z.small_rows) + [z.two_vectors],
        [z.qkv_sum, z.low_scratch, z.wide_scratch, z.small_sum],
        8 << 30,
        18,
        where,
        0,
    )


def on_device(
    section_in,
    ln1_gain,
    ln1_shift,
    qkv_weight,
    out_weight,
    ln2_gain,
    ln2_shift,
    up_weight,
    up_shift,
    down_weight,
    final_gain,
    final_shift,
    bridge_weight,
    codebook,
    codes,
    doc_lengths,
):
    section = lax.axis_index("section")
    encoder_side = section == 0
    micro = doc_lengths.shape[0]
    groups = micro // 2
    rows = section_in.shape[1] // micro
    width = section_in.shape[2]
    hidden_width = up_weight.shape[2]
    latent_width = bridge_weight.shape[1]
    per_device = codebook.shape[1]

    count = lax.axis_size("dp")
    dp = lax.axis_index("dp")
    where = jnp.stack([section, dp & (CHUNKS - 1), dp >> (CHUNKS.bit_length() - 1)]).astype(jnp.int32)

    inverse = lax.rsqrt(jnp.sum(codebook * codebook, axis=0, keepdims=True) + EPS)
    unit_codes = codebook * inverse
    quarter = per_device // 4
    packed = (
        unit_codes.reshape(latent_width, 4, quarter).transpose(2, 1, 0).reshape(quarter, 4 * latent_width)
    )
    deep_table = [packed] + [from_dp(packed, mask) for mask in DEPTH]

    vectors = jnp.concatenate(
        [ln1_gain, ln1_shift, ln2_gain, ln2_shift, final_gain, final_shift]
        + [up_shift.reshape(-1, width), bridge_weight[0].astype(FULL)],
        axis=0,
    )
    qkv_w, out_w, up_w, down_w = qkv_weight[0], out_weight[0], up_weight[0], down_weight[0]
    halves = section_in[0].reshape(2, groups, rows, width)
    other_halves = from_section(section_in[0]).reshape(halves.shape)
    other_vectors, other_qkv, other_out = from_section(vectors), from_section(qkv_w), from_section(out_w)
    patch = jnp.where(encoder_side, halves[0], other_halves[1])
    lengths = lax.dynamic_slice_in_dim(doc_lengths, section * groups, groups, 0)
    own_codes = lax.dynamic_slice_in_dim(codes, section * groups * rows, groups * rows, 0)
    owner, within = own_codes // per_device, own_codes % per_device
    apart = (owner % count) ^ dp
    place = ((owner // count) ^ section) * count + (apart & -CHUNKS) + 4 * (apart & 3) + ((apart >> 2) & 3)
    places = place * quarter + within % quarter
    code_block = within // quarter
    deep_table, patch, other_halves, other_vectors, other_qkv, other_out = lax.optimization_barrier(
        (deep_table, patch, other_halves, other_vectors, other_qkv, other_out)
    )
    hidden_rows = hidden_width // width

    def vectors_of(vector):
        return dict(
            ln1_gain=vector[0:1],
            ln1_shift=vector[1:2],
            qkv_w=(qkv_w, other_qkv),
            out_w=(out_w, other_out),
            ln2_gain=vector[2:3],
            ln2_shift=vector[3:4],
            up_shift=vector[6 : 6 + hidden_rows].reshape(1, hidden_width),
            final_gain=vector[4:5],
            final_shift=vector[5:6],
            bridge=jnp.pad(low(vector[6 + hidden_rows :]), ((0, LANES - latent_width), (0, 0))),
        )

    encoder = vectors_of(jnp.where(encoder_side, vectors, other_vectors))
    decoder = vectors_of(jnp.where(encoder_side, other_vectors, vectors))
    z = Sizes(width, hidden_width, groups, rows)
    deep_table = jnp.concatenate(deep_table, axis=0)
    table = [deep_table] + [from_dp(deep_table, mask) for mask in PLANE]
    other_up, other_down = from_section(up_w), from_section(down_w)
    encoded = encoder_mix(z, lengths, where, patch, encoder)
    table, other_up, other_down, encoded = lax.optimization_barrier((table, other_up, other_down, encoded))
    qkv_e, lse_e, mixed_e, middle_e = encoded
    encoder.update(up_w=(up_w, other_up), down_w=(down_w, other_down))
    decoder.update(up_w=(up_w, other_up), down_w=(down_w, other_down))
    bit = CHUNKS
    while bit < count:
        table = table + [from_dp(piece, bit) for piece in table]
        bit = 2 * bit
    table = table + [from_section(piece) for piece in table]
    encoded = encoder_latent(z, where, middle_e, encoder)
    table, encoded = lax.optimization_barrier((table, encoded))
    cotangent = jnp.where(encoder_side, other_halves[0], halves[1])
    slope_e, active_e, result_e, latent = encoded
    quant, book = quantize(z, places, code_block, latent, table)
    feed_rows, attention_rows = z.feed_rows, z.attention_rows
    book_rows = 4 * latent_width * (lax.axis_size("dp") // CHUNKS) * quarter // width
    final, qkv_d, lse_d, mixed_d, middle_d, keep_1, send_1, vectors_1 = decoder_forward_feed(
        z, lengths, where, quant, cotangent, decoder
    )
    got_1 = from_section(send_1)
    decoder_mixed = attention_gradient(
        z, "decoder_attention_backward", 1, lengths, where, middle_d, (qkv_d, lse_d, mixed_d), decoder
    )
    got_1, decoder_mixed = lax.optimization_barrier((got_1, decoder_mixed))
    grad_qkv_d, out_sum_d = decoder_mixed
    plane_1 = add_cores("decoder_feed", [(keep_1, got_1)])
    moved_1 = exchange(plane_1, PLANE)
    grad_quant, keep_2, send_2, vectors_2, bridge_d = decoder_input(
        z,
        where,
        quant,
        middle_d,
        after(grad_qkv_d, plane_1[0]),
        [out_sum_d, vectors_1],
        decoder,
        book,
        book_rows,
        latent_width,
        lax.axis_size("dp"),
        quarter,
    )
    got_2 = from_section(send_2)
    middle_grad, keep_3, send_3, vectors_3, bridge_e = encoder_feed(
        z, where, grad_quant, middle_e, result_e, slope_e, active_e, encoder
    )
    moved_1, got_2, middle_grad, keep_3, send_3, vectors_3, bridge_e = lax.optimization_barrier(
        (moved_1, got_2, middle_grad, keep_3, send_3, vectors_3, bridge_e)
    )
    got_3 = from_section(send_3)
    depth_1 = add_plane("decoder_feed", moved_1)
    joined_2 = join_cores("decoder_attention", [(keep_2, got_2)])
    depth_2 = scatter_group(joined_2.reshape((4, CHUNKS // 4) + joined_2.shape[1:]), PLANE)
    plane_3 = add_cores("encoder_feed", [(keep_3, got_3)])

    middle_grad = after(middle_grad, plane_3[0], joined_2, depth_1[0])
    moved_3 = exchange(plane_3, PLANE)
    deep_1 = exchange(depth_1, DEPTH)
    grad_qkv, out_sum = attention_gradient(
        z, "encoder_attention_backward", 0, lengths, where, middle_grad, (qkv_e, lse_e, mixed_e), encoder
    )
    grad_patch, keep_4, send_4, _ = encoder_input(
        z, where, patch, middle_grad, grad_qkv, [out_sum, vectors_3, bridge_e], encoder, latent_width
    )
    moved_3, deep_1, depth_2, grad_patch, keep_4, send_4 = lax.optimization_barrier(
        (moved_3, deep_1, depth_2, grad_patch, keep_4, send_4)
    )

    got_4 = from_section(send_4)
    chunk_1 = add_far(add_depth("decoder_feed", deep_1))
    near_1 = [chunk_1] + [from_dp(chunk_1, mask) for mask in DEPTH]
    depth_3 = add_plane("encoder_feed", moved_3, depth_2)
    deep_3 = exchange(depth_3, DEPTH)
    plane_4 = add_cores("encoder_attention", [(keep_4, got_4)])
    moved_4 = exchange(plane_4, PLANE)
    sent = jnp.where(encoder_side, final, grad_patch)
    kept = jnp.where(encoder_side, grad_patch, final)
    got = from_section(sent)
    near_1, deep_3, moved_4, got = lax.optimization_barrier((near_1, deep_3, moved_4, got))
    half_1 = gather_group(jnp.stack(near_1), PLANE)
    deep_4 = exchange(add_plane("encoder_attention", moved_4), DEPTH)
    chunk_3 = add_far(add_depth("encoder_feed", deep_3))
    used_2 = chunk_3[feed_rows : feed_rows + attention_rows + z.small_rows]
    near_2 = [used_2] + [from_dp(used_2, mask) for mask in DEPTH]
    deep_4, near_2 = lax.optimization_barrier((deep_4, near_2))
    chunk_4 = add_far(add_depth("encoder_attention", deep_4))
    chunk_e = jnp.concatenate([chunk_3[:feed_rows], chunk_4], axis=0)
    deep_e = gather_depth_for(chunk_e, 0)
    near_2 = jnp.stack(near_2)
    half_2 = [near_2] + [from_dp(near_2, mask) for mask in PLANE]
    deep_e, half_1, half_2 = lax.optimization_barrier((deep_e, half_1, half_2))
    book_sum = chunk_3[feed_rows + attention_rows + z.small_rows :].astype(FULL)
    book_sum = book_sum.reshape(book_rows, 4, LANES).transpose(1, 0, 2).reshape(-1, quarter, LANES)
    book_own = lax.dynamic_index_in_dim(book_sum, lax.axis_index("dp") // CHUNKS, 0, keepdims=False)
    book_grad = (
        book_own.reshape(quarter, 4, latent_width).transpose(2, 1, 0).reshape(latent_width, per_device)
    )
    book_grad = inverse * (
        book_grad - unit_codes * jnp.sum(unit_codes * book_grad, axis=0, keepdims=True)
    )

    section_out = jnp.where(
        encoder_side, jnp.concatenate([kept, got], axis=0), jnp.concatenate([got, kept], axis=0)
    ).reshape(1, micro * rows, width)
    gathered = gather_plane_for(deep_e, 0)
    half_2 = jnp.stack(half_2)
    halves_d = [half_1, half_2]
    halves_d = halves_d + [lax.ppermute(half, "section", [(0, 1)]) for half in halves_d]

    feed_segments = [(0, z.down_rows, 0, 0)] + [
        (z.down_rows + part * z.thin_rows, z.thin_rows, 1, part * width) for part in range(z.up_parts)
    ]
    attention_segments = [(0, z.thin_rows, 3, 0)] + [
        ((part + 1) * z.thin_rows, z.thin_rows, 2, part * width) for part in range(3)
    ]
    segments = feed_segments + [
        (feed_rows + offset, size, target, column) for offset, size, target, column in attention_segments
    ]
    gathered, section_out, book_grad = lax.optimization_barrier((gathered, section_out, book_grad))
    given = gathered + list(halves_d)
    vmem = pl.BlockSpec(memory_space=pltpu.VMEM)
    down_total, up_total, qkv_total, out_total, small = pl.pallas_call(
        functools.partial(unpack_kernel, feed_segments, attention_segments, segments),
        in_specs=[pl.BlockSpec(memory_space=pltpu.SMEM)] + [vmem] * len(given),
        out_specs=[vmem] * 5,
        out_shape=[
            jax.ShapeDtypeStruct(shape, FULL)
            for shape in (
                (hidden_width, width),
                (width, hidden_width),
                (width, 3 * width),
                (width, width),
                (2 * CHUNKS, z.small_rows // 2, width),
            )
        ],
        compiler_params=pltpu.CompilerParams(vmem_limit_bytes=30 << 20),
        name="unpack",
    )(where, *given)

    small_count = 2 + 4 + z.up_parts + latent_width
    small = small[:, : -(-small_count // (2 * CHUNKS))].reshape(-1, width)

    first_vector = 2
    hidden_vector = first_vector + 4
    return (
        section_out,
        small[0:1],
        small[1:2],
        qkv_total[None],
        out_total[None],
        small[2:3],
        small[3:4],
        up_total[None],
        small[hidden_vector : hidden_vector + z.up_parts].reshape(1, hidden_width),
        down_total[None],
        small[4:5],
        small[5:6],
        small[hidden_vector + z.up_parts : hidden_vector + z.up_parts + latent_width][None],
        book_grad,
    )


def solution(mesh):
    placed = (
        P("section", "dp", None),
        P("section", None),
        P("section", None),
        P("section", None, None),
        P("section", None, None),
        P("section", None),
        P("section", None),
        P("section", None, None),
        P("section", None),
        P("section", None, None),
        P("section", None),
        P("section", None),
        P("section", None, None),
        P(None, ("section", "dp")),
        P("dp"),
        P("dp", None),
    )
    return jax.shard_map(
        on_device,
        mesh=mesh,
        in_specs=placed,
        out_specs=(
            P("section", "dp", None),
            P("section", None),
            P("section", None),
            P("section", None, None),
            P("section", None, None),
            P("section", None),
            P("section", None),
            P("section", None, None),
            P("section", None),
            P("section", None, None),
            P("section", None),
            P("section", None),
            P("section", None, None),
            P(None, ("section", "dp")),
        ),
        check_vma=False,
    )
```

```python
import functools

import jax
import jax.numpy as jnp
from jax import lax
from jax.experimental import pallas as pl
from jax.experimental.pallas import tpu as pltpu
from jax.sharding import PartitionSpec as P

HEADS = 8
PAIRS = HEADS // 2
LANES = 128
EPS = 1e-06
GELU_FACTOR = 0.7978845608028654
GELU_CUBIC = 0.044715
BLOCKED = -1000000000.0
CHUNKS = 16
FULL = jnp.float32
HALF = jnp.bfloat16
VMEM_BYTES = 12 * 1024 * 1024


def low(value):
    return value.astype(HALF)


def mm(left, right):
    return lax.dot_general(left, right, (((1,), (0,)), ((), ())), preferred_element_type=FULL)


def mm_nt(left, right):
    return lax.dot_general(left, right, (((1,), (1,)), ((), ())), preferred_element_type=FULL)


def mm_tn(left, right):
    return lax.dot_general(left, right, (((0,), (0,)), ((), ())), preferred_element_type=FULL)


def norm_forward(inputs, gain, shift):
    centred = inputs - jnp.mean(inputs, axis=-1, keepdims=True)
    scaling = lax.rsqrt(jnp.mean(centred * centred, axis=-1, keepdims=True) + EPS)
    normal = centred * scaling
    return normal * gain + shift, normal, scaling


def row_chunks(rows, size=64):
    return [slice(start, start + size) for start in range(0, rows, size)]


def norm_rows(source, target, gain, shift):
    for part in row_chunks(source.shape[0]):
        target[part, :] = low(norm_forward(source[part, :].astype(FULL), gain[...], shift[...])[0])


def write_bias(lengths_ref, group, bias_ref):
    rows = bias_ref.shape[0]
    down = lax.broadcasted_iota(jnp.int32, (rows, rows), 0)
    across = lax.broadcasted_iota(jnp.int32, (rows, rows), 1)
    row_label = jnp.zeros((rows, rows), jnp.int32)
    column_label = jnp.zeros((rows, rows), jnp.int32)
    bound = jnp.int32(0)
    for doc in range(lengths_ref.shape[1]):
        bound = bound + lengths_ref[group, doc]
        row_label = row_label + (down >= bound).astype(jnp.int32)
        column_label = column_label + (across >= bound).astype(jnp.int32)
    bias_ref[...] = jnp.where(row_label == column_label, 0.0, BLOCKED)


def half_mask(rows, side):
    lane = lax.broadcasted_iota(jnp.int32, (rows, LANES), 1)
    return lane < LANES // 2 if side == 0 else lane >= LANES // 2


def attention_forward(qkv_ref, bias_ref, mixed_ref, lse_ref, lse_scratch):
    rows = qkv_ref.shape[1]
    scale = (LANES // 2) ** (-0.5)
    lane = lax.broadcasted_iota(jnp.int32, (rows, LANES), 1)
    lse_scratch[...] = jnp.zeros_like(lse_scratch)

    def pair_step(pair, carry):
        queries = qkv_ref[pair] * jnp.asarray(scale, HALF)
        keys = qkv_ref[PAIRS + pair]
        values = qkv_ref[2 * PAIRS + pair]
        mixed = jnp.zeros((rows, LANES), FULL)
        for side in range(2):
            inside = half_mask(rows, side)
            zero = jnp.zeros((), HALF)
            scores = mm_nt(jnp.where(inside, queries, zero), keys) + bias_ref[...]
            peak = jnp.max(scores, axis=-1, keepdims=True)
            weight = jnp.exp(scores - peak)
            total = jnp.sum(weight, axis=-1, keepdims=True)
            part = mm(low(weight), jnp.where(inside, values, zero))
            mixed = mixed + part * (1.0 / total)
            log_total = peak + jnp.log(total)
            lse_scratch[...] = jnp.where(lane == 2 * pair + side, log_total, lse_scratch[...])
        mixed_ref[pair] = low(mixed)
        return carry

    lax.fori_loop(0, PAIRS, pair_step, 0, unroll=4)
    lse_ref[...] = jnp.transpose(lse_scratch[...])[:HEADS]


def heads_joined(mixed_ref):
    return jnp.concatenate([mixed_ref[pair] for pair in range(PAIRS)], axis=1)


def mix_forward(
    source, weights, bias_ref, qkv_ref, mixed_ref, lse_ref, lse_scratch, normed_ref, middle_ref
):
    ln1_gain, ln1_shift, qkv_w, out_w = weights
    width = source.shape[1]
    norm_rows(source, normed_ref, ln1_gain, ln1_shift)
    for part in range(3):
        projected = low(mm(normed_ref[...], qkv_w[:, part * width : (part + 1) * width]))
        for pair in range(PAIRS):
            qkv_ref[part * PAIRS + pair] = projected[:, pair * LANES : (pair + 1) * LANES]
    attention_forward(qkv_ref, bias_ref, mixed_ref, lse_ref, lse_scratch)
    middle_ref[...] = source[...].astype(FULL) + mm(heads_joined(mixed_ref), out_w[...])


def feed_forward(middle_ref, weights, normed_ref, slope_ref, active_ref, total_ref):
    ln2_gain, ln2_shift, up_w, up_shift, down_w = weights
    hidden_width = up_w.shape[1]
    norm_rows(middle_ref, normed_ref, ln2_gain, ln2_shift)
    tile = middle_ref.shape[1]
    for step in range(hidden_width // tile):
        place = slice(step * tile, (step + 1) * tile)
        hidden = mm(normed_ref[...], up_w[:, place]) + up_shift[:, place]
        square = hidden * hidden
        tangent = jnp.tanh(hidden * ((GELU_FACTOR * GELU_CUBIC) * square + GELU_FACTOR))
        gate = 0.5 * tangent + 0.5
        active = low(hidden * gate)
        bend = hidden * ((1.5 * GELU_FACTOR * GELU_CUBIC) * square + 0.5 * GELU_FACTOR)
        active_ref[:, place] = active
        slope_ref[:, place] = low(gate + bend * (1.0 - tangent * tangent))
        before = middle_ref[...] if step == 0 else total_ref[...]
        total_ref[...] = before + mm(active, down_w[place, :])


def feed_backward(
    upstream_ref,
    middle_ref,
    weights,
    slope_ref,
    active_ref,
    normed_ref,
    branch_ref,
    total_ref,
    down_out,
    up_out,
    up_shift_out,
    grad_middle_ref,
    vector_out,
):
    ln2_gain, ln2_shift, up_w, down_w = weights
    width = upstream_ref.shape[1]
    hidden_width = up_w.shape[1]
    norm_rows(middle_ref, normed_ref, ln2_gain, ln2_shift)
    tile = width

    def hidden_step(step, carry):
        place = pl.ds(step * tile, tile)
        branch = branch_ref[...]
        down_out[place, :] = down_out[place, :] + mm_tn(active_ref[:, place], branch)
        grad_hidden = mm_nt(branch, down_w[place, :]) * slope_ref[:, place].astype(FULL)
        up_shift_out[:, place] = up_shift_out[:, place] + jnp.sum(grad_hidden, axis=0, keepdims=True)
        grad_low = low(grad_hidden)
        up_out[:, place] = up_out[:, place] + mm_tn(normed_ref[...], grad_low)
        share = mm_nt(grad_low, up_w[:, place])
        total_ref[...] = share if step == 0 else total_ref[...] + share
        return carry

    for step in range(hidden_width // tile):
        hidden_step(step, 0)
    norm_backward_rows(
        total_ref, middle_ref, ln2_gain, ln2_shift, vector_out, 0, upstream_ref, grad_middle_ref
    )


def norm_backward_rows(grad_ref, source, gain, shift, vector_out, row, added_ref, *targets):
    width = source.shape[1]
    grad_gain = jnp.zeros((8, width), FULL)
    grad_shift = jnp.zeros((8, width), FULL)
    for part in row_chunks(source.shape[0]):
        _, normal, scaling = norm_forward(source[part, :].astype(FULL), gain[...], shift[...])
        upstream = grad_ref[part, :].astype(FULL)
        scaled = upstream * gain[...]
        inner = scaled - jnp.mean(scaled, axis=-1, keepdims=True)
        inner = inner - normal * jnp.mean(scaled * normal, axis=-1, keepdims=True)
        grad = scaling * inner
        if added_ref is not None:
            grad = grad + added_ref[part, :]
        for target in targets:
            target[part, :] = grad.astype(target.dtype)
        folded = (upstream.shape[0] // 8, 8, width)
        grad_gain = grad_gain + jnp.sum((upstream * normal).reshape(folded), axis=0)
        grad_shift = grad_shift + jnp.sum(upstream.reshape(folded), axis=0)
    add_row(vector_out, row, jnp.sum(grad_gain, axis=0, keepdims=True))
    add_row(vector_out, row + 1, jnp.sum(grad_shift, axis=0, keepdims=True))


def attention_backward(qkv_ref, grad_mixed_ref, bias_ref, lse_ref, grad_qkv_ref):
    rows = qkv_ref.shape[1]
    scale = (LANES // 2) ** (-0.5)

    def pair_step(pair, carry):
        queries = qkv_ref[pair] * jnp.asarray(scale, HALF)
        keys = qkv_ref[PAIRS + pair]
        values = qkv_ref[2 * PAIRS + pair]
        grads = grad_mixed_ref[pair]
        grad_queries = jnp.zeros((rows, LANES), FULL)
        grad_keys = jnp.zeros((rows, LANES), FULL)
        grad_values = jnp.zeros((rows, LANES), FULL)
        for side in range(2):
            inside = half_mask(rows, side)
            zero = jnp.zeros((), HALF)
            side_queries = jnp.where(inside, queries, zero)
            side_grads = jnp.where(inside, grads, zero)
            scores = mm_nt(keys, side_queries) + bias_ref[...]
            attention = jnp.exp(scores - lse_ref[pl.ds(2 * pair + side, 1), :])
            grad_values = grad_values + mm(low(attention), side_grads)
            grad_attention = mm_nt(values, side_grads)
            delta = jnp.sum(attention * grad_attention, axis=0, keepdims=True)
            grad_scores = low(attention * (grad_attention - delta))
            grad_keys = grad_keys + mm(grad_scores, side_queries)
            grad_queries = grad_queries + mm_tn(grad_scores, jnp.where(inside, keys, zero))
        grad_qkv_ref[pair] = low(grad_queries * scale)
        grad_qkv_ref[PAIRS + pair] = low(grad_keys)
        grad_qkv_ref[2 * PAIRS + pair] = low(grad_values)
        return carry

    lax.fori_loop(0, PAIRS, pair_step, 0, unroll=4)


def attention_gradients(
    grad_middle, out_w, bias_ref, qkv_ref, mixed_ref, lse_ref, grad_mixed_ref, grad_qkv_ref, out_out
):
    grad_low = low(grad_middle)
    out_out[...] = out_out[...] + mm_tn(heads_joined(mixed_ref), grad_low)
    grad_mixed = low(mm_nt(grad_low, out_w[...]))
    for pair in range(PAIRS):
        grad_mixed_ref[pair] = grad_mixed[:, pair * LANES : (pair + 1) * LANES]
    attention_backward(qkv_ref, grad_mixed_ref, bias_ref, lse_ref, grad_qkv_ref)


def projection_gradients(
    source, grad_middle_ref, ln1_gain, ln1_shift, qkv_w, grad_qkv_ref, qkv_out, normed_ref, total_ref, vector_out, target
):
    width = source.shape[1]
    norm_rows(source, normed_ref, ln1_gain, ln1_shift)
    for part in range(3):
        grad_part = jnp.concatenate(
            [grad_qkv_ref[part * PAIRS + pair] for pair in range(PAIRS)], axis=1
        )
        place = slice(part * width, (part + 1) * width)
        qkv_out[:, place] = qkv_out[:, place] + mm_tn(normed_ref[...], grad_part)
        share = mm_nt(grad_part, qkv_w[:, place])
        total_ref[...] = share if part == 0 else total_ref[...] + share
    norm_backward_rows(total_ref, source, ln1_gain, ln1_shift, vector_out, 0, grad_middle_ref, target)


def unit_rows(rows):
    inverse = lax.rsqrt(jnp.sum(rows * rows, axis=-1, keepdims=True) + EPS)
    return rows * inverse, inverse


def start_totals(*refs):
    @pl.when(pl.program_id(0) == 0)
    def _():
        for ref in refs:
            ref[...] = jnp.zeros_like(ref)


def encoder_mix_kernel(
    lengths,
    patch,
    ln1_gain,
    ln1_shift,
    qkv_w,
    out_w,
    qkv_ref,
    lse_ref,
    mixed_ref,
    middle_ref,
    bias_ref,
    lse_scratch,
    normed_ref,
):
    write_bias(lengths, pl.program_id(0), bias_ref)
    mix_forward(
        patch,
        (ln1_gain, ln1_shift, qkv_w, out_w),
        bias_ref,
        qkv_ref,
        mixed_ref,
        lse_ref,
        lse_scratch,
        normed_ref,
        middle_ref,
    )


def encoder_latent_kernel(
    middle,
    ln2_gain,
    ln2_shift,
    up_w,
    up_shift,
    down_w,
    final_gain,
    final_shift,
    bridge,
    slope_ref,
    active_ref,
    result_ref,
    latent_ref,
    normed_ref,
):
    weights = (ln2_gain, ln2_shift, up_w, up_shift, down_w)
    feed_forward(middle, weights, normed_ref, slope_ref, active_ref, result_ref)
    norm_rows(result_ref, normed_ref, final_gain, final_shift)
    latent_ref[...] = unit_rows(mm_nt(normed_ref[...], bridge[...]))[0]


def quant_kernel(places, block_column, latent, *refs):
    pieces, (quant_ref, book_ref, table, gathered, spread, semaphore) = refs[:-6], refs[-6:]
    count = gathered.shape[0]
    size = pieces[0].shape[0]
    copies = [
        pltpu.make_async_copy(piece, table.at[pl.ds(number * size, size)], semaphore.at[number])
        for number, piece in enumerate(pieces)
    ]
    for copy in copies:
        copy.start()
    for copy in copies:
        copy.wait()

    def gather(index, carry):
        gathered[pl.ds(index, 1), :] = table[pl.ds(places[index], 1), :]
        return carry

    lax.fori_loop(0, count, gather, 0, unroll=16)
    block = block_column[...]
    lane = lax.broadcasted_iota(jnp.int32, (count, LANES), 1)
    width = LANES // 4
    rows = gathered[...]
    code = jnp.where(block == 0, rows, 0.0)
    for place in range(1, 4):
        code = code + jnp.where(block == place, pltpu.roll(rows, LANES - width * place, 1), 0.0)
    code = jnp.where(lane < width, code, 0.0)
    held = latent[...]
    quant_ref[...] = low(held + (code - held))
    grad = 2.0 * (code - held)
    placed = jnp.where(block == 0, grad, 0.0)
    for place in range(1, 4):
        placed = placed + jnp.where(block == place, pltpu.roll(grad, width * place, 1), 0.0)
    spread[...] = placed
    book_ref[...] = jnp.zeros_like(book_ref)

    def scatter(index, carry):
        place = pl.ds(places[index], 1)
        book_ref[place, :] = book_ref[place, :] + spread[pl.ds(index, 1), :]
        return carry

    lax.fori_loop(0, count, scatter, 0, unroll=8)


def add_row(ref, row, value):
    ref[row : row + 1, :] = ref[row : row + 1, :] + value


def feed_vectors(vector_out, up_shift_acc):
    width = vector_out.shape[1]
    for part in range(up_shift_acc.shape[1] // width):
        vector_out[4 + part : 5 + part, :] = up_shift_acc[:, part * width : (part + 1) * width]


def last_group():
    return pl.program_id(0) == pl.num_programs(0) - 1


def decoder_mix_kernel(
    lengths,
    quant,
    ln1_gain,
    ln1_shift,
    qkv_w,
    out_w,
    bridge,
    qkv_ref,
    lse_ref,
    mixed_ref,
    middle_ref,
    bias_ref,
    lse_scratch,
    normed_ref,
    source_ref,
):
    write_bias(lengths, pl.program_id(0), bias_ref)
    source_ref[...] = mm(quant[...], bridge[...])
    mix_forward(
        source_ref,
        (ln1_gain, ln1_shift, qkv_w, out_w),
        bias_ref,
        qkv_ref,
        mixed_ref,
        lse_ref,
        lse_scratch,
        normed_ref,
        middle_ref,
    )


def decoder_feed_kernel(
    where,
    middle_ref,
    cotangent,
    ln2_gain,
    ln2_shift,
    up_w,
    up_shift,
    down_w,
    final_gain,
    final_shift,
    final_ref,
    grad_middle_ref,
    keep_ref,
    send_ref,
    vector_out,
    slope_ref,
    active_ref,
    normed_ref,
    branch_ref,
    result_ref,
    upstream_ref,
    down_acc,
    up_acc,
    up_shift_acc,
):
    start_totals(down_acc, up_acc, up_shift_acc, vector_out)
    weights = (ln2_gain, ln2_shift, up_w, up_shift, down_w)
    feed_forward(middle_ref, weights, normed_ref, slope_ref, active_ref, result_ref)
    norm_rows(result_ref, final_ref, final_gain, final_shift)
    norm_backward_rows(
        cotangent, result_ref, final_gain, final_shift, vector_out, 2, None, upstream_ref, branch_ref
    )
    feed_backward(
        upstream_ref,
        middle_ref,
        (ln2_gain, ln2_shift, up_w, down_w),
        slope_ref,
        active_ref,
        normed_ref,
        branch_ref,
        result_ref,
        down_acc,
        up_acc,
        up_shift_acc,
        grad_middle_ref,
        vector_out,
    )

    @pl.when(last_group())
    def _():
        feed_vectors(vector_out, up_shift_acc)
        pieces = [rows_of(down_acc)] + column_parts(up_acc, middle_ref.shape[1])
        store_blocks(where, keep_ref, send_ref, pieces, order="deep")


def decoder_input_kernel(
    where,
    quant,
    grad_middle,
    grad_qkv_ref,
    ln1_gain,
    ln1_shift,
    qkv_w,
    bridge,
    book,
    out_sum,
    feed_vector,
    grad_quant_ref,
    keep_ref,
    send_ref,
    vector_out,
    bridge_out,
    qkv_acc,
    normed_ref,
    source_ref,
    total_ref,
    grad_lift_ref,
    small_ref,
    *,
    owners,
    per_owner,
    latent,
):
    start_totals(qkv_acc, vector_out, bridge_out)
    source_ref[...] = mm(quant[...], bridge[...])
    projection_gradients(
        source_ref,
        grad_middle,
        ln1_gain,
        ln1_shift,
        qkv_w,
        grad_qkv_ref,
        qkv_acc,
        normed_ref,
        total_ref,
        vector_out,
        grad_lift_ref,
    )
    bridge_out[...] = bridge_out[...] + mm_tn(quant[...], grad_lift_ref[...])
    grad_quant_ref[...] = low(mm_nt(grad_lift_ref[...], bridge[...]))

    @pl.when(last_group())
    def _():
        pieces = [rows_of(out_sum)] + column_parts(qkv_acc, source_ref.shape[1])
        spread_rows(small_ref, (vector_out, 2), (feed_vector, feed_vector.shape[0]), (bridge_out, latent))
        pieces = pieces + [lambda block: small_ref[block], codebook_rows(where, book, per_owner, owners)]
        store_blocks(where, keep_ref, send_ref, pieces, order="flat")


def encoder_feed_kernel(
    where,
    grad_quant,
    middle,
    result,
    slope_ref,
    active_ref,
    ln2_gain,
    ln2_shift,
    up_w,
    down_w,
    final_gain,
    final_shift,
    bridge,
    grad_middle_ref,
    keep_ref,
    send_ref,
    vector_out,
    bridge_out,
    normed_ref,
    branch_ref,
    grad_ref,
    upstream_ref,
    down_acc,
    up_acc,
    up_shift_acc,
):
    start_totals(down_acc, up_acc, up_shift_acc, vector_out, bridge_out)
    norm_rows(result, normed_ref, final_gain, final_shift)
    feature = normed_ref[...]
    latent, inverse = unit_rows(mm_nt(feature, bridge[...]))
    grad_latent = grad_quant[...].astype(FULL)
    grad_projection = low(
        inverse * (grad_latent - latent * jnp.sum(latent * grad_latent, axis=1, keepdims=True))
    )
    bridge_out[...] = bridge_out[...] + mm_tn(grad_projection, feature)
    grad_ref[...] = mm(grad_projection, bridge[...])
    norm_backward_rows(
        grad_ref, result, final_gain, final_shift, vector_out, 2, None, upstream_ref, branch_ref
    )
    feed_backward(
        upstream_ref,
        middle,
        (ln2_gain, ln2_shift, up_w, down_w),
        slope_ref,
        active_ref,
        normed_ref,
        branch_ref,
        grad_ref,
        down_acc,
        up_acc,
        up_shift_acc,
        grad_middle_ref,
        vector_out,
    )

    @pl.when(last_group())
    def _():
        feed_vectors(vector_out, up_shift_acc)
        pieces = [rows_of(down_acc)] + column_parts(up_acc, middle.shape[1])
        store_blocks(where, keep_ref, send_ref, pieces)


def attention_backward_kernel(
    lengths,
    grad_middle,
    qkv_ref,
    lse_ref,
    mixed_ref,
    out_w,
    grad_qkv_ref,
    out_acc,
    bias_ref,
    grad_mixed_ref,
):
    start_totals(out_acc)
    write_bias(lengths, pl.program_id(0), bias_ref)
    attention_gradients(
        grad_middle[...], out_w, bias_ref, qkv_ref, mixed_ref, lse_ref, grad_mixed_ref, grad_qkv_ref, out_acc
    )


def encoder_input_kernel(
    where,
    patch,
    grad_middle,
    grad_qkv_ref,
    ln1_gain,
    ln1_shift,
    qkv_w,
    out_sum,
    feed_vector,
    bridge_sum,
    grad_patch_ref,
    keep_ref,
    send_ref,
    vector_out,
    qkv_acc,
    normed_ref,
    total_ref,
    small_ref,
    *,
    latent,
):
    start_totals(qkv_acc, vector_out)
    projection_gradients(
        patch,
        grad_middle,
        ln1_gain,
        ln1_shift,
        qkv_w,
        grad_qkv_ref,
        qkv_acc,
        normed_ref,
        total_ref,
        vector_out,
        grad_patch_ref,
    )

    @pl.when(last_group())
    def _():
        spread_rows(small_ref, (vector_out, 2), (feed_vector, feed_vector.shape[0]), (bridge_sum, latent))
        pieces = [rows_of(out_sum)] + column_parts(qkv_acc, patch.shape[1])
        store_blocks(where, keep_ref, send_ref, pieces + [lambda block: small_ref[block]])


def store_blocks(where, keep_ref, send_ref, pieces, order="relative"):
    def step(index, carry):
        if order == "relative":
            chunk = jnp.bitwise_xor(index, where[1])
        elif order == "deep":
            chunk = jnp.bitwise_xor(index, where[1] & 3)
        else:
            chunk = 4 * jnp.bitwise_xor(index & 3, where[1] >> 2) + (index >> 2)
        for side, ref in ((0, keep_ref), (1, send_ref)):
            block = 2 * chunk + jnp.bitwise_xor(where[0], side)
            offset = 0
            for piece in pieces:
                values = piece(block)
                count = values.shape[0]
                ref[index, offset : offset + count, :] = low(values)
                offset += count
        return carry

    lax.fori_loop(0, CHUNKS, step, 0)


def rows_of(ref, part=None):
    count = ref.shape[0] // (2 * CHUNKS)

    def piece(block):
        place = pl.ds(pl.multiple_of(block * count, count), count)
        if part is None:
            return ref[place, :]
        return ref[place, part]

    return piece


def column_parts(ref, width):
    return [rows_of(ref, slice(start, start + width)) for start in range(0, ref.shape[1], width)]


def codebook_rows(where, book_ref, per_owner, owners):
    def piece(block):
        side = jnp.bitwise_xor(block & 1, where[0])
        chunk = jnp.bitwise_xor(block >> 1, where[1])
        near = 4 * (chunk & 3) + (chunk >> 2)
        rows = []
        for high in range(owners // CHUNKS):
            far = jnp.bitwise_xor(high, where[2]) if owners > CHUNKS else 0
            owner = side * owners + far * CHUNKS + near
            rows.append(book_ref[pl.ds(pl.multiple_of(owner * per_owner, per_owner), per_owner), :])
        joined = jnp.concatenate(rows, axis=0) if len(rows) > 1 else rows[0]
        count = joined.shape[0] // 4
        return jnp.concatenate([joined[part * count : (part + 1) * count] for part in range(4)], axis=1)

    return piece


def spread_rows(target, *sources):
    target[...] = jnp.zeros_like(target)
    rows = [(ref, row) for ref, count in sources for row in range(count)]
    each = -(-len(rows) // target.shape[0])
    for number, (ref, row) in enumerate(rows):
        block, place = number // each, number % each
        target[block, place : place + 1, :] = ref[row : row + 1, :]


class Token:
    def __init__(self, shape, dtype):
        self.shape, self.dtype = shape, dtype

    def struct(self, groups):
        return jax.ShapeDtypeStruct((groups,) + self.shape, self.dtype)


    def spec(self):
        tail = (0,) * len(self.shape)
        return pl.BlockSpec((None,) + self.shape, lambda group: (group,) + tail)


class Parked(Token):
    def struct(self, groups):
        return pltpu.HBM((groups,) + self.shape, self.dtype)


class Whole:
    def __init__(self, shape, dtype):
        self.shape, self.dtype = shape, dtype

    def struct(self, groups):
        return jax.ShapeDtypeStruct(self.shape, self.dtype)

    def spec(self):
        zeros = (0,) * len(self.shape)
        return pl.BlockSpec(self.shape, lambda group: zeros, pipeline_mode=pl.Buffered(1))


class Loaded:
    def __init__(self, where, side, own, other, held, semaphore):
        self.shape = held.shape
        self.copies = [pltpu.make_async_copy(source, held, semaphore) for source in (own, other)]
        self.where, self.side, self.held, self.waited = where, side, held, False

    def start(self):
        @pl.when(self.where[0] == self.side)
        def _():
            self.copies[0].start()

        @pl.when(self.where[0] != self.side)
        def _():
            self.copies[1].start()

    def __getitem__(self, place):
        if not self.waited:
            self.waited = True

            @pl.when(pl.program_id(0) == 0)
            def _():
                self.copies[0].wait()

        return self.held[place]


def run_groups(
    kernel, name, groups, scalars, tokens, wholes, outs, scratch, flops, vmem, where=None, side=None
):
    in_place = pl.BlockSpec(memory_space=pltpu.HBM)
    pairs = [member for member in wholes if isinstance(member, tuple)]
    if pairs:
        scalars = [where] + list(scalars)
    specs = [pl.BlockSpec(memory_space=pltpu.SMEM)] * len(scalars)
    specs += [Token(array.shape[1:], array.dtype).spec() for array in tokens]
    given = list(scalars) + list(tokens)
    for member in wholes:
        if isinstance(member, tuple):
            specs += [in_place] * 2
            given += list(member)
        else:
            specs.append(Whole(member.shape, member.dtype).spec())
            given.append(member)
    held = [pltpu.VMEM(own.shape, own.dtype) for own, _ in pairs]
    semaphores = [pltpu.SemaphoreType.DMA((len(pairs),))] if pairs else []

    def body(*refs):
        if not pairs:
            return kernel(*refs)
        place, refs = refs[0], list(refs[1:])
        semaphore, refs = refs[-1], refs[:-1]
        holders, refs = refs[len(refs) - len(pairs) :], refs[: len(refs) - len(pairs)]
        first = len(scalars) - 1 + len(tokens)
        arguments, rest = refs[:first], refs[first:]
        weights = []
        for member in wholes:
            if isinstance(member, tuple):
                number = len(weights)
                weights.append(
                    Loaded(place, side, rest[0], rest[1], holders[number], semaphore.at[number])
                )
                arguments.append(weights[-1])
                rest = rest[2:]
            else:
                arguments.append(rest[0])
                rest = rest[1:]

        @pl.when(pl.program_id(0) == 0)
        def _():
            for weight in weights:
                weight.start()

        return kernel(*arguments, *rest)

    return pl.pallas_call(
        body,
        grid=(groups,),
        in_specs=specs,
        out_specs=[out.spec() for out in outs],
        out_shape=[out.struct(groups) for out in outs],
        scratch_shapes=list(scratch) + held + semaphores,
        compiler_params=pltpu.CompilerParams(vmem_limit_bytes=vmem << 20),
        cost_estimate=pl.CostEstimate(flops=flops, bytes_accessed=0, transcendentals=0),
        name=name,
    )(*given)


def in_hbm(array):
    return pltpu.with_memory_space_constraint(array, pltpu.HBM)


def from_section(block):
    return lax.ppermute(block, "section", [(0, 1), (1, 0)])


def from_dp(block, mask):
    count = lax.axis_size("dp")
    return lax.ppermute(block, "dp", [(place, place ^ mask) for place in range(count)])


def from_dp_of(block, mask, side):
    count = lax.axis_size("dp")
    first = side * count
    route = [(first + place, first + (place ^ mask)) for place in range(count)]
    return lax.ppermute(block, ("section", "dp"), route)


def small_call(kernel, name, outs, *given):
    vmem = pl.BlockSpec(memory_space=pltpu.VMEM)
    size = sum(member.size * member.dtype.itemsize for member in given)
    return pl.pallas_call(
        kernel,
        in_specs=[vmem] * len(given),
        out_specs=[vmem] * len(outs),
        out_shape=[jax.ShapeDtypeStruct(shape, HALF) for shape in outs],
        compiler_params=pltpu.CompilerParams(vmem_limit_bytes=VMEM_BYTES),
        cost_estimate=pl.CostEstimate(flops=0, bytes_accessed=2 * size, transcendentals=0),
        name=name,
    )(*given)


def total_of(*values):
    total = values[0].astype(FULL)
    for value in values[1:]:
        total = total + value.astype(FULL)
    return low(total)


PLANE, DEPTH = (1, 2, 3), (4, 8, 12)


def groups_of(masks):
    count = lax.axis_size("dp")
    return [[place ^ mask for mask in (0,) + masks] for place in range(count) if place & masks[2] == 0]


def exchange(blocks, masks):
    return [blocks[0]] + [from_dp(block, mask) for block, mask in zip(blocks[1:], masks)]


def add_cores(name, batches):
    rows = sum(kept.shape[1] for kept, _ in batches)
    width = batches[0][0].shape[2]

    def kernel(*refs):
        outs = refs[-4:]
        for chunk in range(CHUNKS):
            start = 0
            for number in range(len(batches)):
                value = total_of(refs[2 * number][chunk], refs[2 * number + 1][chunk])
                outs[chunk % 4][chunk // 4, start : start + value.shape[0], :] = value
                start += value.shape[0]

    flat = [member for batch in batches for member in batch]
    return small_call(kernel, name + "_cores", [(CHUNKS // 4, rows, width)] * 4, *flat)


def exchange_whole(blocks, masks):
    return lax.all_to_all(
        blocks, "dp", split_axis=0, concat_axis=0, tiled=True, axis_index_groups=groups_of(masks)
    )


def split_cores(name, kept, got):
    half, width = kept.shape[1] // 2, kept.shape[2]

    def kernel(kept_ref, got_ref, *outs):
        for chunk in range(CHUNKS):
            deep, first, second = chunk // 4, chunk & 1, (chunk >> 1) & 1
            value = total_of(kept_ref[chunk], got_ref[chunk])
            outs[first][second, deep] = value[:half]
            outs[2 + second][first, deep] = value[half:]

    return small_call(kernel, name + "_cores", [(2, CHUNKS // 4, half, width)] * 4, kept, got)


def split_again(name, upper, lower):
    shape = upper[0].shape[1:]

    def kernel(*refs):
        for part in range(2):
            for side in range(2):
                refs[4 + 2 * part + side][...] = total_of(refs[2 * part][side], refs[2 * part + 1][side])

    return small_call(kernel, name + "_half", [shape] * 4, *upper, *lower)


def join_split(name, upper, lower, joined):
    half, rows = upper[0].shape[1], 2 * upper[0].shape[1]
    shape = (rows + joined.shape[1], joined.shape[2])

    def kernel(*refs):
        for place in range(4):
            out = refs[5 + place]
            out[:half, :] = total_of(refs[0][place], refs[1][place])
            out[half:rows, :] = total_of(refs[2][place], refs[3][place])
            out[rows:, :] = refs[4][place]

    return small_call(kernel, name + "_plane", [shape] * 4, *upper, *lower, joined)


def stack_plane(name, members):
    def kernel(*refs):
        for place in range(4):
            refs[-1][place] = total_of(*[ref[place] for ref in refs[:4]])

    return small_call(kernel, name + "_plane", [members[0].shape], *members)[0]


def add_stacked(name, members):
    def kernel(source, out):
        out[...] = total_of(*[source[place] for place in range(4)])

    return small_call(kernel, name + "_depth", [members.shape[1:]], members)[0]


def add_plane(name, members, joined=None, shared=None):
    rows = members[0].shape[1]
    middle = rows + (joined.shape[1] if joined is not None else 0)
    end = middle + (shared.shape[0] if shared is not None else 0)
    given = list(members) + [extra for extra in (joined, shared) if extra is not None]

    def kernel(*refs):
        for place in range(4):
            out = refs[-4 + place]
            out[:rows, :] = total_of(*[ref[place] for ref in refs[:4]])
            if middle > rows:
                out[rows:middle, :] = refs[4][place]
            if end > middle:
                out[middle:, :] = refs[len(given) - 1][...]

    return small_call(kernel, name + "_plane", [(end, members[0].shape[2])] * 4, *given)


def add_depth(name, members, rows=None):
    shape = (rows or members[0].shape[0], members[0].shape[1])

    def kernel(*refs):
        refs[-1][...] = total_of(*[ref[: shape[0], :] for ref in refs[:4]])

    return small_call(kernel, name + "_depth", [shape], *members)[0]


def add_far(chunk):
    bit = CHUNKS
    while bit < lax.axis_size("dp"):
        chunk = total_of(chunk, from_dp(chunk, bit))
        bit = 2 * bit
    return chunk


def gather_depth_for(chunk, side):
    own = jnp.stack([chunk, from_section(chunk)])
    return jnp.stack([own] + [from_dp_of(own, mask, side) for mask in DEPTH])


def gather_plane_for(deep, side):
    return [deep] + [from_dp_of(deep, mask, side) for mask in PLANE]


def join_cores(name, batches):
    rows = sum(kept.shape[1] for kept, _ in batches)
    width = batches[0][0].shape[2]

    def kernel(*refs):
        def step(chunk, carry):
            start = 0
            for number in range(len(batches)):
                value = total_of(refs[2 * number][chunk], refs[2 * number + 1][chunk])
                refs[-1][chunk, start : start + value.shape[0], :] = value
                start += value.shape[0]
            return carry

        lax.fori_loop(0, CHUNKS, step, 0, unroll=2)

    flat = [member for batch in batches for member in batch]
    return small_call(kernel, name + "_cores", [(CHUNKS, rows, width)], *flat)[0]


def scatter_group(blocks, masks):
    total = lax.psum_scatter(
        blocks.reshape(-1, blocks.shape[-1]),
        "dp",
        scatter_dimension=0,
        tiled=True,
        axis_index_groups=groups_of(masks),
    )
    return total.reshape(blocks.shape[1:])


def gather_group(block, masks):
    joined = lax.all_gather(
        block.reshape(-1, block.shape[-1]),
        "dp",
        axis=0,
        tiled=True,
        axis_index_groups=groups_of(masks),
    )
    return joined.reshape((4,) + block.shape)


def store_segments(outs, segments, block, piece, rows):
    for offset, size, target, column in segments:
        if offset < rows:
            place = pl.ds(pl.multiple_of(block * size, 16), size)
            values = piece[offset : offset + size, :]
            outs[target][place, column : column + values.shape[1]] = values.astype(FULL)


def unpack_kernel(feed_segments, attention_segments, segments, where, *refs):
    encoder, decoder, outs, small_out = refs[:4], refs[4:8], refs[8:-1], refs[-1]
    few = small_out.shape[1]
    rows = feed_segments[-1][0] + feed_segments[-1][1] + attention_segments[-1][0] + attention_segments[-1][1]
    attention_rows = rows - decoder[0].shape[2]

    @pl.when(where[0] == 0)
    def _():
        for flat in range(4):
            for side in range(2):
                block = 2 * jnp.bitwise_xor(flat, where[1] & 3) + side
                piece = encoder[flat].at[0, side]
                store_segments(outs, segments, block, piece, rows)
                small_out[block] = piece[rows : rows + few, :].astype(FULL)

    @pl.when(where[0] != 0)
    def _():
        for flat in range(4):
            for side in range(2):
                block = 2 * flat + jnp.bitwise_xor(where[0], side)
                piece = decoder[2 * side].at[flat, 0]
                store_segments(outs, feed_segments, block, piece, piece.shape[0])
                piece = decoder[2 * side + 1].at[flat, 0]
                store_segments(outs, attention_segments, block, piece, attention_rows)
                small_out[block] = piece[attention_rows : attention_rows + few, :].astype(FULL)


def after(value, *others):
    return lax.optimization_barrier((value, others))[0]


FEED = ["ln1_gain", "ln1_shift", "qkv_w", "out_w", "ln2_gain", "ln2_shift", "up_w", "up_shift", "down_w"]
ENDS = ["final_gain", "final_shift", "bridge"]


def picked(weights, names):
    return [weights[name] for name in names]


class Sizes:
    def __init__(self, width, hidden, groups, rows):
        self.groups, self.rows, self.width, self.hidden = groups, rows, width, hidden
        blocks = 2 * CHUNKS
        self.down_rows = self.hidden // blocks
        self.thin_rows = self.width // blocks
        self.up_parts = self.hidden // self.width
        self.feed_rows = self.down_rows + self.up_parts * self.thin_rows
        self.attention_rows = 4 * self.thin_rows
        self.small_rows = 16
        rows, width = self.rows, self.width
        self.qkv = Token((3 * PAIRS, rows, LANES), HALF)
        self.lse = Token((HEADS, rows), FULL)
        self.mixed = Token((PAIRS, rows, LANES), HALF)
        self.wide = Token((rows, width), FULL)
        self.wide_low = Token((rows, width), HALF)
        self.hidden_low = Token((rows, self.hidden), HALF)
        self.parked_qkv = Parked((3 * PAIRS, rows, LANES), HALF)
        self.parked_mixed = Parked((PAIRS, rows, LANES), HALF)
        self.parked_wide = Parked((rows, width), FULL)
        self.parked_hidden = Parked((rows, self.hidden), HALF)
        self.latent = Token((rows, LANES), FULL)
        self.latent_low = Token((rows, LANES), HALF)
        self.feed_blocks = Whole((CHUNKS, self.feed_rows, width), HALF)
        self.two_vectors = Whole((2, width), FULL)
        self.feed_vector = Whole((4 + self.up_parts, width), FULL)
        self.bridge = Whole((LANES, width), FULL)
        self.bias_scratch = pltpu.VMEM((rows, rows), FULL)
        self.lse_scratch = pltpu.VMEM((rows, LANES), FULL)
        self.wide_scratch = pltpu.VMEM((rows, width), FULL)
        self.low_scratch = pltpu.VMEM((rows, width), HALF)
        self.mixed_scratch = pltpu.VMEM((PAIRS, rows, LANES), HALF)
        self.qkv_scratch = pltpu.VMEM((3 * PAIRS, rows, LANES), HALF)
        self.hidden_scratch = pltpu.VMEM((rows, self.hidden), HALF)
        self.feed_sums = [
            pltpu.VMEM((self.hidden, width), FULL),
            pltpu.VMEM((width, self.hidden), FULL),
            pltpu.VMEM((1, self.hidden), FULL),
        ]
        self.qkv_sum = pltpu.VMEM((width, 3 * width), FULL)
        self.out_sum = pltpu.VMEM((width, width), FULL)
        self.small_sum = pltpu.VMEM((blocks, self.small_rows, width), FULL)

    def blocks(self, rows):
        return [Whole((CHUNKS, rows, self.width), HALF)] * 2


def encoder_mix(z, lengths, where, patch, weights):
    return run_groups(
        encoder_mix_kernel,
        "encoder_mix",
        z.groups,
        [lengths],
        [patch],
        picked(weights, FEED[:4]),
        [z.parked_qkv, z.lse, z.parked_mixed, z.wide],
        [z.bias_scratch, z.lse_scratch, z.low_scratch],
        10 << 30,
        24,
        where,
        0,
    )


def encoder_latent(z, where, middle, weights):
    return run_groups(
        encoder_latent_kernel,
        "encoder_latent",
        z.groups,
        [],
        [middle],
        picked(weights, FEED[4:] + ENDS),
        [z.parked_hidden, z.parked_hidden, z.parked_wide, z.latent],
        [z.low_scratch],
        12 << 30,
        30,
        where,
        0,
    )


def quantize(z, places, block, latent, pieces):
    count = z.groups * z.rows
    vmem = pl.BlockSpec(memory_space=pltpu.VMEM)
    rows = len(pieces) * pieces[0].shape[0]
    quant, book = pl.pallas_call(
        quant_kernel,
        in_specs=[pl.BlockSpec(memory_space=pltpu.SMEM), vmem, vmem]
        + [pl.BlockSpec(memory_space=pl.ANY)] * len(pieces),
        out_specs=[vmem, vmem],
        out_shape=[
            jax.ShapeDtypeStruct((count, LANES), HALF),
            jax.ShapeDtypeStruct((rows, LANES), FULL),
        ],
        scratch_shapes=[
            pltpu.VMEM((rows, LANES), FULL),
            pltpu.VMEM((count, LANES), FULL),
            pltpu.VMEM((count, LANES), FULL),
            pltpu.SemaphoreType.DMA((len(pieces),)),
        ],
        compiler_params=pltpu.CompilerParams(vmem_limit_bytes=VMEM_BYTES),
        cost_estimate=pl.CostEstimate(flops=8 << 30, bytes_accessed=0, transcendentals=0),
        name="quantize",
    )(places, block.reshape(count, 1), latent.reshape(count, LANES), *pieces)
    return quant.reshape(z.groups, z.rows, LANES), book


def decoder_mix(z, lengths, where, quant, weights):
    return run_groups(
        decoder_mix_kernel,
        "decoder_mix",
        z.groups,
        [lengths],
        [quant],
        picked(weights, FEED[:4] + ENDS[2:]),
        [z.qkv, z.lse, z.mixed, z.wide],
        [z.bias_scratch, z.lse_scratch, z.low_scratch, z.wide_scratch],
        10 << 30,
        26,
        where,
        1,
    )


def decoder_feed(z, where, middle, cotangent, weights):
    return run_groups(
        decoder_feed_kernel,
        "decoder_feed_both",
        z.groups,
        [where],
        [middle, cotangent],
        picked(weights, FEED[4:] + ENDS[:2]),
        [z.wide_low, z.parked_wide, z.feed_blocks, z.feed_blocks, z.feed_vector],
        [z.hidden_scratch, z.hidden_scratch, z.low_scratch, z.low_scratch, z.wide_scratch, z.wide_scratch]
        + z.feed_sums,
        28 << 30,
        36,
        where,
        1,
    )


def decoder_input(z, where, quant, grad_middle, grad_qkv, sums, weights, book, book_rows, latent, owners, per_owner):
    return run_groups(
        functools.partial(decoder_input_kernel, owners=owners, per_owner=per_owner, latent=latent),
        "decoder_input_backward",
        z.groups,
        [where],
        [quant, grad_middle, grad_qkv],
        picked(weights, FEED[:3] + ENDS[2:]) + [book] + sums,
        [z.latent_low]
        + z.blocks(z.attention_rows + z.small_rows + book_rows)
        + [z.two_vectors, z.bridge],
        [z.qkv_sum, z.low_scratch, z.wide_scratch, z.wide_scratch, z.low_scratch, z.small_sum],
        8 << 30,
        24,
        where,
        1,
    )


def encoder_feed(z, where, grad_quant, middle, result, slope, active, weights):
    return run_groups(
        encoder_feed_kernel,
        "encoder_feed_backward",
        z.groups,
        [where],
        [grad_quant, middle, in_hbm(result), in_hbm(slope), in_hbm(active)],
        picked(weights, FEED[4:7] + FEED[8:] + ENDS),
        [z.parked_wide, z.feed_blocks, z.feed_blocks, z.feed_vector, z.bridge],
        [z.low_scratch, z.low_scratch, z.wide_scratch, z.wide_scratch] + z.feed_sums,
        20 << 30,
        36,
        where,
        0,
    )


def attention_gradient(z, name, side, lengths, where, grad_middle, saved, weights):
    return run_groups(
        attention_backward_kernel,
        name,
        z.groups,
        [lengths],
        [in_hbm(grad_middle)] + list(saved),
        picked(weights, ["out_w"]),
        [z.qkv, Whole((z.width, z.width), FULL)],
        [z.bias_scratch, z.mixed_scratch],
        20 << 30,
        22,
        where,
        side,
    )


def encoder_input(z, where, patch, grad_middle, grad_qkv, sums, weights, latent):
    return run_groups(
        functools.partial(encoder_input_kernel, latent=latent),
        "encoder_input_backward",
        z.groups,
        [where],
        [in_hbm(patch), in_hbm(grad_middle), in_hbm(grad_qkv)],
        picked(weights, FEED[:3]) + sums,
        [z.wide_low] + z.blocks(z.attention_rows + z.small_rows) + [z.two_vectors],
        [z.qkv_sum, z.low_scratch, z.wide_scratch, z.small_sum],
        8 << 30,
        24,
        where,
        0,
    )


def on_device(
    section_in,
    ln1_gain,
    ln1_shift,
    qkv_weight,
    out_weight,
    ln2_gain,
    ln2_shift,
    up_weight,
    up_shift,
    down_weight,
    final_gain,
    final_shift,
    bridge_weight,
    codebook,
    codes,
    doc_lengths,
):
    section = lax.axis_index("section")
    encoder_side = section == 0
    micro = doc_lengths.shape[0]
    groups = micro // 2
    rows = section_in.shape[1] // micro
    width = section_in.shape[2]
    hidden_width = up_weight.shape[2]
    latent_width = bridge_weight.shape[1]
    per_device = codebook.shape[1]

    count = lax.axis_size("dp")
    dp = lax.axis_index("dp")
    where = jnp.stack([section, dp & (CHUNKS - 1), dp >> (CHUNKS.bit_length() - 1)]).astype(jnp.int32)

    inverse = lax.rsqrt(jnp.sum(codebook * codebook, axis=0, keepdims=True) + EPS)
    unit_codes = codebook * inverse
    quarter = per_device // 4
    packed = (
        unit_codes.reshape(latent_width, 4, quarter).transpose(2, 1, 0).reshape(quarter, 4 * latent_width)
    )
    deep_table = [packed] + [from_dp(packed, mask) for mask in DEPTH]

    vectors = jnp.concatenate(
        [ln1_gain, ln1_shift, ln2_gain, ln2_shift, final_gain, final_shift]
        + [up_shift.reshape(-1, width), bridge_weight[0].astype(FULL)],
        axis=0,
    )
    qkv_w, out_w, up_w, down_w = qkv_weight[0], out_weight[0], up_weight[0], down_weight[0]
    halves = section_in[0].reshape(2, groups, rows, width)
    other_halves = from_section(section_in[0]).reshape(halves.shape)
    other_vectors, other_qkv, other_out = from_section(vectors), from_section(qkv_w), from_section(out_w)
    patch = jnp.where(encoder_side, halves[0], other_halves[1])
    cotangent = jnp.where(encoder_side, other_halves[0], halves[1])
    lengths = lax.dynamic_slice_in_dim(doc_lengths, section * groups, groups, 0)
    own_codes = lax.dynamic_slice_in_dim(codes, section * groups * rows, groups * rows, 0)
    owner, within = own_codes // per_device, own_codes % per_device
    apart = (owner % count) ^ dp
    place = ((owner // count) ^ section) * count + (apart & -CHUNKS) + 4 * (apart & 3) + ((apart >> 2) & 3)
    places = place * quarter + within % quarter
    code_block = within // quarter
    deep_table, patch, cotangent, other_vectors, other_qkv, other_out = lax.optimization_barrier(
        (deep_table, patch, cotangent, other_vectors, other_qkv, other_out)
    )
    hidden_rows = hidden_width // width

    def vectors_of(vector):
        return dict(
            ln1_gain=vector[0:1],
            ln1_shift=vector[1:2],
            qkv_w=(qkv_w, other_qkv),
            out_w=(out_w, other_out),
            ln2_gain=vector[2:3],
            ln2_shift=vector[3:4],
            up_shift=vector[6 : 6 + hidden_rows].reshape(1, hidden_width),
            final_gain=vector[4:5],
            final_shift=vector[5:6],
            bridge=jnp.pad(low(vector[6 + hidden_rows :]), ((0, LANES - latent_width), (0, 0))),
        )

    encoder = vectors_of(jnp.where(encoder_side, vectors, other_vectors))
    decoder = vectors_of(jnp.where(encoder_side, other_vectors, vectors))
    z = Sizes(width, hidden_width, groups, rows)
    deep_table = jnp.concatenate(deep_table, axis=0)
    table = [deep_table] + [from_dp(deep_table, mask) for mask in PLANE]
    other_up, other_down = from_section(up_w), from_section(down_w)
    encoded = encoder_mix(z, lengths, where, patch, encoder)
    table, other_up, other_down, encoded = lax.optimization_barrier((table, other_up, other_down, encoded))
    qkv_e, lse_e, mixed_e, middle_e = encoded
    encoder.update(up_w=(up_w, other_up), down_w=(down_w, other_down))
    decoder.update(up_w=(up_w, other_up), down_w=(down_w, other_down))
    bit = CHUNKS
    while bit < count:
        table = table + [from_dp(piece, bit) for piece in table]
        bit = 2 * bit
    table = table + [from_section(piece) for piece in table]
    encoded = encoder_latent(z, where, middle_e, encoder)
    table, encoded = lax.optimization_barrier((table, encoded))
    slope_e, active_e, result_e, latent = encoded
    quant, book = quantize(z, places, code_block, latent, table)
    feed_rows, attention_rows = z.feed_rows, z.attention_rows
    book_rows = 4 * latent_width * (lax.axis_size("dp") // CHUNKS) * quarter // width
    qkv_d, lse_d, mixed_d, middle = decoder_mix(z, lengths, where, quant, decoder)
    final, middle_d, keep_1, send_1, vectors_1 = decoder_feed(z, where, middle, cotangent, decoder)
    got_1 = from_section(send_1)
    decoder_mixed = attention_gradient(
        z, "decoder_attention_backward", 1, lengths, where, middle_d, (qkv_d, lse_d, mixed_d), decoder
    )
    got_1, decoder_mixed = lax.optimization_barrier((got_1, decoder_mixed))
    grad_qkv_d, out_sum_d = decoder_mixed
    plane_1 = add_cores("decoder_feed", [(keep_1, got_1)])
    moved_1 = exchange(plane_1, PLANE)
    grad_quant, keep_2, send_2, vectors_2, bridge_d = decoder_input(
        z,
        where,
        quant,
        middle_d,
        after(grad_qkv_d, plane_1[0]),
        [out_sum_d, vectors_1],
        decoder,
        book,
        book_rows,
        latent_width,
        lax.axis_size("dp"),
        quarter,
    )
    got_2 = from_section(send_2)
    middle_grad, keep_3, send_3, vectors_3, bridge_e = encoder_feed(
        z, where, grad_quant, middle_e, result_e, slope_e, active_e, encoder
    )
    moved_1, got_2, middle_grad, keep_3, send_3, vectors_3, bridge_e = lax.optimization_barrier(
        (moved_1, got_2, middle_grad, keep_3, send_3, vectors_3, bridge_e)
    )
    got_3 = from_section(send_3)
    depth_1 = stack_plane("decoder_feed", moved_1)
    joined_2 = join_cores("decoder_attention", [(keep_2, got_2)])
    depth_2 = scatter_group(joined_2.reshape((4, CHUNKS // 4) + joined_2.shape[1:]), PLANE)
    upper, upper_sent, lower, lower_sent = split_cores("encoder_feed", keep_3, got_3)

    middle_grad = after(middle_grad, upper, joined_2, depth_1)
    upper_got, lower_got = from_dp(upper_sent, 1), from_dp(lower_sent, 2)
    deep_1 = exchange_whole(depth_1, DEPTH)
    grad_qkv, out_sum = attention_gradient(
        z, "encoder_attention_backward", 0, lengths, where, middle_grad, (qkv_e, lse_e, mixed_e), encoder
    )
    upper_got, lower_got, deep_1, grad_qkv, out_sum = lax.optimization_barrier(
        (upper_got, lower_got, deep_1, grad_qkv, out_sum)
    )
    upper, upper_sent, lower, lower_sent = split_again("encoder_feed", (upper, upper_got), (lower, lower_got))
    upper_got, lower_got = from_dp(upper_sent, 2), from_dp(lower_sent, 1)
    chunk_1 = add_far(add_stacked("decoder_feed", deep_1))
    near_1 = exchange_whole(jnp.broadcast_to(chunk_1[None], (4,) + chunk_1.shape), DEPTH)
    grad_patch, keep_4, send_4, _ = encoder_input(
        z,
        where,
        patch,
        middle_grad,
        after(grad_qkv, chunk_1, upper),
        [out_sum, vectors_3, bridge_e],
        encoder,
        latent_width,
    )
    upper_got, lower_got, near_1, depth_2, grad_patch, keep_4, send_4 = lax.optimization_barrier(
        (upper_got, lower_got, near_1, depth_2, grad_patch, keep_4, send_4)
    )
    half_1 = gather_group(near_1, PLANE)

    got_4 = from_section(send_4)
    depth_3 = join_split("encoder_feed", (upper, upper_got), (lower, lower_got), depth_2)
    deep_3 = exchange(depth_3, DEPTH)
    plane_4 = add_cores("encoder_attention", [(keep_4, got_4)])
    moved_4 = exchange(plane_4, PLANE)
    deep_3, moved_4 = lax.optimization_barrier((deep_3, moved_4))
    chunk_3 = add_far(add_depth("encoder_feed", deep_3))
    used_rows = attention_rows + z.small_rows
    depth_4 = add_plane("encoder_attention", moved_4, shared=chunk_3[feed_rows : feed_rows + used_rows])
    deep_4 = lax.optimization_barrier(exchange(depth_4, DEPTH))
    chunk_4 = add_far(add_depth("encoder_attention", deep_4, used_rows))
    grad_patch = after(grad_patch, chunk_4)
    sent = jnp.where(encoder_side, final, grad_patch)
    kept = jnp.where(encoder_side, grad_patch, final)
    chunk_e = jnp.concatenate([chunk_3[:feed_rows], chunk_4], axis=0)
    deep_e = gather_depth_for(chunk_e, 0)
    near_2 = jnp.stack([piece[used_rows:] for piece in deep_4])
    half_1, near_2 = lax.optimization_barrier((half_1, near_2))
    half_2 = gather_group(near_2, PLANE)
    deep_e = lax.optimization_barrier(deep_e)
    got = from_section(sent)
    book_sum = chunk_3[feed_rows + attention_rows + z.small_rows :].astype(FULL)
    book_sum = book_sum.reshape(book_rows, 4, LANES).transpose(1, 0, 2).reshape(-1, quarter, LANES)
    book_own = lax.dynamic_index_in_dim(book_sum, lax.axis_index("dp") // CHUNKS, 0, keepdims=False)
    book_grad = (
        book_own.reshape(quarter, 4, latent_width).transpose(2, 1, 0).reshape(latent_width, per_device)
    )
    book_grad = inverse * (
        book_grad - unit_codes * jnp.sum(unit_codes * book_grad, axis=0, keepdims=True)
    )

    section_out = jnp.where(
        encoder_side, jnp.concatenate([kept, got], axis=0), jnp.concatenate([got, kept], axis=0)
    ).reshape(1, micro * rows, width)
    gathered = gather_plane_for(deep_e, 0)
    halves_d = [half_1, half_2]
    halves_d = halves_d + [lax.ppermute(half, "section", [(0, 1)]) for half in halves_d]

    feed_segments = [(0, z.down_rows, 0, 0)] + [
        (z.down_rows + part * z.thin_rows, z.thin_rows, 1, part * width) for part in range(z.up_parts)
    ]
    attention_segments = [(0, z.thin_rows, 3, 0)] + [
        ((part + 1) * z.thin_rows, z.thin_rows, 2, part * width) for part in range(3)
    ]
    segments = feed_segments + [
        (feed_rows + offset, size, target, column) for offset, size, target, column in attention_segments
    ]
    gathered, section_out, book_grad = lax.optimization_barrier((gathered, section_out, book_grad))
    given = gathered + list(halves_d)
    vmem = pl.BlockSpec(memory_space=pltpu.VMEM)
    shapes = [(hidden_width, width), (width, hidden_width), (width, 3 * width), (width, width)]
    shapes.append((2 * CHUNKS, z.small_rows // 2, width))

    def part_of(shape):
        rest = (0,) * (len(shape) - 1)
        return pl.BlockSpec((shape[0] // 4,) + shape[1:], lambda depth, place: (depth,) + rest)

    def near(depth, place, side):
        return jnp.where(place[0] == side, jnp.bitwise_xor(depth, place[1] >> 2), 0)

    def same(depth, place, side):
        return jnp.where(place[0] == side, depth, 0)

    def deep_part(array):
        return pl.BlockSpec((1,) + array.shape[1:], lambda depth, place: (near(depth, place, 0), 0, 0, 0))

    def half_part(array, index):
        shape = (array.shape[0], 1) + array.shape[2:]
        return pl.BlockSpec(shape, lambda depth, place: (0, index(depth, place, 1), 0, 0))

    in_specs = [deep_part(piece) for piece in given[:4]]
    in_specs += [half_part(half, index) for half, index in zip(given[4:], (same, near, same, near))]
    down_total, up_total, qkv_total, out_total, small = pl.pallas_call(
        functools.partial(unpack_kernel, feed_segments, attention_segments, segments),
        grid_spec=pltpu.PrefetchScalarGridSpec(
            num_scalar_prefetch=1,
            grid=(4,),
            in_specs=in_specs,
            out_specs=[part_of(shape) for shape in shapes],
        ),
        out_shape=[jax.ShapeDtypeStruct(shape, FULL) for shape in shapes],
        compiler_params=pltpu.CompilerParams(vmem_limit_bytes=30 << 20),
        name="unpack",
    )(where, *given)

    small_count = 2 + 4 + z.up_parts + latent_width
    small = small[:, : -(-small_count // (2 * CHUNKS))].reshape(-1, width)

    first_vector = 2
    hidden_vector = first_vector + 4
    return (
        section_out,
        small[0:1],
        small[1:2],
        qkv_total[None],
        out_total[None],
        small[2:3],
        small[3:4],
        up_total[None],
        small[hidden_vector : hidden_vector + z.up_parts].reshape(1, hidden_width),
        down_total[None],
        small[4:5],
        small[5:6],
        small[hidden_vector + z.up_parts : hidden_vector + z.up_parts + latent_width][None],
        book_grad,
    )


def solution(mesh):
    placed = (
        P("section", "dp", None),
        P("section", None),
        P("section", None),
        P("section", None, None),
        P("section", None, None),
        P("section", None),
        P("section", None),
        P("section", None, None),
        P("section", None),
        P("section", None, None),
        P("section", None),
        P("section", None),
        P("section", None, None),
        P(None, ("section", "dp")),
        P("dp"),
        P("dp", None),
    )
    return jax.shard_map(
        on_device,
        mesh=mesh,
        in_specs=placed,
        out_specs=(
            P("section", "dp", None),
            P("section", None),
            P("section", None),
            P("section", None, None),
            P("section", None, None),
            P("section", None),
            P("section", None),
            P("section", None, None),
            P("section", None),
            P("section", None, None),
            P("section", None),
            P("section", None),
            P("section", None, None),
            P(None, ("section", "dp")),
        ),
        check_vma=False,
    )
```

```python
import functools

import jax
import jax.numpy as jnp
from jax import lax
from jax.experimental import pallas as pl
from jax.experimental.pallas import tpu as pltpu
from jax.sharding import PartitionSpec as P

HEADS = 8
PAIRS = HEADS // 2
LANES = 128
EPS = 1e-06
GELU_FACTOR = 0.7978845608028654
GELU_CUBIC = 0.044715
BLOCKED = -1000000000.0
CHUNKS = 16
FULL = jnp.float32
HALF = jnp.bfloat16
VMEM_BYTES = 12 * 1024 * 1024


def low(value):
    return value.astype(HALF)


def mm(left, right):
    return lax.dot_general(left, right, (((1,), (0,)), ((), ())), preferred_element_type=FULL)


def mm_nt(left, right):
    return lax.dot_general(left, right, (((1,), (1,)), ((), ())), preferred_element_type=FULL)


def mm_tn(left, right):
    return lax.dot_general(left, right, (((0,), (0,)), ((), ())), preferred_element_type=FULL)


def norm_forward(inputs, gain, shift):
    centred = inputs - jnp.mean(inputs, axis=-1, keepdims=True)
    scaling = lax.rsqrt(jnp.mean(centred * centred, axis=-1, keepdims=True) + EPS)
    normal = centred * scaling
    return normal * gain + shift, normal, scaling


def row_chunks(rows, size=64):
    return [slice(start, start + size) for start in range(0, rows, size)]


def norm_rows(source, target, gain, shift):
    for part in row_chunks(source.shape[0]):
        target[part, :] = low(norm_forward(source[part, :].astype(FULL), gain[...], shift[...])[0])


def write_bias(lengths_ref, group, bias_ref):
    rows = bias_ref.shape[0]
    down = lax.broadcasted_iota(jnp.int32, (rows, rows), 0)
    across = lax.broadcasted_iota(jnp.int32, (rows, rows), 1)
    row_label = jnp.zeros((rows, rows), jnp.int32)
    column_label = jnp.zeros((rows, rows), jnp.int32)
    bound = jnp.int32(0)
    for doc in range(lengths_ref.shape[1]):
        bound = bound + lengths_ref[group, doc]
        row_label = row_label + (down >= bound).astype(jnp.int32)
        column_label = column_label + (across >= bound).astype(jnp.int32)
    bias_ref[...] = jnp.where(row_label == column_label, 0.0, BLOCKED)


def half_mask(rows, side):
    lane = lax.broadcasted_iota(jnp.int32, (rows, LANES), 1)
    return lane < LANES // 2 if side == 0 else lane >= LANES // 2


def attention_forward(qkv_ref, bias_ref, mixed_ref, lse_ref, lse_scratch):
    rows = qkv_ref.shape[1]
    scale = (LANES // 2) ** (-0.5)
    lane = lax.broadcasted_iota(jnp.int32, (rows, LANES), 1)
    lse_scratch[...] = jnp.zeros_like(lse_scratch)

    def pair_step(pair, carry):
        queries = qkv_ref[pair] * jnp.asarray(scale, HALF)
        keys = qkv_ref[PAIRS + pair]
        values = qkv_ref[2 * PAIRS + pair]
        mixed = jnp.zeros((rows, LANES), FULL)
        for side in range(2):
            inside = half_mask(rows, side)
            zero = jnp.zeros((), HALF)
            scores = mm_nt(jnp.where(inside, queries, zero), keys) + bias_ref[...]
            peak = jnp.max(scores, axis=-1, keepdims=True)
            weight = jnp.exp(scores - peak)
            total = jnp.sum(weight, axis=-1, keepdims=True)
            part = mm(low(weight), jnp.where(inside, values, zero))
            mixed = mixed + part * (1.0 / total)
            log_total = peak + jnp.log(total)
            lse_scratch[...] = jnp.where(lane == 2 * pair + side, log_total, lse_scratch[...])
        mixed_ref[pair] = low(mixed)
        return carry

    lax.fori_loop(0, PAIRS, pair_step, 0, unroll=4)
    lse_ref[...] = jnp.transpose(lse_scratch[...])[:HEADS]


def heads_joined(mixed_ref):
    return jnp.concatenate([mixed_ref[pair] for pair in range(PAIRS)], axis=1)


def mix_forward(
    source, weights, bias_ref, qkv_ref, mixed_ref, lse_ref, lse_scratch, normed_ref, middle_ref
):
    ln1_gain, ln1_shift, qkv_w, out_w = weights
    width = source.shape[1]
    norm_rows(source, normed_ref, ln1_gain, ln1_shift)
    for part in range(3):
        projected = low(mm(normed_ref[...], qkv_w[:, part * width : (part + 1) * width]))
        for pair in range(PAIRS):
            qkv_ref[part * PAIRS + pair] = projected[:, pair * LANES : (pair + 1) * LANES]
    attention_forward(qkv_ref, bias_ref, mixed_ref, lse_ref, lse_scratch)
    middle_ref[...] = source[...].astype(FULL) + mm(heads_joined(mixed_ref), out_w[...])


def feed_forward(middle_ref, weights, normed_ref, slope_ref, active_ref, total_ref):
    ln2_gain, ln2_shift, up_w, up_shift, down_w = weights
    hidden_width = up_w.shape[1]
    norm_rows(middle_ref, normed_ref, ln2_gain, ln2_shift)
    tile = middle_ref.shape[1]
    for step in range(hidden_width // tile):
        place = slice(step * tile, (step + 1) * tile)
        hidden = mm(normed_ref[...], up_w[:, place]) + up_shift[:, place]
        square = hidden * hidden
        tangent = jnp.tanh(hidden * ((GELU_FACTOR * GELU_CUBIC) * square + GELU_FACTOR))
        gate = 0.5 * tangent + 0.5
        active = low(hidden * gate)
        bend = hidden * ((1.5 * GELU_FACTOR * GELU_CUBIC) * square + 0.5 * GELU_FACTOR)
        active_ref[:, place] = active
        slope_ref[:, place] = low(gate + bend * (1.0 - tangent * tangent))
        before = middle_ref[...] if step == 0 else total_ref[...]
        total_ref[...] = before + mm(active, down_w[place, :])


def feed_backward(
    upstream_ref,
    middle_ref,
    weights,
    slope_ref,
    active_ref,
    normed_ref,
    branch_ref,
    total_ref,
    down_out,
    up_out,
    up_shift_out,
    grad_middle_ref,
    vector_out,
):
    ln2_gain, ln2_shift, up_w, down_w = weights
    width = upstream_ref.shape[1]
    hidden_width = up_w.shape[1]
    norm_rows(middle_ref, normed_ref, ln2_gain, ln2_shift)
    tile = width

    def hidden_step(step, carry):
        place = pl.ds(step * tile, tile)
        branch = branch_ref[...]
        down_out[place, :] = down_out[place, :] + mm_tn(active_ref[:, place], branch)
        grad_hidden = mm_nt(branch, down_w[place, :]) * slope_ref[:, place].astype(FULL)
        up_shift_out[:, place] = up_shift_out[:, place] + jnp.sum(grad_hidden, axis=0, keepdims=True)
        grad_low = low(grad_hidden)
        up_out[:, place] = up_out[:, place] + mm_tn(normed_ref[...], grad_low)
        share = mm_nt(grad_low, up_w[:, place])
        total_ref[...] = share if step == 0 else total_ref[...] + share
        return carry

    for step in range(hidden_width // tile):
        hidden_step(step, 0)
    norm_backward_rows(
        total_ref, middle_ref, ln2_gain, ln2_shift, vector_out, 0, upstream_ref, grad_middle_ref
    )


def norm_backward_rows(grad_ref, source, gain, shift, vector_out, row, added_ref, *targets):
    width = source.shape[1]
    grad_gain = jnp.zeros((8, width), FULL)
    grad_shift = jnp.zeros((8, width), FULL)
    for part in row_chunks(source.shape[0]):
        _, normal, scaling = norm_forward(source[part, :].astype(FULL), gain[...], shift[...])
        upstream = grad_ref[part, :].astype(FULL)
        scaled = upstream * gain[...]
        inner = scaled - jnp.mean(scaled, axis=-1, keepdims=True)
        inner = inner - normal * jnp.mean(scaled * normal, axis=-1, keepdims=True)
        grad = scaling * inner
        if added_ref is not None:
            grad = grad + added_ref[part, :]
        for target in targets:
            target[part, :] = grad.astype(target.dtype)
        folded = (upstream.shape[0] // 8, 8, width)
        grad_gain = grad_gain + jnp.sum((upstream * normal).reshape(folded), axis=0)
        grad_shift = grad_shift + jnp.sum(upstream.reshape(folded), axis=0)
    add_row(vector_out, row, jnp.sum(grad_gain, axis=0, keepdims=True))
    add_row(vector_out, row + 1, jnp.sum(grad_shift, axis=0, keepdims=True))


def attention_backward(qkv_ref, grad_mixed_ref, bias_ref, lse_ref, grad_qkv_ref):
    rows = qkv_ref.shape[1]
    scale = (LANES // 2) ** (-0.5)

    def pair_step(pair, carry):
        queries = qkv_ref[pair] * jnp.asarray(scale, HALF)
        keys = qkv_ref[PAIRS + pair]
        values = qkv_ref[2 * PAIRS + pair]
        grads = grad_mixed_ref[pair]
        grad_queries = jnp.zeros((rows, LANES), FULL)
        grad_keys = jnp.zeros((rows, LANES), FULL)
        grad_values = jnp.zeros((rows, LANES), FULL)
        for side in range(2):
            inside = half_mask(rows, side)
            zero = jnp.zeros((), HALF)
            side_queries = jnp.where(inside, queries, zero)
            side_grads = jnp.where(inside, grads, zero)
            scores = mm_nt(keys, side_queries) + bias_ref[...]
            attention = jnp.exp(scores - lse_ref[pl.ds(2 * pair + side, 1), :])
            grad_values = grad_values + mm(low(attention), side_grads)
            grad_attention = mm_nt(values, side_grads)
            delta = jnp.sum(attention * grad_attention, axis=0, keepdims=True)
            grad_scores = low(attention * (grad_attention - delta))
            grad_keys = grad_keys + mm(grad_scores, side_queries)
            grad_queries = grad_queries + mm_tn(grad_scores, jnp.where(inside, keys, zero))
        grad_qkv_ref[pair] = low(grad_queries * scale)
        grad_qkv_ref[PAIRS + pair] = low(grad_keys)
        grad_qkv_ref[2 * PAIRS + pair] = low(grad_values)
        return carry

    lax.fori_loop(0, PAIRS, pair_step, 0, unroll=4)


def attention_gradients(
    grad_middle, out_w, bias_ref, qkv_ref, mixed_ref, lse_ref, grad_mixed_ref, grad_qkv_ref, out_out
):
    grad_low = low(grad_middle)
    out_out[...] = out_out[...] + mm_tn(heads_joined(mixed_ref), grad_low)
    grad_mixed = low(mm_nt(grad_low, out_w[...]))
    for pair in range(PAIRS):
        grad_mixed_ref[pair] = grad_mixed[:, pair * LANES : (pair + 1) * LANES]
    attention_backward(qkv_ref, grad_mixed_ref, bias_ref, lse_ref, grad_qkv_ref)


def projection_gradients(
    source, grad_middle_ref, ln1_gain, ln1_shift, qkv_w, grad_qkv_ref, qkv_out, normed_ref, total_ref, vector_out, target
):
    width = source.shape[1]
    norm_rows(source, normed_ref, ln1_gain, ln1_shift)
    for part in range(3):
        grad_part = jnp.concatenate(
            [grad_qkv_ref[part * PAIRS + pair] for pair in range(PAIRS)], axis=1
        )
        place = slice(part * width, (part + 1) * width)
        qkv_out[:, place] = qkv_out[:, place] + mm_tn(normed_ref[...], grad_part)
        share = mm_nt(grad_part, qkv_w[:, place])
        total_ref[...] = share if part == 0 else total_ref[...] + share
    norm_backward_rows(total_ref, source, ln1_gain, ln1_shift, vector_out, 0, grad_middle_ref, target)


def unit_rows(rows):
    inverse = lax.rsqrt(jnp.sum(rows * rows, axis=-1, keepdims=True) + EPS)
    return rows * inverse, inverse


def start_totals(*refs):
    @pl.when(pl.program_id(0) == 0)
    def _():
        for ref in refs:
            ref[...] = jnp.zeros_like(ref)


def encoder_mix_kernel(
    lengths,
    patch,
    ln1_gain,
    ln1_shift,
    qkv_w,
    out_w,
    qkv_ref,
    lse_ref,
    mixed_ref,
    middle_ref,
    bias_ref,
    lse_scratch,
    normed_ref,
):
    write_bias(lengths, pl.program_id(0), bias_ref)
    mix_forward(
        patch,
        (ln1_gain, ln1_shift, qkv_w, out_w),
        bias_ref,
        qkv_ref,
        mixed_ref,
        lse_ref,
        lse_scratch,
        normed_ref,
        middle_ref,
    )


def encoder_latent_kernel(
    middle,
    ln2_gain,
    ln2_shift,
    up_w,
    up_shift,
    down_w,
    final_gain,
    final_shift,
    bridge,
    slope_ref,
    active_ref,
    result_ref,
    latent_ref,
    normed_ref,
):
    weights = (ln2_gain, ln2_shift, up_w, up_shift, down_w)
    feed_forward(middle, weights, normed_ref, slope_ref, active_ref, result_ref)
    norm_rows(result_ref, normed_ref, final_gain, final_shift)
    latent_ref[...] = unit_rows(mm_nt(normed_ref[...], bridge[...]))[0]


def quant_kernel(places, block_column, latent, *refs):
    pieces, (quant_ref, book_ref, table, gathered, spread, semaphore) = refs[:-9], refs[-9:-3]
    books = (book_ref,) + refs[-3:]
    count = gathered.shape[0]
    size = pieces[0].shape[0]
    copies = [
        pltpu.make_async_copy(piece, table.at[pl.ds(number * size, size)], semaphore.at[number])
        for number, piece in enumerate(pieces)
    ]
    for copy in copies:
        copy.start()
    for copy in copies:
        copy.wait()

    def gather(index, carry):
        gathered[pl.ds(index, 1), :] = table[pl.ds(places[index], 1), :]
        return carry

    lax.fori_loop(0, count, gather, 0, unroll=16)
    block = block_column[...]
    lane = lax.broadcasted_iota(jnp.int32, (count, LANES), 1)
    width = LANES // 4
    rows = gathered[...]
    code = jnp.where(block == 0, rows, 0.0)
    for place in range(1, 4):
        code = code + jnp.where(block == place, pltpu.roll(rows, LANES - width * place, 1), 0.0)
    code = jnp.where(lane < width, code, 0.0)
    held = latent[...]
    quant_ref[...] = low(held + (code - held))
    grad = 2.0 * (code - held)
    placed = jnp.where(block == 0, grad, 0.0)
    for place in range(1, 4):
        placed = placed + jnp.where(block == place, pltpu.roll(grad, width * place, 1), 0.0)
    spread[...] = placed
    for book in books:
        book[...] = jnp.zeros_like(book)
    part = count // len(books)

    def scatter(index, carry):
        for number, book in enumerate(books):
            row = number * part + index
            place = pl.ds(places[row], 1)
            book[place, :] = book[place, :] + spread[pl.ds(row, 1), :]
        return carry

    lax.fori_loop(0, part, scatter, 0, unroll=4)
    book_ref[...] = (books[0][...] + books[1][...]) + (books[2][...] + books[3][...])


def add_row(ref, row, value):
    ref[row : row + 1, :] = ref[row : row + 1, :] + value


def feed_vectors(vector_out, up_shift_acc):
    width = vector_out.shape[1]
    for part in range(up_shift_acc.shape[1] // width):
        vector_out[4 + part : 5 + part, :] = up_shift_acc[:, part * width : (part + 1) * width]


def last_group():
    return pl.program_id(0) == pl.num_programs(0) - 1


def decoder_mix_kernel(
    lengths,
    quant,
    ln1_gain,
    ln1_shift,
    qkv_w,
    out_w,
    bridge,
    qkv_ref,
    lse_ref,
    mixed_ref,
    middle_ref,
    bias_ref,
    lse_scratch,
    normed_ref,
    source_ref,
):
    write_bias(lengths, pl.program_id(0), bias_ref)
    source_ref[...] = mm(quant[...], bridge[...])
    mix_forward(
        source_ref,
        (ln1_gain, ln1_shift, qkv_w, out_w),
        bias_ref,
        qkv_ref,
        mixed_ref,
        lse_ref,
        lse_scratch,
        normed_ref,
        middle_ref,
    )


def decoder_feed_kernel(
    where,
    middle_ref,
    cotangent,
    ln2_gain,
    ln2_shift,
    up_w,
    up_shift,
    down_w,
    final_gain,
    final_shift,
    final_ref,
    grad_middle_ref,
    keep_ref,
    send_ref,
    vector_out,
    slope_ref,
    active_ref,
    normed_ref,
    branch_ref,
    result_ref,
    upstream_ref,
    down_acc,
    up_acc,
    up_shift_acc,
):
    start_totals(down_acc, up_acc, up_shift_acc, vector_out)
    weights = (ln2_gain, ln2_shift, up_w, up_shift, down_w)
    feed_forward(middle_ref, weights, normed_ref, slope_ref, active_ref, result_ref)
    norm_rows(result_ref, final_ref, final_gain, final_shift)
    norm_backward_rows(
        cotangent, result_ref, final_gain, final_shift, vector_out, 2, None, upstream_ref, branch_ref
    )
    feed_backward(
        upstream_ref,
        middle_ref,
        (ln2_gain, ln2_shift, up_w, down_w),
        slope_ref,
        active_ref,
        normed_ref,
        branch_ref,
        result_ref,
        down_acc,
        up_acc,
        up_shift_acc,
        grad_middle_ref,
        vector_out,
    )

    @pl.when(last_group())
    def _():
        feed_vectors(vector_out, up_shift_acc)
        pieces = [rows_of(down_acc)] + column_parts(up_acc, middle_ref.shape[1])
        store_blocks(where, keep_ref, send_ref, pieces, order="deep")


def decoder_input_kernel(
    where,
    quant,
    grad_middle,
    grad_qkv_ref,
    ln1_gain,
    ln1_shift,
    qkv_w,
    bridge,
    book,
    out_sum,
    feed_vector,
    grad_quant_ref,
    keep_ref,
    send_ref,
    vector_out,
    bridge_out,
    qkv_acc,
    normed_ref,
    source_ref,
    total_ref,
    grad_lift_ref,
    small_ref,
    *,
    owners,
    per_owner,
    latent,
):
    start_totals(qkv_acc, vector_out, bridge_out)
    source_ref[...] = mm(quant[...], bridge[...])
    projection_gradients(
        source_ref,
        grad_middle,
        ln1_gain,
        ln1_shift,
        qkv_w,
        grad_qkv_ref,
        qkv_acc,
        normed_ref,
        total_ref,
        vector_out,
        grad_lift_ref,
    )
    bridge_out[...] = bridge_out[...] + mm_tn(quant[...], grad_lift_ref[...])
    grad_quant_ref[...] = low(mm_nt(grad_lift_ref[...], bridge[...]))

    @pl.when(last_group())
    def _():
        pieces = [rows_of(out_sum)] + column_parts(qkv_acc, source_ref.shape[1])
        spread_rows(small_ref, (vector_out, 2), (feed_vector, feed_vector.shape[0]), (bridge_out, latent))
        pieces = pieces + [lambda block: small_ref[block], codebook_rows(where, book, per_owner, owners)]
        store_blocks(where, keep_ref, send_ref, pieces, order="flat")


def encoder_feed_kernel(
    where,
    grad_quant,
    middle,
    result,
    slope_ref,
    active_ref,
    ln2_gain,
    ln2_shift,
    up_w,
    down_w,
    final_gain,
    final_shift,
    bridge,
    grad_middle_ref,
    keep_ref,
    send_ref,
    vector_out,
    bridge_out,
    normed_ref,
    branch_ref,
    grad_ref,
    upstream_ref,
    down_acc,
    up_acc,
    up_shift_acc,
):
    start_totals(down_acc, up_acc, up_shift_acc, vector_out, bridge_out)
    norm_rows(result, normed_ref, final_gain, final_shift)
    feature = normed_ref[...]
    latent, inverse = unit_rows(mm_nt(feature, bridge[...]))
    grad_latent = grad_quant[...].astype(FULL)
    grad_projection = low(
        inverse * (grad_latent - latent * jnp.sum(latent * grad_latent, axis=1, keepdims=True))
    )
    bridge_out[...] = bridge_out[...] + mm_tn(grad_projection, feature)
    grad_ref[...] = mm(grad_projection, bridge[...])
    norm_backward_rows(
        grad_ref, result, final_gain, final_shift, vector_out, 2, None, upstream_ref, branch_ref
    )
    feed_backward(
        upstream_ref,
        middle,
        (ln2_gain, ln2_shift, up_w, down_w),
        slope_ref,
        active_ref,
        normed_ref,
        branch_ref,
        grad_ref,
        down_acc,
        up_acc,
        up_shift_acc,
        grad_middle_ref,
        vector_out,
    )

    @pl.when(last_group())
    def _():
        feed_vectors(vector_out, up_shift_acc)
        pieces = [rows_of(down_acc)] + column_parts(up_acc, middle.shape[1])
        store_blocks(where, keep_ref, send_ref, pieces)


def attention_backward_kernel(
    lengths,
    grad_middle,
    qkv_ref,
    lse_ref,
    mixed_ref,
    out_w,
    grad_qkv_ref,
    out_acc,
    bias_ref,
    grad_mixed_ref,
):
    start_totals(out_acc)
    write_bias(lengths, pl.program_id(0), bias_ref)
    attention_gradients(
        grad_middle[...], out_w, bias_ref, qkv_ref, mixed_ref, lse_ref, grad_mixed_ref, grad_qkv_ref, out_acc
    )


def encoder_input_kernel(
    where,
    patch,
    grad_middle,
    grad_qkv_ref,
    ln1_gain,
    ln1_shift,
    qkv_w,
    out_sum,
    feed_vector,
    bridge_sum,
    grad_patch_ref,
    keep_ref,
    send_ref,
    vector_out,
    qkv_acc,
    normed_ref,
    total_ref,
    small_ref,
    *,
    latent,
):
    start_totals(qkv_acc, vector_out)
    projection_gradients(
        patch,
        grad_middle,
        ln1_gain,
        ln1_shift,
        qkv_w,
        grad_qkv_ref,
        qkv_acc,
        normed_ref,
        total_ref,
        vector_out,
        grad_patch_ref,
    )

    @pl.when(last_group())
    def _():
        spread_rows(small_ref, (vector_out, 2), (feed_vector, feed_vector.shape[0]), (bridge_sum, latent))
        pieces = [rows_of(out_sum)] + column_parts(qkv_acc, patch.shape[1])
        store_blocks(where, keep_ref, send_ref, pieces + [lambda block: small_ref[block]])


def store_blocks(where, keep_ref, send_ref, pieces, order="relative"):
    def step(index, carry):
        if order == "relative":
            chunk = jnp.bitwise_xor(index, where[1])
        elif order == "deep":
            chunk = jnp.bitwise_xor(index, where[1] & 3)
        else:
            chunk = 4 * jnp.bitwise_xor(index & 3, where[1] >> 2) + (index >> 2)
        for side, ref in ((0, keep_ref), (1, send_ref)):
            block = 2 * chunk + jnp.bitwise_xor(where[0], side)
            offset = 0
            for piece in pieces:
                values = piece(block)
                count = values.shape[0]
                ref[index, offset : offset + count, :] = low(values)
                offset += count
        return carry

    lax.fori_loop(0, CHUNKS, step, 0)


def rows_of(ref, part=None):
    count = ref.shape[0] // (2 * CHUNKS)

    def piece(block):
        place = pl.ds(pl.multiple_of(block * count, count), count)
        if part is None:
            return ref[place, :]
        return ref[place, part]

    return piece


def column_parts(ref, width):
    return [rows_of(ref, slice(start, start + width)) for start in range(0, ref.shape[1], width)]


def codebook_rows(where, book_ref, per_owner, owners):
    def piece(block):
        side = jnp.bitwise_xor(block & 1, where[0])
        chunk = jnp.bitwise_xor(block >> 1, where[1])
        near = 4 * (chunk & 3) + (chunk >> 2)
        rows = []
        for high in range(owners // CHUNKS):
            far = jnp.bitwise_xor(high, where[2]) if owners > CHUNKS else 0
            owner = side * owners + far * CHUNKS + near
            rows.append(book_ref[pl.ds(pl.multiple_of(owner * per_owner, per_owner), per_owner), :])
        joined = jnp.concatenate(rows, axis=0) if len(rows) > 1 else rows[0]
        count = joined.shape[0] // 4
        return jnp.concatenate([joined[part * count : (part + 1) * count] for part in range(4)], axis=1)

    return piece


def spread_rows(target, *sources):
    target[...] = jnp.zeros_like(target)
    rows = [(ref, row) for ref, count in sources for row in range(count)]
    each = -(-len(rows) // target.shape[0])
    for number, (ref, row) in enumerate(rows):
        block, place = number // each, number % each
        target[block, place : place + 1, :] = ref[row : row + 1, :]


class Token:
    def __init__(self, shape, dtype):
        self.shape, self.dtype = shape, dtype

    def struct(self, groups):
        return jax.ShapeDtypeStruct((groups,) + self.shape, self.dtype)


    def spec(self):
        tail = (0,) * len(self.shape)
        return pl.BlockSpec((None,) + self.shape, lambda group: (group,) + tail)


class Parked(Token):
    def struct(self, groups):
        return pltpu.HBM((groups,) + self.shape, self.dtype)


class Whole:
    def __init__(self, shape, dtype):
        self.shape, self.dtype = shape, dtype

    def struct(self, groups):
        return jax.ShapeDtypeStruct(self.shape, self.dtype)

    def spec(self):
        zeros = (0,) * len(self.shape)
        return pl.BlockSpec(self.shape, lambda group: zeros, pipeline_mode=pl.Buffered(1))


class ParkedWhole(Whole):
    def struct(self, groups):
        return pltpu.HBM(self.shape, self.dtype)


class Loaded:
    def __init__(self, where, side, own, other, held, semaphore):
        self.shape = held.shape
        self.copies = [pltpu.make_async_copy(source, held, semaphore) for source in (own, other)]
        self.where, self.side, self.held, self.waited = where, side, held, False

    def start(self):
        @pl.when(self.where[0] == self.side)
        def _():
            self.copies[0].start()

        @pl.when(self.where[0] != self.side)
        def _():
            self.copies[1].start()

    def __getitem__(self, place):
        if not self.waited:
            self.waited = True

            @pl.when(pl.program_id(0) == 0)
            def _():
                self.copies[0].wait()

        return self.held[place]


def run_groups(
    kernel, name, groups, scalars, tokens, wholes, outs, scratch, flops, vmem, where=None, side=None
):
    in_place = pl.BlockSpec(memory_space=pltpu.HBM)
    pairs = [member for member in wholes if isinstance(member, tuple)]
    if pairs:
        scalars = [where] + list(scalars)
    specs = [pl.BlockSpec(memory_space=pltpu.SMEM)] * len(scalars)
    specs += [Token(array.shape[1:], array.dtype).spec() for array in tokens]
    given = list(scalars) + list(tokens)
    for member in wholes:
        if isinstance(member, tuple):
            specs += [in_place] * 2
            given += [in_hbm(member[0]), member[1]]
        else:
            specs.append(Whole(member.shape, member.dtype).spec())
            given.append(member)
    held = [pltpu.VMEM(own.shape, own.dtype) for own, _ in pairs]
    semaphores = [pltpu.SemaphoreType.DMA((len(pairs),))] if pairs else []

    def body(*refs):
        if not pairs:
            return kernel(*refs)
        place, refs = refs[0], list(refs[1:])
        semaphore, refs = refs[-1], refs[:-1]
        holders, refs = refs[len(refs) - len(pairs) :], refs[: len(refs) - len(pairs)]
        first = len(scalars) - 1 + len(tokens)
        arguments, rest = refs[:first], refs[first:]
        weights = []
        for member in wholes:
            if isinstance(member, tuple):
                number = len(weights)
                weights.append(
                    Loaded(place, side, rest[0], rest[1], holders[number], semaphore.at[number])
                )
                arguments.append(weights[-1])
                rest = rest[2:]
            else:
                arguments.append(rest[0])
                rest = rest[1:]

        @pl.when(pl.program_id(0) == 0)
        def _():
            for weight in weights:
                weight.start()

        return kernel(*arguments, *rest)

    return pl.pallas_call(
        body,
        grid=(groups,),
        in_specs=specs,
        out_specs=[out.spec() for out in outs],
        out_shape=[out.struct(groups) for out in outs],
        scratch_shapes=list(scratch) + held + semaphores,
        compiler_params=pltpu.CompilerParams(vmem_limit_bytes=vmem << 20),
        cost_estimate=pl.CostEstimate(flops=flops, bytes_accessed=0, transcendentals=0),
        name=name,
    )(*given)


def in_hbm(array):
    return pltpu.with_memory_space_constraint(array, pltpu.HBM)


def from_section(block):
    return lax.ppermute(block, "section", [(0, 1), (1, 0)])


def from_dp(block, mask):
    count = lax.axis_size("dp")
    return lax.ppermute(block, "dp", [(place, place ^ mask) for place in range(count)])


def from_dp_of(block, mask, side):
    count = lax.axis_size("dp")
    first = side * count
    route = [(first + place, first + (place ^ mask)) for place in range(count)]
    return lax.ppermute(block, ("section", "dp"), route)


def small_call(kernel, name, outs, *given):
    vmem = pl.BlockSpec(memory_space=pltpu.VMEM)
    size = sum(member.size * member.dtype.itemsize for member in given)
    return pl.pallas_call(
        kernel,
        in_specs=[vmem] * len(given),
        out_specs=[vmem] * len(outs),
        out_shape=[jax.ShapeDtypeStruct(shape, HALF) for shape in outs],
        compiler_params=pltpu.CompilerParams(vmem_limit_bytes=VMEM_BYTES),
        cost_estimate=pl.CostEstimate(flops=0, bytes_accessed=2 * size, transcendentals=0),
        name=name,
    )(*given)


def total_of(*values):
    total = values[0].astype(FULL)
    for value in values[1:]:
        total = total + value.astype(FULL)
    return low(total)


PLANE, DEPTH = (1, 2, 3), (4, 8, 12)


def groups_of(masks):
    count = lax.axis_size("dp")
    return [[place ^ mask for mask in (0,) + masks] for place in range(count) if place & masks[2] == 0]


def exchange(blocks, masks):
    return [blocks[0]] + [from_dp(block, mask) for block, mask in zip(blocks[1:], masks)]


def add_cores(name, batches):
    rows = sum(kept.shape[1] for kept, _ in batches)
    width = batches[0][0].shape[2]

    def kernel(*refs):
        outs = refs[-4:]
        for chunk in range(CHUNKS):
            start = 0
            for number in range(len(batches)):
                value = total_of(refs[2 * number][chunk], refs[2 * number + 1][chunk])
                outs[chunk % 4][chunk // 4, start : start + value.shape[0], :] = value
                start += value.shape[0]

    flat = [member for batch in batches for member in batch]
    return small_call(kernel, name + "_cores", [(CHUNKS // 4, rows, width)] * 4, *flat)


def exchange_whole(blocks, masks):
    return lax.all_to_all(
        blocks, "dp", split_axis=0, concat_axis=0, tiled=True, axis_index_groups=groups_of(masks)
    )


def split_cores(name, kept, got):
    half, width = kept.shape[1] // 2, kept.shape[2]

    def kernel(kept_ref, got_ref, *outs):
        for chunk in range(CHUNKS):
            deep, first, second = chunk // 4, chunk & 1, (chunk >> 1) & 1
            value = total_of(kept_ref[chunk], got_ref[chunk])
            outs[first][second, deep] = value[:half]
            outs[2 + second][first, deep] = value[half:]

    return small_call(kernel, name + "_cores", [(2, CHUNKS // 4, half, width)] * 4, kept, got)


def split_again(name, upper, lower):
    shape = upper[0].shape[1:]

    def kernel(*refs):
        for part in range(2):
            for side in range(2):
                refs[4 + 2 * part + side][...] = total_of(refs[2 * part][side], refs[2 * part + 1][side])

    return small_call(kernel, name + "_half", [shape] * 4, *upper, *lower)


def join_split(name, upper, lower, joined):
    half, rows = upper[0].shape[1], 2 * upper[0].shape[1]
    shape = (rows + joined.shape[1], joined.shape[2])

    def kernel(*refs):
        for place in range(4):
            out = refs[5 + place]
            out[:half, :] = total_of(refs[0][place], refs[1][place])
            out[half:rows, :] = total_of(refs[2][place], refs[3][place])
            out[rows:, :] = refs[4][place]

    return small_call(kernel, name + "_plane", [shape] * 4, *upper, *lower, joined)


def stack_plane(name, members):
    def kernel(*refs):
        for place in range(4):
            refs[-1][place] = total_of(*[ref[place] for ref in refs[:4]])

    return small_call(kernel, name + "_plane", [members[0].shape], *members)[0]


def add_stacked(name, members):
    def kernel(source, out):
        out[...] = total_of(*[source[place] for place in range(4)])

    return small_call(kernel, name + "_depth", [members.shape[1:]], members)[0]


def add_plane(name, members, joined=None, shared=None):
    rows = members[0].shape[1]
    middle = rows + (joined.shape[1] if joined is not None else 0)
    end = middle + (shared.shape[0] if shared is not None else 0)
    given = list(members) + [extra for extra in (joined, shared) if extra is not None]

    def kernel(*refs):
        for place in range(4):
            out = refs[-4 + place]
            out[:rows, :] = total_of(*[ref[place] for ref in refs[:4]])
            if middle > rows:
                out[rows:middle, :] = refs[4][place]
            if end > middle:
                out[middle:, :] = refs[len(given) - 1][...]

    return small_call(kernel, name + "_plane", [(end, members[0].shape[2])] * 4, *given)


def add_depth(name, members, rows=None):
    shape = (rows or members[0].shape[0], members[0].shape[1])

    def kernel(*refs):
        refs[-1][...] = total_of(*[ref[: shape[0], :] for ref in refs[:4]])

    return small_call(kernel, name + "_depth", [shape], *members)[0]


def add_far(chunk):
    bit = CHUNKS
    while bit < lax.axis_size("dp"):
        chunk = total_of(chunk, from_dp(chunk, bit))
        bit = 2 * bit
    return chunk


def gather_depth_for(chunk, side):
    own = jnp.stack([chunk, from_section(chunk)])
    return jnp.stack([own] + [from_dp_of(own, mask, side) for mask in DEPTH])


def gather_plane_for(deep, side):
    return [deep] + [from_dp_of(deep, mask, side) for mask in PLANE]


def join_cores(name, batches):
    rows = sum(kept.shape[1] for kept, _ in batches)
    width = batches[0][0].shape[2]

    def kernel(*refs):
        def step(chunk, carry):
            start = 0
            for number in range(len(batches)):
                value = total_of(refs[2 * number][chunk], refs[2 * number + 1][chunk])
                refs[-1][chunk, start : start + value.shape[0], :] = value
                start += value.shape[0]
            return carry

        lax.fori_loop(0, CHUNKS, step, 0, unroll=2)

    flat = [member for batch in batches for member in batch]
    return small_call(kernel, name + "_cores", [(CHUNKS, rows, width)], *flat)[0]


def scatter_group(blocks, masks):
    total = lax.psum_scatter(
        blocks.reshape(-1, blocks.shape[-1]),
        "dp",
        scatter_dimension=0,
        tiled=True,
        axis_index_groups=groups_of(masks),
    )
    return total.reshape(blocks.shape[1:])


def gather_group(block, masks):
    joined = lax.all_gather(
        block.reshape(-1, block.shape[-1]),
        "dp",
        axis=0,
        tiled=True,
        axis_index_groups=groups_of(masks),
    )
    return joined.reshape((4,) + block.shape)


def store_segments(outs, segments, block, piece, rows):
    for offset, size, target, column in segments:
        if offset < rows:
            place = pl.ds(pl.multiple_of(block * size, 16), size)
            values = piece[offset : offset + size, :]
            outs[target][place, column : column + values.shape[1]] = values.astype(FULL)


def unpack_kernel(feed_segments, attention_segments, segments, where, *refs):
    encoder, decoder, outs, small_out = refs[:4], refs[4:8], refs[8:-1], refs[-1]
    few = small_out.shape[1]
    rows = feed_segments[-1][0] + feed_segments[-1][1] + attention_segments[-1][0] + attention_segments[-1][1]
    attention_rows = rows - decoder[0].shape[2]

    @pl.when(where[0] == 0)
    def _():
        for flat in range(4):
            for side in range(2):
                block = 2 * jnp.bitwise_xor(flat, where[1] & 3) + side
                piece = encoder[flat].at[0, side]
                store_segments(outs, segments, block, piece, rows)
                small_out[block] = piece[rows : rows + few, :].astype(FULL)

    @pl.when(where[0] != 0)
    def _():
        for flat in range(4):
            for side in range(2):
                block = 2 * flat + jnp.bitwise_xor(where[0], side)
                piece = decoder[2 * side].at[flat, 0]
                store_segments(outs, feed_segments, block, piece, piece.shape[0])
                piece = decoder[2 * side + 1].at[flat, 0]
                store_segments(outs, attention_segments, block, piece, attention_rows)
                small_out[block] = piece[attention_rows : attention_rows + few, :].astype(FULL)


def after(value, *others):
    return lax.optimization_barrier((value, others))[0]


FEED = ["ln1_gain", "ln1_shift", "qkv_w", "out_w", "ln2_gain", "ln2_shift", "up_w", "up_shift", "down_w"]
ENDS = ["final_gain", "final_shift", "bridge"]


def picked(weights, names):
    return [weights[name] for name in names]


class Sizes:
    def __init__(self, width, hidden, groups, rows):
        self.groups, self.rows, self.width, self.hidden = groups, rows, width, hidden
        blocks = 2 * CHUNKS
        self.down_rows = self.hidden // blocks
        self.thin_rows = self.width // blocks
        self.up_parts = self.hidden // self.width
        self.feed_rows = self.down_rows + self.up_parts * self.thin_rows
        self.attention_rows = 4 * self.thin_rows
        self.small_rows = 16
        rows, width = self.rows, self.width
        self.qkv = Token((3 * PAIRS, rows, LANES), HALF)
        self.lse = Token((HEADS, rows), FULL)
        self.mixed = Token((PAIRS, rows, LANES), HALF)
        self.wide = Token((rows, width), FULL)
        self.wide_low = Token((rows, width), HALF)
        self.hidden_low = Token((rows, self.hidden), HALF)
        self.parked_qkv = Parked((3 * PAIRS, rows, LANES), HALF)
        self.parked_mixed = Parked((PAIRS, rows, LANES), HALF)
        self.parked_wide = Parked((rows, width), FULL)
        self.parked_hidden = Parked((rows, self.hidden), HALF)
        self.latent = Token((rows, LANES), FULL)
        self.latent_low = Token((rows, LANES), HALF)
        self.feed_blocks = Whole((CHUNKS, self.feed_rows, width), HALF)
        self.two_vectors = Whole((2, width), FULL)
        self.feed_vector = Whole((4 + self.up_parts, width), FULL)
        self.bridge = Whole((LANES, width), FULL)
        self.bias_scratch = pltpu.VMEM((rows, rows), FULL)
        self.lse_scratch = pltpu.VMEM((rows, LANES), FULL)
        self.wide_scratch = pltpu.VMEM((rows, width), FULL)
        self.low_scratch = pltpu.VMEM((rows, width), HALF)
        self.mixed_scratch = pltpu.VMEM((PAIRS, rows, LANES), HALF)
        self.qkv_scratch = pltpu.VMEM((3 * PAIRS, rows, LANES), HALF)
        self.hidden_scratch = pltpu.VMEM((rows, self.hidden), HALF)
        self.feed_sums = [
            pltpu.VMEM((self.hidden, width), FULL),
            pltpu.VMEM((width, self.hidden), FULL),
            pltpu.VMEM((1, self.hidden), FULL),
        ]
        self.qkv_sum = pltpu.VMEM((width, 3 * width), FULL)
        self.out_sum = pltpu.VMEM((width, width), FULL)
        self.small_sum = pltpu.VMEM((blocks, self.small_rows, width), FULL)

    def blocks(self, rows):
        return [Whole((CHUNKS, rows, self.width), HALF)] * 2


def encoder_mix(z, lengths, where, patch, weights):
    return run_groups(
        encoder_mix_kernel,
        "encoder_mix",
        z.groups,
        [lengths],
        [patch],
        picked(weights, FEED[:4]),
        [z.parked_qkv, z.lse, z.parked_mixed, z.wide],
        [z.bias_scratch, z.lse_scratch, z.low_scratch],
        10 << 30,
        24,
        where,
        0,
    )


def encoder_latent(z, where, middle, weights):
    return run_groups(
        encoder_latent_kernel,
        "encoder_latent",
        z.groups,
        [],
        [middle],
        picked(weights, FEED[4:] + ENDS),
        [z.parked_hidden, z.parked_hidden, z.parked_wide, z.latent],
        [z.low_scratch],
        12 << 30,
        30,
        where,
        0,
    )


def quantize(z, places, block, latent, pieces):
    count = z.groups * z.rows
    vmem = pl.BlockSpec(memory_space=pltpu.VMEM)
    rows = len(pieces) * pieces[0].shape[0]
    quant, book = pl.pallas_call(
        quant_kernel,
        in_specs=[pl.BlockSpec(memory_space=pltpu.SMEM), vmem, vmem]
        + [pl.BlockSpec(memory_space=pl.ANY)] * len(pieces),
        out_specs=[vmem, vmem],
        out_shape=[
            jax.ShapeDtypeStruct((count, LANES), HALF),
            jax.ShapeDtypeStruct((rows, LANES), FULL),
        ],
        scratch_shapes=[
            pltpu.VMEM((rows, LANES), FULL),
            pltpu.VMEM((count, LANES), FULL),
            pltpu.VMEM((count, LANES), FULL),
            pltpu.SemaphoreType.DMA((len(pieces),)),
        ]
        + [pltpu.VMEM((rows, LANES), FULL)] * 3,
        compiler_params=pltpu.CompilerParams(vmem_limit_bytes=VMEM_BYTES),
        cost_estimate=pl.CostEstimate(flops=8 << 30, bytes_accessed=0, transcendentals=0),
        name="quantize",
    )(places, block.reshape(count, 1), latent.reshape(count, LANES), *pieces)
    return quant.reshape(z.groups, z.rows, LANES), book


def decoder_mix(z, lengths, where, quant, weights):
    return run_groups(
        decoder_mix_kernel,
        "decoder_mix",
        z.groups,
        [lengths],
        [quant],
        picked(weights, FEED[:4] + ENDS[2:]),
        [z.parked_qkv, z.lse, z.parked_mixed, z.wide],
        [z.bias_scratch, z.lse_scratch, z.low_scratch, z.wide_scratch],
        10 << 30,
        26,
        where,
        1,
    )


def decoder_feed(z, where, middle, cotangent, weights):
    return run_groups(
        decoder_feed_kernel,
        "decoder_feed_both",
        z.groups,
        [where],
        [middle, cotangent],
        picked(weights, FEED[4:] + ENDS[:2]),
        [z.wide_low, z.parked_wide, z.feed_blocks, z.feed_blocks, z.feed_vector],
        [z.hidden_scratch, z.hidden_scratch, z.low_scratch, z.low_scratch, z.wide_scratch, z.wide_scratch]
        + z.feed_sums,
        28 << 30,
        36,
        where,
        1,
    )


def decoder_input(z, where, quant, grad_middle, grad_qkv, sums, weights, book, book_rows, latent, owners, per_owner):
    return run_groups(
        functools.partial(decoder_input_kernel, owners=owners, per_owner=per_owner, latent=latent),
        "decoder_input_backward",
        z.groups,
        [where],
        [quant, grad_middle, in_hbm(grad_qkv)],
        picked(weights, FEED[:3] + ENDS[2:]) + [book, in_hbm(sums[0]), sums[1]],
        [z.latent_low]
        + z.blocks(z.attention_rows + z.small_rows + book_rows)
        + [z.two_vectors, z.bridge],
        [z.qkv_sum, z.low_scratch, z.wide_scratch, z.wide_scratch, z.low_scratch, z.small_sum],
        8 << 30,
        28,
        where,
        1,
    )


def encoder_feed(z, where, grad_quant, middle, result, slope, active, weights):
    return run_groups(
        encoder_feed_kernel,
        "encoder_feed_backward",
        z.groups,
        [where],
        [grad_quant, middle, in_hbm(result), in_hbm(slope), in_hbm(active)],
        picked(weights, FEED[4:7] + FEED[8:] + ENDS),
        [z.parked_wide, z.feed_blocks, z.feed_blocks, z.feed_vector, z.bridge],
        [z.low_scratch, z.low_scratch, z.wide_scratch, z.wide_scratch] + z.feed_sums,
        20 << 30,
        36,
        where,
        0,
    )


def attention_gradient(z, name, side, lengths, where, grad_middle, saved, weights):
    return run_groups(
        attention_backward_kernel,
        name,
        z.groups,
        [lengths],
        [in_hbm(grad_middle), in_hbm(saved[0]), saved[1], in_hbm(saved[2])],
        picked(weights, ["out_w"]),
        [z.parked_qkv, ParkedWhole((z.width, z.width), FULL)],
        [z.bias_scratch, z.mixed_scratch],
        20 << 30,
        26,
        where,
        side,
    )


def encoder_input(z, where, patch, grad_middle, grad_qkv, sums, weights, latent):
    return run_groups(
        functools.partial(encoder_input_kernel, latent=latent),
        "encoder_input_backward",
        z.groups,
        [where],
        [in_hbm(patch), in_hbm(grad_middle), in_hbm(grad_qkv)],
        picked(weights, FEED[:3]) + [in_hbm(sums[0])] + sums[1:],
        [z.wide_low] + z.blocks(z.attention_rows + z.small_rows) + [z.two_vectors],
        [z.qkv_sum, z.low_scratch, z.wide_scratch, z.small_sum],
        8 << 30,
        24,
        where,
        0,
    )


def on_device(
    section_in,
    ln1_gain,
    ln1_shift,
    qkv_weight,
    out_weight,
    ln2_gain,
    ln2_shift,
    up_weight,
    up_shift,
    down_weight,
    final_gain,
    final_shift,
    bridge_weight,
    codebook,
    codes,
    doc_lengths,
):
    section = lax.axis_index("section")
    encoder_side = section == 0
    micro = doc_lengths.shape[0]
    groups = micro // 2
    rows = section_in.shape[1] // micro
    width = section_in.shape[2]
    hidden_width = up_weight.shape[2]
    latent_width = bridge_weight.shape[1]
    per_device = codebook.shape[1]

    count = lax.axis_size("dp")
    dp = lax.axis_index("dp")
    where = jnp.stack([section, dp & (CHUNKS - 1), dp >> (CHUNKS.bit_length() - 1)]).astype(jnp.int32)

    inverse = lax.rsqrt(jnp.sum(codebook * codebook, axis=0, keepdims=True) + EPS)
    unit_codes = codebook * inverse
    quarter = per_device // 4
    packed = (
        unit_codes.reshape(latent_width, 4, quarter).transpose(2, 1, 0).reshape(quarter, 4 * latent_width)
    )
    deep_table = [packed] + [from_dp(packed, mask) for mask in DEPTH]

    vectors = jnp.concatenate(
        [ln1_gain, ln1_shift, ln2_gain, ln2_shift, final_gain, final_shift]
        + [up_shift.reshape(-1, width), bridge_weight[0].astype(FULL)],
        axis=0,
    )
    qkv_w, out_w, up_w, down_w = qkv_weight[0], out_weight[0], up_weight[0], down_weight[0]
    halves = section_in[0].reshape(2, groups, rows, width)
    other_halves = from_section(section_in[0]).reshape(halves.shape)
    other_vectors, other_qkv, other_out = from_section(vectors), from_section(qkv_w), from_section(out_w)
    patch = jnp.where(encoder_side, halves[0], other_halves[1])
    cotangent = jnp.where(encoder_side, other_halves[0], halves[1])
    lengths = lax.dynamic_slice_in_dim(doc_lengths, section * groups, groups, 0)
    own_codes = lax.dynamic_slice_in_dim(codes, section * groups * rows, groups * rows, 0)
    owner, within = own_codes // per_device, own_codes % per_device
    apart = (owner % count) ^ dp
    place = ((owner // count) ^ section) * count + (apart & -CHUNKS) + 4 * (apart & 3) + ((apart >> 2) & 3)
    places = place * quarter + within % quarter
    code_block = within // quarter
    deep_table, patch, cotangent, other_vectors, other_qkv, other_out = lax.optimization_barrier(
        (deep_table, patch, cotangent, other_vectors, other_qkv, other_out)
    )
    hidden_rows = hidden_width // width

    def vectors_of(vector):
        return dict(
            ln1_gain=vector[0:1],
            ln1_shift=vector[1:2],
            qkv_w=(qkv_w, other_qkv),
            out_w=(out_w, other_out),
            ln2_gain=vector[2:3],
            ln2_shift=vector[3:4],
            up_shift=vector[6 : 6 + hidden_rows].reshape(1, hidden_width),
            final_gain=vector[4:5],
            final_shift=vector[5:6],
            bridge=jnp.pad(low(vector[6 + hidden_rows :]), ((0, LANES - latent_width), (0, 0))),
        )

    encoder = vectors_of(jnp.where(encoder_side, vectors, other_vectors))
    decoder = vectors_of(jnp.where(encoder_side, other_vectors, vectors))
    z = Sizes(width, hidden_width, groups, rows)
    deep_table = jnp.concatenate(deep_table, axis=0)
    table = [deep_table] + [from_dp(deep_table, mask) for mask in PLANE]
    other_up, other_down = from_section(up_w), from_section(down_w)
    encoded = encoder_mix(z, lengths, where, patch, encoder)
    table, other_up, other_down, encoded = lax.optimization_barrier((table, other_up, other_down, encoded))
    qkv_e, lse_e, mixed_e, middle_e = encoded
    encoder.update(up_w=(up_w, other_up), down_w=(down_w, other_down))
    decoder.update(up_w=(up_w, other_up), down_w=(down_w, other_down))
    bit = CHUNKS
    while bit < count:
        table = table + [from_dp(piece, bit) for piece in table]
        bit = 2 * bit
    table = table + [from_section(piece) for piece in table]
    encoded = encoder_latent(z, where, middle_e, encoder)
    table, encoded = lax.optimization_barrier((table, encoded))
    slope_e, active_e, result_e, latent = encoded
    quant, book = quantize(z, places, code_block, latent, table)
    feed_rows, attention_rows = z.feed_rows, z.attention_rows
    book_rows = 4 * latent_width * (lax.axis_size("dp") // CHUNKS) * quarter // width
    qkv_d, lse_d, mixed_d, middle = decoder_mix(z, lengths, where, quant, decoder)
    final, middle_d, keep_1, send_1, vectors_1 = decoder_feed(z, where, middle, cotangent, decoder)
    got_1 = from_section(send_1)
    decoder_mixed = attention_gradient(
        z, "decoder_attention_backward", 1, lengths, where, middle_d, (qkv_d, lse_d, mixed_d), decoder
    )
    got_1, decoder_mixed = lax.optimization_barrier((got_1, decoder_mixed))
    grad_qkv_d, out_sum_d = decoder_mixed
    plane_1 = add_cores("decoder_feed", [(keep_1, got_1)])
    moved_1 = exchange(plane_1, PLANE)
    grad_quant, keep_2, send_2, vectors_2, bridge_d = decoder_input(
        z,
        where,
        quant,
        middle_d,
        after(grad_qkv_d, plane_1[0]),
        [out_sum_d, vectors_1],
        decoder,
        book,
        book_rows,
        latent_width,
        lax.axis_size("dp"),
        quarter,
    )
    got_2 = from_section(send_2)
    middle_grad, keep_3, send_3, vectors_3, bridge_e = encoder_feed(
        z, where, grad_quant, middle_e, result_e, slope_e, active_e, encoder
    )
    moved_1, got_2, middle_grad, keep_3, send_3, vectors_3, bridge_e = lax.optimization_barrier(
        (moved_1, got_2, middle_grad, keep_3, send_3, vectors_3, bridge_e)
    )
    got_3 = from_section(send_3)
    depth_1 = stack_plane("decoder_feed", moved_1)
    joined_2 = join_cores("decoder_attention", [(keep_2, got_2)])
    depth_2 = scatter_group(joined_2.reshape((4, CHUNKS // 4) + joined_2.shape[1:]), PLANE)
    upper, upper_sent, lower, lower_sent = split_cores("encoder_feed", keep_3, got_3)

    middle_grad = after(middle_grad, upper, joined_2, depth_1)
    upper_got, lower_got = from_dp(upper_sent, 1), from_dp(lower_sent, 2)
    deep_1 = exchange_whole(depth_1, DEPTH)
    grad_qkv, out_sum = attention_gradient(
        z, "encoder_attention_backward", 0, lengths, where, middle_grad, (qkv_e, lse_e, mixed_e), encoder
    )
    upper_got, lower_got, deep_1, grad_qkv, out_sum = lax.optimization_barrier(
        (upper_got, lower_got, deep_1, grad_qkv, out_sum)
    )
    upper, upper_sent, lower, lower_sent = split_again("encoder_feed", (upper, upper_got), (lower, lower_got))
    upper_got, lower_got = from_dp(upper_sent, 2), from_dp(lower_sent, 1)
    chunk_1 = add_far(add_stacked("decoder_feed", deep_1))
    near_1 = exchange_whole(jnp.broadcast_to(chunk_1[None], (4,) + chunk_1.shape), DEPTH)
    grad_patch, keep_4, send_4, _ = encoder_input(
        z,
        where,
        patch,
        middle_grad,
        after(grad_qkv, chunk_1, upper),
        [out_sum, vectors_3, bridge_e],
        encoder,
        latent_width,
    )
    upper_got, lower_got, near_1, depth_2, grad_patch, keep_4, send_4 = lax.optimization_barrier(
        (upper_got, lower_got, near_1, depth_2, grad_patch, keep_4, send_4)
    )
    half_1 = gather_group(near_1, PLANE)

    got_4 = from_section(send_4)
    depth_3 = join_split("encoder_feed", (upper, upper_got), (lower, lower_got), depth_2)
    deep_3 = exchange(depth_3, DEPTH)
    plane_4 = add_cores("encoder_attention", [(keep_4, got_4)])
    moved_4 = exchange(plane_4, PLANE)
    deep_3, moved_4 = lax.optimization_barrier((deep_3, moved_4))
    chunk_3 = add_far(add_depth("encoder_feed", deep_3))
    used_rows = attention_rows + z.small_rows
    depth_4 = add_plane("encoder_attention", moved_4, shared=chunk_3[feed_rows : feed_rows + used_rows])
    deep_4 = lax.optimization_barrier(exchange(depth_4, DEPTH))
    chunk_4 = add_far(add_depth("encoder_attention", deep_4, used_rows))
    grad_patch = after(grad_patch, chunk_4)
    sent = jnp.where(encoder_side, final, grad_patch)
    kept = jnp.where(encoder_side, grad_patch, final)
    chunk_e = jnp.concatenate([chunk_3[:feed_rows], chunk_4], axis=0)
    deep_e = gather_depth_for(chunk_e, 0)
    near_2 = jnp.stack([piece[used_rows:] for piece in deep_4])
    half_1, near_2 = lax.optimization_barrier((half_1, near_2))
    half_2 = gather_group(near_2, PLANE)
    deep_e = lax.optimization_barrier(deep_e)
    got = from_section(sent)
    book_sum = chunk_3[feed_rows + attention_rows + z.small_rows :].astype(FULL)
    book_sum = book_sum.reshape(book_rows, 4, LANES).transpose(1, 0, 2).reshape(-1, quarter, LANES)
    book_own = lax.dynamic_index_in_dim(book_sum, lax.axis_index("dp") // CHUNKS, 0, keepdims=False)
    book_grad = (
        book_own.reshape(quarter, 4, latent_width).transpose(2, 1, 0).reshape(latent_width, per_device)
    )
    book_grad = inverse * (
        book_grad - unit_codes * jnp.sum(unit_codes * book_grad, axis=0, keepdims=True)
    )

    section_out = jnp.where(
        encoder_side, jnp.concatenate([kept, got], axis=0), jnp.concatenate([got, kept], axis=0)
    ).reshape(1, micro * rows, width)
    gathered = gather_plane_for(deep_e, 0)
    halves_d = [half_1, half_2]
    halves_d = halves_d + [lax.ppermute(half, "section", [(0, 1)]) for half in halves_d]

    feed_segments = [(0, z.down_rows, 0, 0)] + [
        (z.down_rows + part * z.thin_rows, z.thin_rows, 1, part * width) for part in range(z.up_parts)
    ]
    attention_segments = [(0, z.thin_rows, 3, 0)] + [
        ((part + 1) * z.thin_rows, z.thin_rows, 2, part * width) for part in range(3)
    ]
    segments = feed_segments + [
        (feed_rows + offset, size, target, column) for offset, size, target, column in attention_segments
    ]
    gathered, section_out, book_grad = lax.optimization_barrier((gathered, section_out, book_grad))
    given = gathered + list(halves_d)
    vmem = pl.BlockSpec(memory_space=pltpu.VMEM)
    shapes = [(hidden_width, width), (width, hidden_width), (width, 3 * width), (width, width)]
    shapes.append((2 * CHUNKS, z.small_rows // 2, width))

    def part_of(shape):
        rest = (0,) * (len(shape) - 1)
        return pl.BlockSpec((shape[0] // 4,) + shape[1:], lambda depth, place: (depth,) + rest)

    def near(depth, place, side):
        return jnp.where(place[0] == side, jnp.bitwise_xor(depth, place[1] >> 2), 0)

    def same(depth, place, side):
        return jnp.where(place[0] == side, depth, 0)

    def deep_part(array):
        return pl.BlockSpec((1,) + array.shape[1:], lambda depth, place: (near(depth, place, 0), 0, 0, 0))

    def half_part(array, index):
        shape = (array.shape[0], 1) + array.shape[2:]
        return pl.BlockSpec(shape, lambda depth, place: (0, index(depth, place, 1), 0, 0))

    in_specs = [deep_part(piece) for piece in given[:4]]
    in_specs += [half_part(half, index) for half, index in zip(given[4:], (same, near, same, near))]
    down_total, up_total, qkv_total, out_total, small = pl.pallas_call(
        functools.partial(unpack_kernel, feed_segments, attention_segments, segments),
        grid_spec=pltpu.PrefetchScalarGridSpec(
            num_scalar_prefetch=1,
            grid=(4,),
            in_specs=in_specs,
            out_specs=[part_of(shape) for shape in shapes],
        ),
        out_shape=[jax.ShapeDtypeStruct(shape, FULL) for shape in shapes],
        compiler_params=pltpu.CompilerParams(vmem_limit_bytes=30 << 20),
        name="unpack",
    )(where, *given)

    small_count = 2 + 4 + z.up_parts + latent_width
    small = small[:, : -(-small_count // (2 * CHUNKS))].reshape(-1, width)

    first_vector = 2
    hidden_vector = first_vector + 4
    return (
        section_out,
        small[0:1],
        small[1:2],
        qkv_total[None],
        out_total[None],
        small[2:3],
        small[3:4],
        up_total[None],
        small[hidden_vector : hidden_vector + z.up_parts].reshape(1, hidden_width),
        down_total[None],
        small[4:5],
        small[5:6],
        small[hidden_vector + z.up_parts : hidden_vector + z.up_parts + latent_width][None],
        book_grad,
    )


def solution(mesh):
    placed = (
        P("section", "dp", None),
        P("section", None),
        P("section", None),
        P("section", None, None),
        P("section", None, None),
        P("section", None),
        P("section", None),
        P("section", None, None),
        P("section", None),
        P("section", None, None),
        P("section", None),
        P("section", None),
        P("section", None, None),
        P(None, ("section", "dp")),
        P("dp"),
        P("dp", None),
    )
    return jax.shard_map(
        on_device,
        mesh=mesh,
        in_specs=placed,
        out_specs=(
            P("section", "dp", None),
            P("section", None),
            P("section", None),
            P("section", None, None),
            P("section", None, None),
            P("section", None),
            P("section", None),
            P("section", None, None),
            P("section", None),
            P("section", None, None),
            P("section", None),
            P("section", None),
            P("section", None, None),
            P(None, ("section", "dp")),
        ),
        check_vma=False,
    )
```

```python
import functools

import jax
import jax.numpy as jnp
from jax import lax
from jax.experimental import pallas as pl
from jax.experimental.pallas import tpu as pltpu
from jax.sharding import PartitionSpec as P

HEADS = 8
PAIRS = HEADS // 2
LANES = 128
EPS = 1e-06
GELU_FACTOR = 0.7978845608028654
GELU_CUBIC = 0.044715
BLOCKED = -1000000000.0
CHUNKS = 16
FULL = jnp.float32
HALF = jnp.bfloat16
VMEM_BYTES = 12 * 1024 * 1024


def low(value):
    return value.astype(HALF)


def mm(left, right):
    return lax.dot_general(left, right, (((1,), (0,)), ((), ())), preferred_element_type=FULL)


def mm_nt(left, right):
    return lax.dot_general(left, right, (((1,), (1,)), ((), ())), preferred_element_type=FULL)


def mm_tn(left, right):
    return lax.dot_general(left, right, (((0,), (0,)), ((), ())), preferred_element_type=FULL)


def norm_forward(inputs, gain, shift):
    centred = inputs - jnp.mean(inputs, axis=-1, keepdims=True)
    scaling = lax.rsqrt(jnp.mean(centred * centred, axis=-1, keepdims=True) + EPS)
    normal = centred * scaling
    return normal * gain + shift, normal, scaling


def row_chunks(rows, size=64):
    return [slice(start, start + size) for start in range(0, rows, size)]


def norm_rows(source, target, gain, shift):
    for part in row_chunks(source.shape[0]):
        target[part, :] = low(norm_forward(source[part, :].astype(FULL), gain[...], shift[...])[0])


def write_bias(lengths_ref, group, bias_ref):
    rows = bias_ref.shape[0]
    down = lax.broadcasted_iota(jnp.int32, (rows, rows), 0)
    across = lax.broadcasted_iota(jnp.int32, (rows, rows), 1)
    row_label = jnp.zeros((rows, rows), jnp.int32)
    column_label = jnp.zeros((rows, rows), jnp.int32)
    bound = jnp.int32(0)
    for doc in range(lengths_ref.shape[1]):
        bound = bound + lengths_ref[group, doc]
        row_label = row_label + (down >= bound).astype(jnp.int32)
        column_label = column_label + (across >= bound).astype(jnp.int32)
    bias_ref[...] = jnp.where(row_label == column_label, 0.0, BLOCKED)


def half_mask(rows, side):
    lane = lax.broadcasted_iota(jnp.int32, (rows, LANES), 1)
    return lane < LANES // 2 if side == 0 else lane >= LANES // 2


def attention_forward(qkv_ref, bias_ref, mixed_ref, lse_ref, lse_scratch):
    rows = qkv_ref.shape[1]
    scale = (LANES // 2) ** (-0.5)
    lane = lax.broadcasted_iota(jnp.int32, (rows, LANES), 1)
    lse_scratch[...] = jnp.zeros_like(lse_scratch)

    def pair_step(pair, carry):
        queries = qkv_ref[pair] * jnp.asarray(scale, HALF)
        keys = qkv_ref[PAIRS + pair]
        values = qkv_ref[2 * PAIRS + pair]
        mixed = jnp.zeros((rows, LANES), FULL)
        for side in range(2):
            inside = half_mask(rows, side)
            zero = jnp.zeros((), HALF)
            scores = mm_nt(jnp.where(inside, queries, zero), keys) + bias_ref[...]
            peak = jnp.max(scores, axis=-1, keepdims=True)
            weight = jnp.exp(scores - peak)
            total = jnp.sum(weight, axis=-1, keepdims=True)
            part = mm(low(weight), jnp.where(inside, values, zero))
            mixed = mixed + part * (1.0 / total)
            log_total = peak + jnp.log(total)
            lse_scratch[...] = jnp.where(lane == 2 * pair + side, log_total, lse_scratch[...])
        mixed_ref[pair] = low(mixed)
        return carry

    lax.fori_loop(0, PAIRS, pair_step, 0, unroll=4)
    lse_ref[...] = jnp.transpose(lse_scratch[...])[:HEADS]


def heads_joined(mixed_ref):
    return jnp.concatenate([mixed_ref[pair] for pair in range(PAIRS)], axis=1)


def mix_forward(
    source, weights, bias_ref, qkv_ref, mixed_ref, lse_ref, lse_scratch, normed_ref, middle_ref
):
    ln1_gain, ln1_shift, qkv_w, out_w = weights
    width = source.shape[1]
    norm_rows(source, normed_ref, ln1_gain, ln1_shift)
    for part in range(3):
        projected = low(mm(normed_ref[...], qkv_w[:, part * width : (part + 1) * width]))
        for pair in range(PAIRS):
            qkv_ref[part * PAIRS + pair] = projected[:, pair * LANES : (pair + 1) * LANES]
    attention_forward(qkv_ref, bias_ref, mixed_ref, lse_ref, lse_scratch)
    middle_ref[...] = source[...].astype(FULL) + mm(heads_joined(mixed_ref), out_w[...])


def feed_forward(middle_ref, weights, normed_ref, slope_ref, active_ref, total_ref):
    ln2_gain, ln2_shift, up_w, up_shift, down_w = weights
    hidden_width = up_w.shape[1]
    norm_rows(middle_ref, normed_ref, ln2_gain, ln2_shift)
    tile = middle_ref.shape[1]
    for step in range(hidden_width // tile):
        place = slice(step * tile, (step + 1) * tile)
        hidden = mm(normed_ref[...], up_w[:, place]) + up_shift[:, place]
        square = hidden * hidden
        tangent = jnp.tanh(hidden * ((GELU_FACTOR * GELU_CUBIC) * square + GELU_FACTOR))
        gate = 0.5 * tangent + 0.5
        active = low(hidden * gate)
        bend = hidden * ((1.5 * GELU_FACTOR * GELU_CUBIC) * square + 0.5 * GELU_FACTOR)
        active_ref[:, place] = active
        slope_ref[:, place] = low(gate + bend * (1.0 - tangent * tangent))
        before = middle_ref[...] if step == 0 else total_ref[...]
        total_ref[...] = before + mm(active, down_w[place, :])


def feed_backward(
    upstream_ref,
    middle_ref,
    weights,
    slope_ref,
    active_ref,
    normed_ref,
    branch_ref,
    total_ref,
    down_out,
    up_out,
    up_shift_out,
    grad_middle_ref,
    vector_out,
):
    ln2_gain, ln2_shift, up_w, down_w = weights
    width = upstream_ref.shape[1]
    hidden_width = up_w.shape[1]
    norm_rows(middle_ref, normed_ref, ln2_gain, ln2_shift)
    tile = width

    def hidden_step(step, carry):
        place = pl.ds(step * tile, tile)
        branch = branch_ref[...]
        down_out[place, :] = down_out[place, :] + mm_tn(active_ref[:, place], branch)
        grad_hidden = mm_nt(branch, down_w[place, :]) * slope_ref[:, place].astype(FULL)
        up_shift_out[:, place] = up_shift_out[:, place] + jnp.sum(grad_hidden, axis=0, keepdims=True)
        grad_low = low(grad_hidden)
        up_out[:, place] = up_out[:, place] + mm_tn(normed_ref[...], grad_low)
        share = mm_nt(grad_low, up_w[:, place])
        total_ref[...] = share if step == 0 else total_ref[...] + share
        return carry

    for step in range(hidden_width // tile):
        hidden_step(step, 0)
    norm_backward_rows(
        total_ref, middle_ref, ln2_gain, ln2_shift, vector_out, 0, upstream_ref, grad_middle_ref
    )


def norm_backward_rows(grad_ref, source, gain, shift, vector_out, row, added_ref, *targets):
    width = source.shape[1]
    grad_gain = jnp.zeros((8, width), FULL)
    grad_shift = jnp.zeros((8, width), FULL)
    for part in row_chunks(source.shape[0]):
        _, normal, scaling = norm_forward(source[part, :].astype(FULL), gain[...], shift[...])
        upstream = grad_ref[part, :].astype(FULL)
        scaled = upstream * gain[...]
        inner = scaled - jnp.mean(scaled, axis=-1, keepdims=True)
        inner = inner - normal * jnp.mean(scaled * normal, axis=-1, keepdims=True)
        grad = scaling * inner
        if added_ref is not None:
            grad = grad + added_ref[part, :]
        for target in targets:
            target[part, :] = grad.astype(target.dtype)
        folded = (upstream.shape[0] // 8, 8, width)
        grad_gain = grad_gain + jnp.sum((upstream * normal).reshape(folded), axis=0)
        grad_shift = grad_shift + jnp.sum(upstream.reshape(folded), axis=0)
    add_row(vector_out, row, jnp.sum(grad_gain, axis=0, keepdims=True))
    add_row(vector_out, row + 1, jnp.sum(grad_shift, axis=0, keepdims=True))


def attention_backward(qkv_ref, grad_mixed_ref, bias_ref, lse_ref, grad_qkv_ref):
    rows = qkv_ref.shape[1]
    scale = (LANES // 2) ** (-0.5)

    def pair_step(pair, carry):
        queries = qkv_ref[pair] * jnp.asarray(scale, HALF)
        keys = qkv_ref[PAIRS + pair]
        values = qkv_ref[2 * PAIRS + pair]
        grads = grad_mixed_ref[pair]
        grad_queries = jnp.zeros((rows, LANES), FULL)
        grad_keys = jnp.zeros((rows, LANES), FULL)
        grad_values = jnp.zeros((rows, LANES), FULL)
        for side in range(2):
            inside = half_mask(rows, side)
            zero = jnp.zeros((), HALF)
            side_queries = jnp.where(inside, queries, zero)
            side_grads = jnp.where(inside, grads, zero)
            scores = mm_nt(keys, side_queries) + bias_ref[...]
            attention = jnp.exp(scores - lse_ref[pl.ds(2 * pair + side, 1), :])
            grad_values = grad_values + mm(low(attention), side_grads)
            grad_attention = mm_nt(values, side_grads)
            delta = jnp.sum(attention * grad_attention, axis=0, keepdims=True)
            grad_scores = low(attention * (grad_attention - delta))
            grad_keys = grad_keys + mm(grad_scores, side_queries)
            grad_queries = grad_queries + mm_tn(grad_scores, jnp.where(inside, keys, zero))
        grad_qkv_ref[pair] = low(grad_queries * scale)
        grad_qkv_ref[PAIRS + pair] = low(grad_keys)
        grad_qkv_ref[2 * PAIRS + pair] = low(grad_values)
        return carry

    lax.fori_loop(0, PAIRS, pair_step, 0, unroll=4)


def attention_gradients(
    grad_middle, out_w, bias_ref, qkv_ref, mixed_ref, lse_ref, grad_mixed_ref, grad_qkv_ref, out_out
):
    grad_low = low(grad_middle)
    out_out[...] = out_out[...] + mm_tn(heads_joined(mixed_ref), grad_low)
    grad_mixed = low(mm_nt(grad_low, out_w[...]))
    for pair in range(PAIRS):
        grad_mixed_ref[pair] = grad_mixed[:, pair * LANES : (pair + 1) * LANES]
    attention_backward(qkv_ref, grad_mixed_ref, bias_ref, lse_ref, grad_qkv_ref)


def projection_gradients(
    source, grad_middle_ref, ln1_gain, ln1_shift, qkv_w, grad_qkv_ref, qkv_out, normed_ref, total_ref, vector_out, target
):
    width = source.shape[1]
    norm_rows(source, normed_ref, ln1_gain, ln1_shift)
    for part in range(3):
        grad_part = jnp.concatenate(
            [grad_qkv_ref[part * PAIRS + pair] for pair in range(PAIRS)], axis=1
        )
        place = slice(part * width, (part + 1) * width)
        qkv_out[:, place] = qkv_out[:, place] + mm_tn(normed_ref[...], grad_part)
        share = mm_nt(grad_part, qkv_w[:, place])
        total_ref[...] = share if part == 0 else total_ref[...] + share
    norm_backward_rows(total_ref, source, ln1_gain, ln1_shift, vector_out, 0, grad_middle_ref, target)


def unit_rows(rows):
    inverse = lax.rsqrt(jnp.sum(rows * rows, axis=-1, keepdims=True) + EPS)
    return rows * inverse, inverse


def start_totals(*refs):
    @pl.when(pl.program_id(0) == 0)
    def _():
        for ref in refs:
            ref[...] = jnp.zeros_like(ref)


def encoder_mix_kernel(
    lengths,
    patch,
    ln1_gain,
    ln1_shift,
    qkv_w,
    out_w,
    qkv_ref,
    lse_ref,
    mixed_ref,
    middle_ref,
    bias_ref,
    lse_scratch,
    normed_ref,
):
    write_bias(lengths, pl.program_id(0), bias_ref)
    mix_forward(
        patch,
        (ln1_gain, ln1_shift, qkv_w, out_w),
        bias_ref,
        qkv_ref,
        mixed_ref,
        lse_ref,
        lse_scratch,
        normed_ref,
        middle_ref,
    )


def encoder_latent_kernel(
    middle,
    ln2_gain,
    ln2_shift,
    up_w,
    up_shift,
    down_w,
    final_gain,
    final_shift,
    bridge,
    slope_ref,
    active_ref,
    result_ref,
    latent_ref,
    normed_ref,
):
    weights = (ln2_gain, ln2_shift, up_w, up_shift, down_w)
    feed_forward(middle, weights, normed_ref, slope_ref, active_ref, result_ref)
    norm_rows(result_ref, normed_ref, final_gain, final_shift)
    latent_ref[...] = unit_rows(mm_nt(normed_ref[...], bridge[...]))[0]


def quant_kernel(places, block_column, latent, *refs):
    pieces, (quant_ref, book_ref, table, gathered, spread, semaphore) = refs[:-9], refs[-9:-3]
    books = (book_ref,) + refs[-3:]
    count = gathered.shape[0]
    size = pieces[0].shape[0]
    copies = [
        pltpu.make_async_copy(piece, table.at[pl.ds(number * size, size)], semaphore.at[number])
        for number, piece in enumerate(pieces)
    ]
    for copy in copies:
        copy.start()
    for copy in copies:
        copy.wait()

    def gather(index, carry):
        gathered[pl.ds(index, 1), :] = table[pl.ds(places[index], 1), :]
        return carry

    lax.fori_loop(0, count, gather, 0, unroll=16)
    block = block_column[...]
    lane = lax.broadcasted_iota(jnp.int32, (count, LANES), 1)
    width = LANES // 4
    rows = gathered[...]
    code = jnp.where(block == 0, rows, 0.0)
    for place in range(1, 4):
        code = code + jnp.where(block == place, pltpu.roll(rows, LANES - width * place, 1), 0.0)
    code = jnp.where(lane < width, code, 0.0)
    held = latent[...]
    quant_ref[...] = low(held + (code - held))
    grad = 2.0 * (code - held)
    placed = jnp.where(block == 0, grad, 0.0)
    for place in range(1, 4):
        placed = placed + jnp.where(block == place, pltpu.roll(grad, width * place, 1), 0.0)
    spread[...] = placed
    for book in books:
        book[...] = jnp.zeros_like(book)
    part = count // len(books)

    def scatter(index, carry):
        for number, book in enumerate(books):
            row = number * part + index
            place = pl.ds(places[row], 1)
            book[place, :] = book[place, :] + spread[pl.ds(row, 1), :]
        return carry

    lax.fori_loop(0, part, scatter, 0, unroll=4)
    book_ref[...] = (books[0][...] + books[1][...]) + (books[2][...] + books[3][...])


def add_row(ref, row, value):
    ref[row : row + 1, :] = ref[row : row + 1, :] + value


def feed_vectors(vector_out, up_shift_acc):
    width = vector_out.shape[1]
    for part in range(up_shift_acc.shape[1] // width):
        vector_out[4 + part : 5 + part, :] = up_shift_acc[:, part * width : (part + 1) * width]


def last_group():
    return pl.program_id(0) == pl.num_programs(0) - 1


def decoder_mix_kernel(
    lengths,
    quant,
    ln1_gain,
    ln1_shift,
    qkv_w,
    out_w,
    bridge,
    qkv_ref,
    lse_ref,
    mixed_ref,
    middle_ref,
    bias_ref,
    lse_scratch,
    normed_ref,
    source_ref,
):
    write_bias(lengths, pl.program_id(0), bias_ref)
    source_ref[...] = mm(quant[...], bridge[...])
    mix_forward(
        source_ref,
        (ln1_gain, ln1_shift, qkv_w, out_w),
        bias_ref,
        qkv_ref,
        mixed_ref,
        lse_ref,
        lse_scratch,
        normed_ref,
        middle_ref,
    )


def decoder_feed_kernel(
    where,
    middle_ref,
    cotangent,
    ln2_gain,
    ln2_shift,
    up_w,
    up_shift,
    down_w,
    final_gain,
    final_shift,
    final_ref,
    grad_middle_ref,
    keep_ref,
    send_ref,
    vector_out,
    slope_ref,
    active_ref,
    normed_ref,
    branch_ref,
    result_ref,
    upstream_ref,
    down_acc,
    up_acc,
    up_shift_acc,
):
    start_totals(down_acc, up_acc, up_shift_acc, vector_out)
    weights = (ln2_gain, ln2_shift, up_w, up_shift, down_w)
    feed_forward(middle_ref, weights, normed_ref, slope_ref, active_ref, result_ref)
    norm_rows(result_ref, final_ref, final_gain, final_shift)
    norm_backward_rows(
        cotangent, result_ref, final_gain, final_shift, vector_out, 2, None, upstream_ref, branch_ref
    )
    feed_backward(
        upstream_ref,
        middle_ref,
        (ln2_gain, ln2_shift, up_w, down_w),
        slope_ref,
        active_ref,
        normed_ref,
        branch_ref,
        result_ref,
        down_acc,
        up_acc,
        up_shift_acc,
        grad_middle_ref,
        vector_out,
    )

    @pl.when(last_group())
    def _():
        feed_vectors(vector_out, up_shift_acc)
        pieces = [rows_of(down_acc)] + column_parts(up_acc, middle_ref.shape[1])
        store_blocks(where, keep_ref, send_ref, pieces, order="deep")


def decoder_input_kernel(
    where,
    quant,
    grad_middle,
    grad_qkv_ref,
    ln1_gain,
    ln1_shift,
    qkv_w,
    bridge,
    book,
    out_sum,
    feed_vector,
    grad_quant_ref,
    keep_ref,
    send_ref,
    vector_out,
    bridge_out,
    qkv_acc,
    normed_ref,
    source_ref,
    total_ref,
    grad_lift_ref,
    small_ref,
    *,
    owners,
    per_owner,
    latent,
):
    start_totals(qkv_acc, vector_out, bridge_out)
    source_ref[...] = mm(quant[...], bridge[...])
    projection_gradients(
        source_ref,
        grad_middle,
        ln1_gain,
        ln1_shift,
        qkv_w,
        grad_qkv_ref,
        qkv_acc,
        normed_ref,
        total_ref,
        vector_out,
        grad_lift_ref,
    )
    bridge_out[...] = bridge_out[...] + mm_tn(quant[...], grad_lift_ref[...])
    grad_quant_ref[...] = low(mm_nt(grad_lift_ref[...], bridge[...]))

    @pl.when(last_group())
    def _():
        pieces = [rows_of(out_sum)] + column_parts(qkv_acc, source_ref.shape[1])
        spread_rows(small_ref, (vector_out, 2), (feed_vector, feed_vector.shape[0]), (bridge_out, latent))
        pieces = pieces + [lambda block: small_ref[block], codebook_rows(where, book, per_owner, owners)]
        store_blocks(where, keep_ref, send_ref, pieces, order="flat")


def encoder_feed_kernel(
    where,
    grad_quant,
    middle,
    result,
    slope_ref,
    active_ref,
    ln2_gain,
    ln2_shift,
    up_w,
    down_w,
    final_gain,
    final_shift,
    bridge,
    grad_middle_ref,
    keep_ref,
    send_ref,
    vector_out,
    bridge_out,
    normed_ref,
    branch_ref,
    grad_ref,
    upstream_ref,
    down_acc,
    up_acc,
    up_shift_acc,
):
    start_totals(down_acc, up_acc, up_shift_acc, vector_out, bridge_out)
    norm_rows(result, normed_ref, final_gain, final_shift)
    feature = normed_ref[...]
    latent, inverse = unit_rows(mm_nt(feature, bridge[...]))
    grad_latent = grad_quant[...].astype(FULL)
    grad_projection = low(
        inverse * (grad_latent - latent * jnp.sum(latent * grad_latent, axis=1, keepdims=True))
    )
    bridge_out[...] = bridge_out[...] + mm_tn(grad_projection, feature)
    grad_ref[...] = mm(grad_projection, bridge[...])
    norm_backward_rows(
        grad_ref, result, final_gain, final_shift, vector_out, 2, None, upstream_ref, branch_ref
    )
    feed_backward(
        upstream_ref,
        middle,
        (ln2_gain, ln2_shift, up_w, down_w),
        slope_ref,
        active_ref,
        normed_ref,
        branch_ref,
        grad_ref,
        down_acc,
        up_acc,
        up_shift_acc,
        grad_middle_ref,
        vector_out,
    )

    @pl.when(last_group())
    def _():
        feed_vectors(vector_out, up_shift_acc)
        pieces = [rows_of(down_acc)] + column_parts(up_acc, middle.shape[1])
        store_blocks(where, keep_ref, send_ref, pieces)


def attention_backward_kernel(
    lengths,
    grad_middle,
    qkv_ref,
    lse_ref,
    mixed_ref,
    out_w,
    grad_qkv_ref,
    out_acc,
    bias_ref,
    grad_mixed_ref,
):
    start_totals(out_acc)
    write_bias(lengths, pl.program_id(0), bias_ref)
    attention_gradients(
        grad_middle[...], out_w, bias_ref, qkv_ref, mixed_ref, lse_ref, grad_mixed_ref, grad_qkv_ref, out_acc
    )


def encoder_input_kernel(
    where,
    patch,
    grad_middle,
    grad_qkv_ref,
    ln1_gain,
    ln1_shift,
    qkv_w,
    out_sum,
    feed_vector,
    bridge_sum,
    grad_patch_ref,
    keep_ref,
    send_ref,
    vector_out,
    qkv_acc,
    normed_ref,
    total_ref,
    small_ref,
    *,
    latent,
):
    start_totals(qkv_acc, vector_out)
    projection_gradients(
        patch,
        grad_middle,
        ln1_gain,
        ln1_shift,
        qkv_w,
        grad_qkv_ref,
        qkv_acc,
        normed_ref,
        total_ref,
        vector_out,
        grad_patch_ref,
    )

    @pl.when(last_group())
    def _():
        spread_rows(small_ref, (vector_out, 2), (feed_vector, feed_vector.shape[0]), (bridge_sum, latent))
        pieces = [rows_of(out_sum)] + column_parts(qkv_acc, patch.shape[1])
        store_blocks(where, keep_ref, send_ref, pieces + [lambda block: small_ref[block]])


def store_blocks(where, keep_ref, send_ref, pieces, order="relative"):
    def step(index, carry):
        if order == "relative":
            chunk = jnp.bitwise_xor(index, where[1])
        elif order == "deep":
            chunk = jnp.bitwise_xor(index, where[1] & 3)
        else:
            chunk = 4 * jnp.bitwise_xor(index & 3, where[1] >> 2) + (index >> 2)
        for side, ref in ((0, keep_ref), (1, send_ref)):
            block = 2 * chunk + jnp.bitwise_xor(where[0], side)
            offset = 0
            for piece in pieces:
                values = piece(block)
                count = values.shape[0]
                ref[index, offset : offset + count, :] = low(values)
                offset += count
        return carry

    lax.fori_loop(0, CHUNKS, step, 0)


def rows_of(ref, part=None):
    count = ref.shape[0] // (2 * CHUNKS)

    def piece(block):
        place = pl.ds(pl.multiple_of(block * count, count), count)
        if part is None:
            return ref[place, :]
        return ref[place, part]

    return piece


def column_parts(ref, width):
    return [rows_of(ref, slice(start, start + width)) for start in range(0, ref.shape[1], width)]


def codebook_rows(where, book_ref, per_owner, owners):
    def piece(block):
        side = jnp.bitwise_xor(block & 1, where[0])
        chunk = jnp.bitwise_xor(block >> 1, where[1])
        near = 4 * (chunk & 3) + (chunk >> 2)
        rows = []
        for high in range(owners // CHUNKS):
            far = jnp.bitwise_xor(high, where[2]) if owners > CHUNKS else 0
            owner = side * owners + far * CHUNKS + near
            rows.append(book_ref[pl.ds(pl.multiple_of(owner * per_owner, per_owner), per_owner), :])
        joined = jnp.concatenate(rows, axis=0) if len(rows) > 1 else rows[0]
        count = joined.shape[0] // 4
        return jnp.concatenate([joined[part * count : (part + 1) * count] for part in range(4)], axis=1)

    return piece


def spread_rows(target, *sources):
    target[...] = jnp.zeros_like(target)
    rows = [(ref, row) for ref, count in sources for row in range(count)]
    each = -(-len(rows) // target.shape[0])
    for number, (ref, row) in enumerate(rows):
        block, place = number // each, number % each
        target[block, place : place + 1, :] = ref[row : row + 1, :]


class Token:
    def __init__(self, shape, dtype):
        self.shape, self.dtype = shape, dtype

    def struct(self, groups):
        return jax.ShapeDtypeStruct((groups,) + self.shape, self.dtype)


    def spec(self):
        tail = (0,) * len(self.shape)
        return pl.BlockSpec((None,) + self.shape, lambda group: (group,) + tail)


class Parked(Token):
    def struct(self, groups):
        return pltpu.HBM((groups,) + self.shape, self.dtype)


class Whole:
    def __init__(self, shape, dtype):
        self.shape, self.dtype = shape, dtype

    def struct(self, groups):
        return jax.ShapeDtypeStruct(self.shape, self.dtype)

    def spec(self):
        zeros = (0,) * len(self.shape)
        return pl.BlockSpec(self.shape, lambda group: zeros, pipeline_mode=pl.Buffered(1))


class ParkedWhole(Whole):
    def struct(self, groups):
        return pltpu.HBM(self.shape, self.dtype)


class Loaded:
    def __init__(self, where, side, own, other, held, semaphore):
        self.shape = held.shape
        self.copies = [pltpu.make_async_copy(source, held, semaphore) for source in (own, other)]
        self.where, self.side, self.held, self.waited = where, side, held, False

    def start(self):
        @pl.when(self.where[0] == self.side)
        def _():
            self.copies[0].start()

        @pl.when(self.where[0] != self.side)
        def _():
            self.copies[1].start()

    def __getitem__(self, place):
        if not self.waited:
            self.waited = True

            @pl.when(pl.program_id(0) == 0)
            def _():
                self.copies[0].wait()

        return self.held[place]


def run_groups(
    kernel, name, groups, scalars, tokens, wholes, outs, scratch, flops, vmem, where=None, side=None
):
    in_place = pl.BlockSpec(memory_space=pltpu.HBM)
    pairs = [member for member in wholes if isinstance(member, tuple)]
    if pairs:
        scalars = [where] + list(scalars)
    specs = [pl.BlockSpec(memory_space=pltpu.SMEM)] * len(scalars)
    specs += [Token(array.shape[1:], array.dtype).spec() for array in tokens]
    given = list(scalars) + list(tokens)
    for member in wholes:
        if isinstance(member, tuple):
            specs += [in_place] * 2
            given += [in_hbm(member[0]), member[1]]
        else:
            specs.append(Whole(member.shape, member.dtype).spec())
            given.append(member)
    held = [pltpu.VMEM(own.shape, own.dtype) for own, _ in pairs]
    semaphores = [pltpu.SemaphoreType.DMA((len(pairs),))] if pairs else []

    def body(*refs):
        if not pairs:
            return kernel(*refs)
        place, refs = refs[0], list(refs[1:])
        semaphore, refs = refs[-1], refs[:-1]
        holders, refs = refs[len(refs) - len(pairs) :], refs[: len(refs) - len(pairs)]
        first = len(scalars) - 1 + len(tokens)
        arguments, rest = refs[:first], refs[first:]
        weights = []
        for member in wholes:
            if isinstance(member, tuple):
                number = len(weights)
                weights.append(
                    Loaded(place, side, rest[0], rest[1], holders[number], semaphore.at[number])
                )
                arguments.append(weights[-1])
                rest = rest[2:]
            else:
                arguments.append(rest[0])
                rest = rest[1:]

        @pl.when(pl.program_id(0) == 0)
        def _():
            for weight in weights:
                weight.start()

        return kernel(*arguments, *rest)

    return pl.pallas_call(
        body,
        grid=(groups,),
        in_specs=specs,
        out_specs=[out.spec() for out in outs],
        out_shape=[out.struct(groups) for out in outs],
        scratch_shapes=list(scratch) + held + semaphores,
        compiler_params=pltpu.CompilerParams(vmem_limit_bytes=vmem << 20),
        cost_estimate=pl.CostEstimate(flops=flops, bytes_accessed=0, transcendentals=0),
        name=name,
    )(*given)


def in_hbm(array):
    return pltpu.with_memory_space_constraint(array, pltpu.HBM)


def from_section(block):
    return lax.ppermute(block, "section", [(0, 1), (1, 0)])


def from_dp(block, mask):
    count = lax.axis_size("dp")
    return lax.ppermute(block, "dp", [(place, place ^ mask) for place in range(count)])


def from_dp_of(block, mask, side):
    count = lax.axis_size("dp")
    first = side * count
    route = [(first + place, first + (place ^ mask)) for place in range(count)]
    return lax.ppermute(block, ("section", "dp"), route)


def small_call(kernel, name, outs, *given):
    vmem = pl.BlockSpec(memory_space=pltpu.VMEM)
    size = sum(member.size * member.dtype.itemsize for member in given)
    return pl.pallas_call(
        kernel,
        in_specs=[vmem] * len(given),
        out_specs=[vmem] * len(outs),
        out_shape=[jax.ShapeDtypeStruct(shape, HALF) for shape in outs],
        compiler_params=pltpu.CompilerParams(vmem_limit_bytes=VMEM_BYTES),
        cost_estimate=pl.CostEstimate(flops=0, bytes_accessed=2 * size, transcendentals=0),
        name=name,
    )(*given)


def total_of(*values):
    total = values[0].astype(FULL)
    for value in values[1:]:
        total = total + value.astype(FULL)
    return low(total)


PLANE, DEPTH = (1, 2, 3), (4, 8, 12)


def groups_of(masks):
    count = lax.axis_size("dp")
    return [[place ^ mask for mask in (0,) + masks] for place in range(count) if place & masks[2] == 0]


def exchange(blocks, masks):
    return [blocks[0]] + [from_dp(block, mask) for block, mask in zip(blocks[1:], masks)]


def add_cores(name, batches):
    rows = sum(kept.shape[1] for kept, _ in batches)
    width = batches[0][0].shape[2]

    def kernel(*refs):
        outs = refs[-4:]
        for chunk in range(CHUNKS):
            start = 0
            for number in range(len(batches)):
                value = total_of(refs[2 * number][chunk], refs[2 * number + 1][chunk])
                outs[chunk % 4][chunk // 4, start : start + value.shape[0], :] = value
                start += value.shape[0]

    flat = [member for batch in batches for member in batch]
    return small_call(kernel, name + "_cores", [(CHUNKS // 4, rows, width)] * 4, *flat)


def exchange_whole(blocks, masks):
    return lax.all_to_all(
        blocks, "dp", split_axis=0, concat_axis=0, tiled=True, axis_index_groups=groups_of(masks)
    )


def split_cores(name, kept, got):
    half, width = kept.shape[1] // 2, kept.shape[2]

    def kernel(kept_ref, got_ref, *outs):
        for chunk in range(CHUNKS):
            deep, first, second = chunk // 4, chunk & 1, (chunk >> 1) & 1
            value = total_of(kept_ref[chunk], got_ref[chunk])
            outs[first][second, deep] = value[:half]
            outs[2 + second][first, deep] = value[half:]

    return small_call(kernel, name + "_cores", [(2, CHUNKS // 4, half, width)] * 4, kept, got)


def split_again(name, upper, lower):
    shape = upper[0].shape[1:]

    def kernel(*refs):
        for part in range(2):
            for side in range(2):
                refs[4 + 2 * part + side][...] = total_of(refs[2 * part][side], refs[2 * part + 1][side])

    return small_call(kernel, name + "_half", [shape] * 4, *upper, *lower)


def join_split(name, upper, lower, joined):
    half, rows = upper[0].shape[1], 2 * upper[0].shape[1]
    shape = (rows + joined.shape[1], joined.shape[2])

    def kernel(*refs):
        for place in range(4):
            out = refs[5 + place]
            out[:half, :] = total_of(refs[0][place], refs[1][place])
            out[half:rows, :] = total_of(refs[2][place], refs[3][place])
            out[rows:, :] = refs[4][place]

    return small_call(kernel, name + "_plane", [shape] * 4, *upper, *lower, joined)


def stack_plane(name, members):
    def kernel(*refs):
        for place in range(4):
            refs[-1][place] = total_of(*[ref[place] for ref in refs[:4]])

    return small_call(kernel, name + "_plane", [members[0].shape], *members)[0]


def add_stacked(name, members):
    def kernel(source, out):
        out[...] = total_of(*[source[place] for place in range(4)])

    return small_call(kernel, name + "_depth", [members.shape[1:]], members)[0]


def add_plane(name, members, joined=None, shared=None):
    rows = members[0].shape[1]
    middle = rows + (joined.shape[1] if joined is not None else 0)
    end = middle + (shared.shape[0] if shared is not None else 0)
    given = list(members) + [extra for extra in (joined, shared) if extra is not None]

    def kernel(*refs):
        for place in range(4):
            out = refs[-4 + place]
            out[:rows, :] = total_of(*[ref[place] for ref in refs[:4]])
            if middle > rows:
                out[rows:middle, :] = refs[4][place]
            if end > middle:
                out[middle:, :] = refs[len(given) - 1][...]

    return small_call(kernel, name + "_plane", [(end, members[0].shape[2])] * 4, *given)


def add_depth(name, members, rows=None):
    shape = (rows or members[0].shape[0], members[0].shape[1])

    def kernel(*refs):
        refs[-1][...] = total_of(*[ref[: shape[0], :] for ref in refs[:4]])

    return small_call(kernel, name + "_depth", [shape], *members)[0]


def add_far(chunk):
    bit = CHUNKS
    while bit < lax.axis_size("dp"):
        chunk = total_of(chunk, from_dp(chunk, bit))
        bit = 2 * bit
    return chunk


def gather_depth_for(chunk, side):
    own = jnp.stack([chunk, from_section(chunk)])
    return jnp.stack([own] + [from_dp_of(own, mask, side) for mask in DEPTH])


def gather_plane_for(deep, side):
    return [deep] + [from_dp_of(deep, mask, side) for mask in PLANE]


def join_cores(name, batches):
    rows = sum(kept.shape[1] for kept, _ in batches)
    width = batches[0][0].shape[2]

    def kernel(*refs):
        def step(chunk, carry):
            start = 0
            for number in range(len(batches)):
                value = total_of(refs[2 * number][chunk], refs[2 * number + 1][chunk])
                refs[-1][chunk, start : start + value.shape[0], :] = value
                start += value.shape[0]
            return carry

        lax.fori_loop(0, CHUNKS, step, 0, unroll=2)

    flat = [member for batch in batches for member in batch]
    return small_call(kernel, name + "_cores", [(CHUNKS, rows, width)], *flat)[0]


def scatter_group(blocks, masks):
    total = lax.psum_scatter(
        blocks.reshape(-1, blocks.shape[-1]),
        "dp",
        scatter_dimension=0,
        tiled=True,
        axis_index_groups=groups_of(masks),
    )
    return total.reshape(blocks.shape[1:])


def gather_group(block, masks):
    joined = lax.all_gather(
        block.reshape(-1, block.shape[-1]),
        "dp",
        axis=0,
        tiled=True,
        axis_index_groups=groups_of(masks),
    )
    return joined.reshape((4,) + block.shape)


def store_segments(outs, segments, block, piece, rows):
    for offset, size, target, column in segments:
        if offset < rows:
            place = pl.ds(pl.multiple_of(block * size, 16), size)
            values = piece[offset : offset + size, :]
            outs[target][place, column : column + values.shape[1]] = values.astype(FULL)


def unpack_kernel(feed_segments, attention_segments, segments, where, *refs):
    encoder, decoder, outs, small_out = refs[:4], refs[4:8], refs[8:-1], refs[-1]
    few = small_out.shape[1]
    rows = feed_segments[-1][0] + feed_segments[-1][1] + attention_segments[-1][0] + attention_segments[-1][1]
    attention_rows = rows - decoder[0].shape[2]

    @pl.when(where[0] == 0)
    def _():
        for flat in range(4):
            for side in range(2):
                block = 2 * jnp.bitwise_xor(flat, where[1] & 3) + side
                piece = encoder[flat].at[0, side]
                store_segments(outs, segments, block, piece, rows)
                small_out[block] = piece[rows : rows + 2 * few, :].astype(FULL)[:few]

    @pl.when(where[0] != 0)
    def _():
        for flat in range(4):
            for side in range(2):
                block = 2 * flat + jnp.bitwise_xor(where[0], side)
                piece = decoder[2 * side].at[flat, 0]
                store_segments(outs, feed_segments, block, piece, piece.shape[0])
                piece = decoder[2 * side + 1].at[flat, 0]
                store_segments(outs, attention_segments, block, piece, attention_rows)
                small_out[block] = piece[attention_rows : attention_rows + 2 * few, :].astype(FULL)[:few]


def after(value, *others):
    return lax.optimization_barrier((value, others))[0]


FEED = ["ln1_gain", "ln1_shift", "qkv_w", "out_w", "ln2_gain", "ln2_shift", "up_w", "up_shift", "down_w"]
ENDS = ["final_gain", "final_shift", "bridge"]


def picked(weights, names):
    return [weights[name] for name in names]


class Sizes:
    def __init__(self, width, hidden, groups, rows):
        self.groups, self.rows, self.width, self.hidden = groups, rows, width, hidden
        blocks = 2 * CHUNKS
        self.down_rows = self.hidden // blocks
        self.thin_rows = self.width // blocks
        self.up_parts = self.hidden // self.width
        self.feed_rows = self.down_rows + self.up_parts * self.thin_rows
        self.attention_rows = 4 * self.thin_rows
        self.small_rows = 16
        rows, width = self.rows, self.width
        self.qkv = Token((3 * PAIRS, rows, LANES), HALF)
        self.lse = Token((HEADS, rows), FULL)
        self.mixed = Token((PAIRS, rows, LANES), HALF)
        self.wide = Token((rows, width), FULL)
        self.wide_low = Token((rows, width), HALF)
        self.hidden_low = Token((rows, self.hidden), HALF)
        self.parked_qkv = Parked((3 * PAIRS, rows, LANES), HALF)
        self.parked_mixed = Parked((PAIRS, rows, LANES), HALF)
        self.parked_wide = Parked((rows, width), FULL)
        self.parked_hidden = Parked((rows, self.hidden), HALF)
        self.latent = Token((rows, LANES), FULL)
        self.latent_low = Token((rows, LANES), HALF)
        self.feed_blocks = Whole((CHUNKS, self.feed_rows, width), HALF)
        self.two_vectors = Whole((2, width), FULL)
        self.feed_vector = Whole((4 + self.up_parts, width), FULL)
        self.bridge = Whole((LANES, width), FULL)
        self.bias_scratch = pltpu.VMEM((rows, rows), FULL)
        self.lse_scratch = pltpu.VMEM((rows, LANES), FULL)
        self.wide_scratch = pltpu.VMEM((rows, width), FULL)
        self.low_scratch = pltpu.VMEM((rows, width), HALF)
        self.mixed_scratch = pltpu.VMEM((PAIRS, rows, LANES), HALF)
        self.qkv_scratch = pltpu.VMEM((3 * PAIRS, rows, LANES), HALF)
        self.hidden_scratch = pltpu.VMEM((rows, self.hidden), HALF)
        self.feed_sums = [
            pltpu.VMEM((self.hidden, width), FULL),
            pltpu.VMEM((width, self.hidden), FULL),
            pltpu.VMEM((1, self.hidden), FULL),
        ]
        self.qkv_sum = pltpu.VMEM((width, 3 * width), FULL)
        self.out_sum = pltpu.VMEM((width, width), FULL)
        self.small_sum = pltpu.VMEM((blocks, self.small_rows, width), FULL)

    def blocks(self, rows):
        return [Whole((CHUNKS, rows, self.width), HALF)] * 2


def encoder_mix(z, lengths, where, patch, weights):
    return run_groups(
        encoder_mix_kernel,
        "encoder_mix",
        z.groups,
        [lengths],
        [patch],
        picked(weights, FEED[:4]),
        [z.parked_qkv, z.lse, z.parked_mixed, z.wide],
        [z.bias_scratch, z.lse_scratch, z.low_scratch],
        10 << 30,
        24,
        where,
        0,
    )


def encoder_latent(z, where, middle, weights):
    return run_groups(
        encoder_latent_kernel,
        "encoder_latent",
        z.groups,
        [],
        [middle],
        picked(weights, FEED[4:] + ENDS),
        [z.parked_hidden, z.parked_hidden, z.parked_wide, z.latent],
        [z.low_scratch],
        12 << 30,
        30,
        where,
        0,
    )


def quantize(z, places, block, latent, pieces):
    count = z.groups * z.rows
    vmem = pl.BlockSpec(memory_space=pltpu.VMEM)
    rows = len(pieces) * pieces[0].shape[0]
    quant, book = pl.pallas_call(
        quant_kernel,
        in_specs=[pl.BlockSpec(memory_space=pltpu.SMEM), vmem, vmem]
        + [pl.BlockSpec(memory_space=pl.ANY)] * len(pieces),
        out_specs=[vmem, vmem],
        out_shape=[
            jax.ShapeDtypeStruct((count, LANES), HALF),
            jax.ShapeDtypeStruct((rows, LANES), FULL),
        ],
        scratch_shapes=[
            pltpu.VMEM((rows, LANES), FULL),
            pltpu.VMEM((count, LANES), FULL),
            pltpu.VMEM((count, LANES), FULL),
            pltpu.SemaphoreType.DMA((len(pieces),)),
        ]
        + [pltpu.VMEM((rows, LANES), FULL)] * 3,
        compiler_params=pltpu.CompilerParams(vmem_limit_bytes=VMEM_BYTES),
        cost_estimate=pl.CostEstimate(flops=8 << 30, bytes_accessed=0, transcendentals=0),
        name="quantize",
    )(places, block.reshape(count, 1), latent.reshape(count, LANES), *pieces)
    return quant.reshape(z.groups, z.rows, LANES), book


def decoder_mix(z, lengths, where, quant, weights):
    return run_groups(
        decoder_mix_kernel,
        "decoder_mix",
        z.groups,
        [lengths],
        [quant],
        picked(weights, FEED[:4] + ENDS[2:]),
        [z.parked_qkv, z.lse, z.parked_mixed, z.wide],
        [z.bias_scratch, z.lse_scratch, z.low_scratch, z.wide_scratch],
        10 << 30,
        26,
        where,
        1,
    )


def decoder_feed(z, where, middle, cotangent, weights):
    return run_groups(
        decoder_feed_kernel,
        "decoder_feed_both",
        z.groups,
        [where],
        [middle, cotangent],
        picked(weights, FEED[4:] + ENDS[:2]),
        [z.wide_low, z.parked_wide, z.feed_blocks, z.feed_blocks, z.feed_vector],
        [z.hidden_scratch, z.hidden_scratch, z.low_scratch, z.low_scratch, z.wide_scratch, z.wide_scratch]
        + z.feed_sums,
        28 << 30,
        36,
        where,
        1,
    )


def decoder_input(z, where, quant, grad_middle, grad_qkv, sums, weights, book, book_rows, latent, owners, per_owner):
    return run_groups(
        functools.partial(decoder_input_kernel, owners=owners, per_owner=per_owner, latent=latent),
        "decoder_input_backward",
        z.groups,
        [where],
        [quant, grad_middle, in_hbm(grad_qkv)],
        picked(weights, FEED[:3] + ENDS[2:]) + [book, in_hbm(sums[0]), sums[1]],
        [z.latent_low]
        + z.blocks(z.attention_rows + z.small_rows + book_rows)
        + [z.two_vectors, z.bridge],
        [z.qkv_sum, z.low_scratch, z.wide_scratch, z.wide_scratch, z.low_scratch, z.small_sum],
        8 << 30,
        28,
        where,
        1,
    )


def encoder_feed(z, where, grad_quant, middle, result, slope, active, weights):
    return run_groups(
        encoder_feed_kernel,
        "encoder_feed_backward",
        z.groups,
        [where],
        [grad_quant, middle, in_hbm(result), in_hbm(slope), in_hbm(active)],
        picked(weights, FEED[4:7] + FEED[8:] + ENDS),
        [z.parked_wide, z.feed_blocks, z.feed_blocks, z.feed_vector, z.bridge],
        [z.low_scratch, z.low_scratch, z.wide_scratch, z.wide_scratch] + z.feed_sums,
        20 << 30,
        36,
        where,
        0,
    )


def attention_gradient(z, name, side, lengths, where, grad_middle, saved, weights):
    return run_groups(
        attention_backward_kernel,
        name,
        z.groups,
        [lengths],
        [in_hbm(grad_middle), in_hbm(saved[0]), saved[1], in_hbm(saved[2])],
        picked(weights, ["out_w"]),
        [z.parked_qkv, ParkedWhole((z.width, z.width), FULL)],
        [z.bias_scratch, z.mixed_scratch],
        20 << 30,
        26,
        where,
        side,
    )


def encoder_input(z, where, patch, grad_middle, grad_qkv, sums, weights, latent):
    return run_groups(
        functools.partial(encoder_input_kernel, latent=latent),
        "encoder_input_backward",
        z.groups,
        [where],
        [in_hbm(patch), in_hbm(grad_middle), in_hbm(grad_qkv)],
        picked(weights, FEED[:3]) + [in_hbm(sums[0])] + sums[1:],
        [z.wide_low] + z.blocks(z.attention_rows + z.small_rows) + [z.two_vectors],
        [z.qkv_sum, z.low_scratch, z.wide_scratch, z.small_sum],
        8 << 30,
        24,
        where,
        0,
    )


def on_device(
    section_in,
    ln1_gain,
    ln1_shift,
    qkv_weight,
    out_weight,
    ln2_gain,
    ln2_shift,
    up_weight,
    up_shift,
    down_weight,
    final_gain,
    final_shift,
    bridge_weight,
    codebook,
    codes,
    doc_lengths,
):
    section = lax.axis_index("section")
    encoder_side = section == 0
    micro = doc_lengths.shape[0]
    groups = micro // 2
    rows = section_in.shape[1] // micro
    width = section_in.shape[2]
    hidden_width = up_weight.shape[2]
    latent_width = bridge_weight.shape[1]
    per_device = codebook.shape[1]

    count = lax.axis_size("dp")
    dp = lax.axis_index("dp")
    where = jnp.stack([section, dp & (CHUNKS - 1), dp >> (CHUNKS.bit_length() - 1)]).astype(jnp.int32)

    inverse = lax.rsqrt(jnp.sum(codebook * codebook, axis=0, keepdims=True) + EPS)
    unit_codes = codebook * inverse
    quarter = per_device // 4
    packed = (
        unit_codes.reshape(latent_width, 4, quarter).transpose(2, 1, 0).reshape(quarter, 4 * latent_width)
    )
    deep_table = [packed] + [from_dp(packed, mask) for mask in DEPTH]

    vectors = jnp.concatenate(
        [ln1_gain, ln1_shift, ln2_gain, ln2_shift, final_gain, final_shift]
        + [up_shift.reshape(-1, width), bridge_weight[0].astype(FULL)],
        axis=0,
    )
    qkv_w, out_w, up_w, down_w = qkv_weight[0], out_weight[0], up_weight[0], down_weight[0]
    halves = section_in[0].reshape(2, groups, rows, width)
    other_halves = from_section(section_in[0]).reshape(halves.shape)
    other_vectors, other_qkv, other_out = from_section(vectors), from_section(qkv_w), from_section(out_w)
    patch = jnp.where(encoder_side, halves[0], other_halves[1])
    cotangent = jnp.where(encoder_side, other_halves[0], halves[1])
    lengths = lax.dynamic_slice_in_dim(doc_lengths, section * groups, groups, 0)
    own_codes = lax.dynamic_slice_in_dim(codes, section * groups * rows, groups * rows, 0)
    owner, within = own_codes // per_device, own_codes % per_device
    apart = (owner % count) ^ dp
    place = ((owner // count) ^ section) * count + (apart & -CHUNKS) + 4 * (apart & 3) + ((apart >> 2) & 3)
    places = place * quarter + within % quarter
    code_block = within // quarter
    deep_table, patch, cotangent, other_vectors, other_qkv, other_out = lax.optimization_barrier(
        (deep_table, patch, cotangent, other_vectors, other_qkv, other_out)
    )
    hidden_rows = hidden_width // width

    def vectors_of(vector):
        return dict(
            ln1_gain=vector[0:1],
            ln1_shift=vector[1:2],
            qkv_w=(qkv_w, other_qkv),
            out_w=(out_w, other_out),
            ln2_gain=vector[2:3],
            ln2_shift=vector[3:4],
            up_shift=vector[6 : 6 + hidden_rows].reshape(1, hidden_width),
            final_gain=vector[4:5],
            final_shift=vector[5:6],
            bridge=jnp.pad(low(vector[6 + hidden_rows :]), ((0, LANES - latent_width), (0, 0))),
        )

    encoder = vectors_of(jnp.where(encoder_side, vectors, other_vectors))
    decoder = vectors_of(jnp.where(encoder_side, other_vectors, vectors))
    z = Sizes(width, hidden_width, groups, rows)
    deep_table = jnp.concatenate(deep_table, axis=0)
    table = [deep_table] + [from_dp(deep_table, mask) for mask in PLANE]
    other_up, other_down = from_section(up_w), from_section(down_w)
    encoded = encoder_mix(z, lengths, where, patch, encoder)
    table, other_up, other_down, encoded = lax.optimization_barrier((table, other_up, other_down, encoded))
    qkv_e, lse_e, mixed_e, middle_e = encoded
    encoder.update(up_w=(up_w, other_up), down_w=(down_w, other_down))
    decoder.update(up_w=(up_w, other_up), down_w=(down_w, other_down))
    bit = CHUNKS
    while bit < count:
        table = table + [from_dp(piece, bit) for piece in table]
        bit = 2 * bit
    table = table + [from_section(piece) for piece in table]
    encoded = encoder_latent(z, where, middle_e, encoder)
    table, encoded = lax.optimization_barrier((table, encoded))
    slope_e, active_e, result_e, latent = encoded
    quant, book = quantize(z, places, code_block, latent, table)
    feed_rows, attention_rows = z.feed_rows, z.attention_rows
    book_rows = 4 * latent_width * (lax.axis_size("dp") // CHUNKS) * quarter // width
    qkv_d, lse_d, mixed_d, middle = decoder_mix(z, lengths, where, quant, decoder)
    final, middle_d, keep_1, send_1, vectors_1 = decoder_feed(z, where, middle, cotangent, decoder)
    got_1 = from_section(send_1)
    decoder_mixed = attention_gradient(
        z, "decoder_attention_backward", 1, lengths, where, middle_d, (qkv_d, lse_d, mixed_d), decoder
    )
    got_1, decoder_mixed = lax.optimization_barrier((got_1, decoder_mixed))
    grad_qkv_d, out_sum_d = decoder_mixed
    plane_1 = add_cores("decoder_feed", [(keep_1, got_1)])
    moved_1 = exchange(plane_1, PLANE)
    grad_quant, keep_2, send_2, vectors_2, bridge_d = decoder_input(
        z,
        where,
        quant,
        middle_d,
        after(grad_qkv_d, plane_1[0]),
        [out_sum_d, vectors_1],
        decoder,
        book,
        book_rows,
        latent_width,
        lax.axis_size("dp"),
        quarter,
    )
    got_2 = from_section(send_2)
    middle_grad, keep_3, send_3, vectors_3, bridge_e = encoder_feed(
        z, where, grad_quant, middle_e, result_e, slope_e, active_e, encoder
    )
    moved_1, got_2, middle_grad, keep_3, send_3, vectors_3, bridge_e = lax.optimization_barrier(
        (moved_1, got_2, middle_grad, keep_3, send_3, vectors_3, bridge_e)
    )
    got_3 = from_section(send_3)
    depth_1 = stack_plane("decoder_feed", moved_1)
    joined_2 = join_cores("decoder_attention", [(keep_2, got_2)])
    depth_2 = scatter_group(joined_2.reshape((4, CHUNKS // 4) + joined_2.shape[1:]), PLANE)
    upper, upper_sent, lower, lower_sent = split_cores("encoder_feed", keep_3, got_3)

    middle_grad = after(middle_grad, upper, joined_2, depth_1)
    upper_got, lower_got = from_dp(upper_sent, 1), from_dp(lower_sent, 2)
    deep_1 = exchange_whole(depth_1, DEPTH)
    grad_qkv, out_sum = attention_gradient(
        z, "encoder_attention_backward", 0, lengths, where, middle_grad, (qkv_e, lse_e, mixed_e), encoder
    )
    upper_got, lower_got, deep_1, grad_qkv, out_sum = lax.optimization_barrier(
        (upper_got, lower_got, deep_1, grad_qkv, out_sum)
    )
    upper, upper_sent, lower, lower_sent = split_again("encoder_feed", (upper, upper_got), (lower, lower_got))
    upper_got, lower_got = from_dp(upper_sent, 2), from_dp(lower_sent, 1)
    chunk_1 = add_far(add_stacked("decoder_feed", deep_1))
    near_1 = exchange_whole(jnp.broadcast_to(chunk_1[None], (4,) + chunk_1.shape), DEPTH)
    grad_patch, keep_4, send_4, _ = encoder_input(
        z,
        where,
        patch,
        middle_grad,
        after(grad_qkv, chunk_1, upper),
        [out_sum, vectors_3, bridge_e],
        encoder,
        latent_width,
    )
    upper_got, lower_got, near_1, depth_2, grad_patch, keep_4, send_4 = lax.optimization_barrier(
        (upper_got, lower_got, near_1, depth_2, grad_patch, keep_4, send_4)
    )
    half_1 = gather_group(near_1, PLANE)

    got_4 = from_section(send_4)
    depth_3 = join_split("encoder_feed", (upper, upper_got), (lower, lower_got), depth_2)
    deep_3 = exchange(depth_3, DEPTH)
    plane_4 = add_cores("encoder_attention", [(keep_4, got_4)])
    moved_4 = exchange(plane_4, PLANE)
    deep_3, moved_4 = lax.optimization_barrier((deep_3, moved_4))
    chunk_3 = add_far(add_depth("encoder_feed", deep_3))
    used_rows = attention_rows + z.small_rows
    depth_4 = add_plane("encoder_attention", moved_4, shared=chunk_3[feed_rows : feed_rows + used_rows])
    deep_4 = lax.optimization_barrier(exchange(depth_4, DEPTH))
    chunk_4 = add_far(add_depth("encoder_attention", deep_4, used_rows))
    grad_patch = after(grad_patch, chunk_4)
    sent = jnp.where(encoder_side, final, grad_patch)
    kept = jnp.where(encoder_side, grad_patch, final)
    chunk_e = jnp.concatenate([chunk_3[:feed_rows], chunk_4], axis=0)
    deep_e = gather_depth_for(chunk_e, 0)
    near_2 = jnp.stack([piece[used_rows:] for piece in deep_4])
    half_1, near_2 = lax.optimization_barrier((half_1, near_2))
    half_2 = gather_group(near_2, PLANE)
    deep_e = lax.optimization_barrier(deep_e)
    got = from_section(sent)
    book_sum = chunk_3[feed_rows + attention_rows + z.small_rows :].astype(FULL)
    book_sum = book_sum.reshape(book_rows, 4, LANES).transpose(1, 0, 2).reshape(-1, quarter, LANES)
    book_own = lax.dynamic_index_in_dim(book_sum, lax.axis_index("dp") // CHUNKS, 0, keepdims=False)
    book_grad = (
        book_own.reshape(quarter, 4, latent_width).transpose(2, 1, 0).reshape(latent_width, per_device)
    )
    book_grad = inverse * (
        book_grad - unit_codes * jnp.sum(unit_codes * book_grad, axis=0, keepdims=True)
    )

    section_out = jnp.where(
        encoder_side, jnp.concatenate([kept, got], axis=0), jnp.concatenate([got, kept], axis=0)
    ).reshape(1, micro * rows, width)
    gathered = gather_plane_for(deep_e, 0)
    halves_d = [half_1, half_2]
    halves_d = halves_d + [lax.ppermute(half, "section", [(0, 1)]) for half in halves_d]

    feed_segments = [(0, z.down_rows, 0, 0)] + [
        (z.down_rows + part * z.thin_rows, z.thin_rows, 1, part * width) for part in range(z.up_parts)
    ]
    attention_segments = [(0, z.thin_rows, 3, 0)] + [
        ((part + 1) * z.thin_rows, z.thin_rows, 2, part * width) for part in range(3)
    ]
    segments = feed_segments + [
        (feed_rows + offset, size, target, column) for offset, size, target, column in attention_segments
    ]
    gathered, section_out, book_grad = lax.optimization_barrier((gathered, section_out, book_grad))
    given = gathered + list(halves_d)
    vmem = pl.BlockSpec(memory_space=pltpu.VMEM)
    shapes = [(hidden_width, width), (width, hidden_width), (width, 3 * width), (width, width)]
    shapes.append((2 * CHUNKS, z.small_rows // 2, width))

    def part_of(shape):
        rest = (0,) * (len(shape) - 1)
        return pl.BlockSpec((shape[0] // 4,) + shape[1:], lambda depth, place: (depth,) + rest)

    def near(depth, place, side):
        return jnp.where(place[0] == side, jnp.bitwise_xor(depth, place[1] >> 2), 0)

    def same(depth, place, side):
        return jnp.where(place[0] == side, depth, 0)

    def deep_part(array):
        return pl.BlockSpec((1,) + array.shape[1:], lambda depth, place: (near(depth, place, 0), 0, 0, 0))

    def half_part(array, index):
        shape = (array.shape[0], 1) + array.shape[2:]
        return pl.BlockSpec(shape, lambda depth, place: (0, index(depth, place, 1), 0, 0))

    in_specs = [deep_part(piece) for piece in given[:4]]
    in_specs += [half_part(half, index) for half, index in zip(given[4:], (same, near, same, near))]
    down_total, up_total, qkv_total, out_total, small = pl.pallas_call(
        functools.partial(unpack_kernel, feed_segments, attention_segments, segments),
        grid_spec=pltpu.PrefetchScalarGridSpec(
            num_scalar_prefetch=1,
            grid=(4,),
            in_specs=in_specs,
            out_specs=[part_of(shape) for shape in shapes],
        ),
        out_shape=[jax.ShapeDtypeStruct(shape, FULL) for shape in shapes],
        compiler_params=pltpu.CompilerParams(vmem_limit_bytes=30 << 20),
        name="unpack",
    )(where, *given)

    small_count = 2 + 4 + z.up_parts + latent_width
    small = small[:, : -(-small_count // (2 * CHUNKS))].reshape(-1, width)

    first_vector = 2
    hidden_vector = first_vector + 4
    return (
        section_out,
        small[0:1],
        small[1:2],
        qkv_total[None],
        out_total[None],
        small[2:3],
        small[3:4],
        up_total[None],
        small[hidden_vector : hidden_vector + z.up_parts].reshape(1, hidden_width),
        down_total[None],
        small[4:5],
        small[5:6],
        small[hidden_vector + z.up_parts : hidden_vector + z.up_parts + latent_width][None],
        book_grad,
    )


def solution(mesh):
    placed = (
        P("section", "dp", None),
        P("section", None),
        P("section", None),
        P("section", None, None),
        P("section", None, None),
        P("section", None),
        P("section", None),
        P("section", None, None),
        P("section", None),
        P("section", None, None),
        P("section", None),
        P("section", None),
        P("section", None, None),
        P(None, ("section", "dp")),
        P("dp"),
        P("dp", None),
    )
    return jax.shard_map(
        on_device,
        mesh=mesh,
        in_specs=placed,
        out_specs=(
            P("section", "dp", None),
            P("section", None),
            P("section", None),
            P("section", None, None),
            P("section", None, None),
            P("section", None),
            P("section", None),
            P("section", None, None),
            P("section", None),
            P("section", None, None),
            P("section", None),
            P("section", None),
            P("section", None, None),
            P(None, ("section", "dp")),
        ),
        check_vma=False,
    )
```

```python
import functools

import jax
import jax.numpy as jnp
from jax import lax
from jax.experimental import pallas as pl
from jax.experimental.pallas import tpu as pltpu
from jax.sharding import PartitionSpec as P

HEADS = 8
PAIRS = HEADS // 2
LANES = 128
EPS = 1e-06
GELU_FACTOR = 0.7978845608028654
GELU_CUBIC = 0.044715
BLOCKED = -1000000000.0
CHUNKS = 16
FULL = jnp.float32
HALF = jnp.bfloat16
VMEM_BYTES = 12 * 1024 * 1024


def low(value):
    return value.astype(HALF)


def mm(left, right):
    return lax.dot_general(left, right, (((1,), (0,)), ((), ())), preferred_element_type=FULL)


def mm_nt(left, right):
    return lax.dot_general(left, right, (((1,), (1,)), ((), ())), preferred_element_type=FULL)


def mm_tn(left, right):
    return lax.dot_general(left, right, (((0,), (0,)), ((), ())), preferred_element_type=FULL)


def norm_forward(inputs, gain, shift):
    centred = inputs - jnp.mean(inputs, axis=-1, keepdims=True)
    scaling = lax.rsqrt(jnp.mean(centred * centred, axis=-1, keepdims=True) + EPS)
    normal = centred * scaling
    return normal * gain + shift, normal, scaling


def row_chunks(rows, size=64):
    return [slice(start, start + size) for start in range(0, rows, size)]


def norm_rows(source, target, gain, shift):
    for part in row_chunks(source.shape[0]):
        target[part, :] = low(norm_forward(source[part, :].astype(FULL), gain[...], shift[...])[0])


def write_bias(lengths_ref, group, bias_ref):
    rows = bias_ref.shape[0]
    down = lax.broadcasted_iota(jnp.int32, (rows, rows), 0)
    across = lax.broadcasted_iota(jnp.int32, (rows, rows), 1)
    row_label = jnp.zeros((rows, rows), jnp.int32)
    column_label = jnp.zeros((rows, rows), jnp.int32)
    bound = jnp.int32(0)
    for doc in range(lengths_ref.shape[1]):
        bound = bound + lengths_ref[group, doc]
        row_label = row_label + (down >= bound).astype(jnp.int32)
        column_label = column_label + (across >= bound).astype(jnp.int32)
    bias_ref[...] = jnp.where(row_label == column_label, 0.0, BLOCKED)


def half_mask(rows, side):
    lane = lax.broadcasted_iota(jnp.int32, (rows, LANES), 1)
    return lane < LANES // 2 if side == 0 else lane >= LANES // 2


def attention_forward(qkv_ref, bias_ref, mixed_ref, lse_ref, lse_scratch):
    rows = qkv_ref.shape[1]
    scale = (LANES // 2) ** (-0.5)
    lane = lax.broadcasted_iota(jnp.int32, (rows, LANES), 1)
    lse_scratch[...] = jnp.zeros_like(lse_scratch)

    def pair_step(pair, carry):
        queries = qkv_ref[pair] * jnp.asarray(scale, HALF)
        keys = qkv_ref[PAIRS + pair]
        values = qkv_ref[2 * PAIRS + pair]
        mixed = jnp.zeros((rows, LANES), FULL)
        for side in range(2):
            inside = half_mask(rows, side)
            zero = jnp.zeros((), HALF)
            scores = mm_nt(jnp.where(inside, queries, zero), keys) + bias_ref[...]
            peak = jnp.max(scores, axis=-1, keepdims=True)
            weight = jnp.exp(scores - peak)
            total = jnp.sum(weight, axis=-1, keepdims=True)
            part = mm(low(weight), jnp.where(inside, values, zero))
            mixed = mixed + part * (1.0 / total)
            log_total = peak + jnp.log(total)
            lse_scratch[...] = jnp.where(lane == 2 * pair + side, log_total, lse_scratch[...])
        mixed_ref[pair] = low(mixed)
        return carry

    lax.fori_loop(0, PAIRS, pair_step, 0, unroll=4)
    lse_ref[...] = jnp.transpose(lse_scratch[...])[:HEADS]


def heads_joined(mixed_ref):
    return jnp.concatenate([mixed_ref[pair] for pair in range(PAIRS)], axis=1)


def mix_forward(
    source, weights, bias_ref, qkv_ref, mixed_ref, lse_ref, lse_scratch, normed_ref, middle_ref
):
    ln1_gain, ln1_shift, qkv_w, out_w = weights
    width = source.shape[1]
    norm_rows(source, normed_ref, ln1_gain, ln1_shift)
    for part in range(3):
        projected = low(mm(normed_ref[...], qkv_w[:, part * width : (part + 1) * width]))
        for pair in range(PAIRS):
            qkv_ref[part * PAIRS + pair] = projected[:, pair * LANES : (pair + 1) * LANES]
    attention_forward(qkv_ref, bias_ref, mixed_ref, lse_ref, lse_scratch)
    middle_ref[...] = source[...].astype(FULL) + mm(heads_joined(mixed_ref), out_w[...])


def feed_forward(middle_ref, weights, normed_ref, slope_ref, active_ref, total_ref):
    ln2_gain, ln2_shift, up_w, up_shift, down_w = weights
    hidden_width = up_w.shape[1]
    norm_rows(middle_ref, normed_ref, ln2_gain, ln2_shift)
    tile = middle_ref.shape[1]
    for step in range(hidden_width // tile):
        place = slice(step * tile, (step + 1) * tile)
        hidden = mm(normed_ref[...], up_w[:, place]) + up_shift[:, place]
        square = hidden * hidden
        tangent = jnp.tanh(hidden * ((GELU_FACTOR * GELU_CUBIC) * square + GELU_FACTOR))
        gate = 0.5 * tangent + 0.5
        active = low(hidden * gate)
        bend = hidden * ((1.5 * GELU_FACTOR * GELU_CUBIC) * square + 0.5 * GELU_FACTOR)
        active_ref[:, place] = active
        slope_ref[:, place] = low(gate + bend * (1.0 - tangent * tangent))
        before = middle_ref[...] if step == 0 else total_ref[...]
        total_ref[...] = before + mm(active, down_w[place, :])


def feed_backward(
    upstream_ref,
    middle_ref,
    weights,
    slope_ref,
    active_ref,
    normed_ref,
    branch_ref,
    total_ref,
    down_out,
    up_out,
    up_shift_out,
    grad_middle_ref,
    vector_out,
):
    ln2_gain, ln2_shift, up_w, down_w = weights
    width = upstream_ref.shape[1]
    hidden_width = up_w.shape[1]
    norm_rows(middle_ref, normed_ref, ln2_gain, ln2_shift)
    tile = width

    def hidden_step(step, carry):
        place = pl.ds(step * tile, tile)
        branch = branch_ref[...]
        down_out[place, :] = down_out[place, :] + mm_tn(active_ref[:, place], branch)
        grad_hidden = mm_nt(branch, down_w[place, :]) * slope_ref[:, place].astype(FULL)
        up_shift_out[:, place] = up_shift_out[:, place] + jnp.sum(grad_hidden, axis=0, keepdims=True)
        grad_low = low(grad_hidden)
        up_out[:, place] = up_out[:, place] + mm_tn(normed_ref[...], grad_low)
        share = mm_nt(grad_low, up_w[:, place])
        total_ref[...] = share if step == 0 else total_ref[...] + share
        return carry

    for step in range(hidden_width // tile):
        hidden_step(step, 0)
    norm_backward_rows(
        total_ref, middle_ref, ln2_gain, ln2_shift, vector_out, 0, upstream_ref, grad_middle_ref
    )


def norm_backward_rows(grad_ref, source, gain, shift, vector_out, row, added_ref, *targets):
    width = source.shape[1]
    grad_gain = jnp.zeros((8, width), FULL)
    grad_shift = jnp.zeros((8, width), FULL)
    for part in row_chunks(source.shape[0]):
        _, normal, scaling = norm_forward(source[part, :].astype(FULL), gain[...], shift[...])
        upstream = grad_ref[part, :].astype(FULL)
        scaled = upstream * gain[...]
        inner = scaled - jnp.mean(scaled, axis=-1, keepdims=True)
        inner = inner - normal * jnp.mean(scaled * normal, axis=-1, keepdims=True)
        grad = scaling * inner
        if added_ref is not None:
            grad = grad + added_ref[part, :]
        for target in targets:
            target[part, :] = grad.astype(target.dtype)
        folded = (upstream.shape[0] // 8, 8, width)
        grad_gain = grad_gain + jnp.sum((upstream * normal).reshape(folded), axis=0)
        grad_shift = grad_shift + jnp.sum(upstream.reshape(folded), axis=0)
    add_row(vector_out, row, jnp.sum(grad_gain, axis=0, keepdims=True))
    add_row(vector_out, row + 1, jnp.sum(grad_shift, axis=0, keepdims=True))


def attention_backward(qkv_ref, grad_mixed_ref, bias_ref, lse_ref, grad_qkv_ref):
    rows = qkv_ref.shape[1]
    scale = (LANES // 2) ** (-0.5)

    def pair_step(pair, carry):
        queries = qkv_ref[pair] * jnp.asarray(scale, HALF)
        keys = qkv_ref[PAIRS + pair]
        values = qkv_ref[2 * PAIRS + pair]
        grads = grad_mixed_ref[pair]
        grad_queries = jnp.zeros((rows, LANES), FULL)
        grad_keys = jnp.zeros((rows, LANES), FULL)
        grad_values = jnp.zeros((rows, LANES), FULL)
        for side in range(2):
            inside = half_mask(rows, side)
            zero = jnp.zeros((), HALF)
            side_queries = jnp.where(inside, queries, zero)
            side_grads = jnp.where(inside, grads, zero)
            scores = mm_nt(keys, side_queries) + bias_ref[...]
            attention = jnp.exp(scores - lse_ref[pl.ds(2 * pair + side, 1), :])
            grad_values = grad_values + mm(low(attention), side_grads)
            grad_attention = mm_nt(values, side_grads)
            delta = jnp.sum(attention * grad_attention, axis=0, keepdims=True)
            grad_scores = low(attention * (grad_attention - delta))
            grad_keys = grad_keys + mm(grad_scores, side_queries)
            grad_queries = grad_queries + mm_tn(grad_scores, jnp.where(inside, keys, zero))
        grad_qkv_ref[pair] = low(grad_queries * scale)
        grad_qkv_ref[PAIRS + pair] = low(grad_keys)
        grad_qkv_ref[2 * PAIRS + pair] = low(grad_values)
        return carry

    lax.fori_loop(0, PAIRS, pair_step, 0, unroll=4)


def attention_gradients(
    grad_middle, out_w, bias_ref, qkv_ref, mixed_ref, lse_ref, grad_mixed_ref, grad_qkv_ref, out_out
):
    grad_low = low(grad_middle)
    out_out[...] = out_out[...] + mm_tn(heads_joined(mixed_ref), grad_low)
    grad_mixed = low(mm_nt(grad_low, out_w[...]))
    for pair in range(PAIRS):
        grad_mixed_ref[pair] = grad_mixed[:, pair * LANES : (pair + 1) * LANES]
    attention_backward(qkv_ref, grad_mixed_ref, bias_ref, lse_ref, grad_qkv_ref)


def projection_gradients(
    source, grad_middle_ref, ln1_gain, ln1_shift, qkv_w, grad_qkv_ref, qkv_out, normed_ref, total_ref, vector_out, target
):
    width = source.shape[1]
    norm_rows(source, normed_ref, ln1_gain, ln1_shift)
    for part in range(3):
        grad_part = jnp.concatenate(
            [grad_qkv_ref[part * PAIRS + pair] for pair in range(PAIRS)], axis=1
        )
        place = slice(part * width, (part + 1) * width)
        qkv_out[:, place] = qkv_out[:, place] + mm_tn(normed_ref[...], grad_part)
        share = mm_nt(grad_part, qkv_w[:, place])
        total_ref[...] = share if part == 0 else total_ref[...] + share
    norm_backward_rows(total_ref, source, ln1_gain, ln1_shift, vector_out, 0, grad_middle_ref, target)


def unit_rows(rows):
    inverse = lax.rsqrt(jnp.sum(rows * rows, axis=-1, keepdims=True) + EPS)
    return rows * inverse, inverse


def start_totals(*refs):
    @pl.when(pl.program_id(0) == 0)
    def _():
        for ref in refs:
            ref[...] = jnp.zeros_like(ref)


def encoder_mix_kernel(
    lengths,
    patch,
    ln1_gain,
    ln1_shift,
    qkv_w,
    out_w,
    qkv_ref,
    lse_ref,
    mixed_ref,
    middle_ref,
    bias_ref,
    lse_scratch,
    normed_ref,
):
    write_bias(lengths, pl.program_id(0), bias_ref)
    mix_forward(
        patch,
        (ln1_gain, ln1_shift, qkv_w, out_w),
        bias_ref,
        qkv_ref,
        mixed_ref,
        lse_ref,
        lse_scratch,
        normed_ref,
        middle_ref,
    )


def encoder_latent_kernel(
    middle,
    ln2_gain,
    ln2_shift,
    up_w,
    up_shift,
    down_w,
    final_gain,
    final_shift,
    bridge,
    slope_ref,
    active_ref,
    result_ref,
    latent_ref,
    normed_ref,
):
    weights = (ln2_gain, ln2_shift, up_w, up_shift, down_w)
    feed_forward(middle, weights, normed_ref, slope_ref, active_ref, result_ref)
    norm_rows(result_ref, normed_ref, final_gain, final_shift)
    latent_ref[...] = unit_rows(mm_nt(normed_ref[...], bridge[...]))[0]


def quant_kernel(places, block_column, latent, *refs):
    pieces, (quant_ref, book_ref, table, gathered, spread, semaphore) = refs[:-9], refs[-9:-3]
    books = (book_ref,) + refs[-3:]
    count = gathered.shape[0]
    size = pieces[0].shape[0]
    copies = [
        pltpu.make_async_copy(piece, table.at[pl.ds(number * size, size)], semaphore.at[number])
        for number, piece in enumerate(pieces)
    ]
    for copy in copies:
        copy.start()
    for copy in copies:
        copy.wait()

    def gather(index, carry):
        gathered[pl.ds(index, 1), :] = table[pl.ds(places[index], 1), :]
        return carry

    lax.fori_loop(0, count, gather, 0, unroll=16)
    block = block_column[...]
    lane = lax.broadcasted_iota(jnp.int32, (count, LANES), 1)
    width = LANES // 4
    rows = gathered[...]
    code = jnp.where(block == 0, rows, 0.0)
    for place in range(1, 4):
        code = code + jnp.where(block == place, pltpu.roll(rows, LANES - width * place, 1), 0.0)
    code = jnp.where(lane < width, code, 0.0)
    held = latent[...]
    quant_ref[...] = low(held + (code - held))
    grad = 2.0 * (code - held)
    placed = jnp.where(block == 0, grad, 0.0)
    for place in range(1, 4):
        placed = placed + jnp.where(block == place, pltpu.roll(grad, width * place, 1), 0.0)
    spread[...] = placed
    for book in books:
        book[...] = jnp.zeros_like(book)
    part = count // len(books)

    def scatter(index, carry):
        for number, book in enumerate(books):
            row = number * part + index
            place = pl.ds(places[row], 1)
            book[place, :] = book[place, :] + spread[pl.ds(row, 1), :]
        return carry

    lax.fori_loop(0, part, scatter, 0, unroll=4)
    book_ref[...] = (books[0][...] + books[1][...]) + (books[2][...] + books[3][...])


def add_row(ref, row, value):
    ref[row : row + 1, :] = ref[row : row + 1, :] + value


def feed_vectors(vector_out, up_shift_acc):
    width = vector_out.shape[1]
    for part in range(up_shift_acc.shape[1] // width):
        vector_out[4 + part : 5 + part, :] = up_shift_acc[:, part * width : (part + 1) * width]


def last_group():
    return pl.program_id(0) == pl.num_programs(0) - 1


def decoder_mix_kernel(
    lengths,
    quant,
    ln1_gain,
    ln1_shift,
    qkv_w,
    out_w,
    bridge,
    qkv_ref,
    lse_ref,
    mixed_ref,
    middle_ref,
    bias_ref,
    lse_scratch,
    normed_ref,
    source_ref,
):
    write_bias(lengths, pl.program_id(0), bias_ref)
    source_ref[...] = mm(quant[...], bridge[...])
    mix_forward(
        source_ref,
        (ln1_gain, ln1_shift, qkv_w, out_w),
        bias_ref,
        qkv_ref,
        mixed_ref,
        lse_ref,
        lse_scratch,
        normed_ref,
        middle_ref,
    )


def decoder_feed_kernel(
    where,
    middle_ref,
    cotangent,
    ln2_gain,
    ln2_shift,
    up_w,
    up_shift,
    down_w,
    final_gain,
    final_shift,
    final_ref,
    grad_middle_ref,
    keep_ref,
    send_ref,
    vector_out,
    slope_ref,
    active_ref,
    normed_ref,
    branch_ref,
    result_ref,
    upstream_ref,
    down_acc,
    up_acc,
    up_shift_acc,
):
    start_totals(down_acc, up_acc, up_shift_acc, vector_out)
    weights = (ln2_gain, ln2_shift, up_w, up_shift, down_w)
    feed_forward(middle_ref, weights, normed_ref, slope_ref, active_ref, result_ref)
    norm_rows(result_ref, final_ref, final_gain, final_shift)
    norm_backward_rows(
        cotangent, result_ref, final_gain, final_shift, vector_out, 2, None, upstream_ref, branch_ref
    )
    feed_backward(
        upstream_ref,
        middle_ref,
        (ln2_gain, ln2_shift, up_w, down_w),
        slope_ref,
        active_ref,
        normed_ref,
        branch_ref,
        result_ref,
        down_acc,
        up_acc,
        up_shift_acc,
        grad_middle_ref,
        vector_out,
    )

    @pl.when(last_group())
    def _():
        feed_vectors(vector_out, up_shift_acc)
        pieces = [rows_of(down_acc)] + column_parts(up_acc, middle_ref.shape[1])
        store_blocks(where, keep_ref, send_ref, pieces, order="deep")


def decoder_input_kernel(
    where,
    quant,
    grad_middle,
    grad_qkv_ref,
    ln1_gain,
    ln1_shift,
    qkv_w,
    bridge,
    book,
    out_sum,
    feed_vector,
    grad_quant_ref,
    keep_ref,
    send_ref,
    vector_out,
    bridge_out,
    qkv_acc,
    normed_ref,
    source_ref,
    total_ref,
    grad_lift_ref,
    small_ref,
    *,
    owners,
    per_owner,
    latent,
):
    start_totals(qkv_acc, vector_out, bridge_out)
    source_ref[...] = mm(quant[...], bridge[...])
    projection_gradients(
        source_ref,
        grad_middle,
        ln1_gain,
        ln1_shift,
        qkv_w,
        grad_qkv_ref,
        qkv_acc,
        normed_ref,
        total_ref,
        vector_out,
        grad_lift_ref,
    )
    bridge_out[...] = bridge_out[...] + mm_tn(quant[...], grad_lift_ref[...])
    grad_quant_ref[...] = low(mm_nt(grad_lift_ref[...], bridge[...]))

    @pl.when(last_group())
    def _():
        pieces = [rows_of(out_sum)] + column_parts(qkv_acc, source_ref.shape[1])
        spread_rows(small_ref, (vector_out, 2), (feed_vector, feed_vector.shape[0]), (bridge_out, latent))
        pieces = pieces + [lambda block: small_ref[block], codebook_rows(where, book, per_owner, owners)]
        store_blocks(where, keep_ref, send_ref, pieces, order="flat")


def encoder_feed_kernel(
    where,
    grad_quant,
    middle,
    result,
    slope_ref,
    active_ref,
    ln2_gain,
    ln2_shift,
    up_w,
    down_w,
    final_gain,
    final_shift,
    bridge,
    grad_middle_ref,
    keep_ref,
    send_ref,
    vector_out,
    bridge_out,
    normed_ref,
    branch_ref,
    grad_ref,
    upstream_ref,
    down_acc,
    up_acc,
    up_shift_acc,
):
    start_totals(down_acc, up_acc, up_shift_acc, vector_out, bridge_out)
    norm_rows(result, normed_ref, final_gain, final_shift)
    feature = normed_ref[...]
    latent, inverse = unit_rows(mm_nt(feature, bridge[...]))
    grad_latent = grad_quant[...].astype(FULL)
    grad_projection = low(
        inverse * (grad_latent - latent * jnp.sum(latent * grad_latent, axis=1, keepdims=True))
    )
    bridge_out[...] = bridge_out[...] + mm_tn(grad_projection, feature)
    grad_ref[...] = mm(grad_projection, bridge[...])
    norm_backward_rows(
        grad_ref, result, final_gain, final_shift, vector_out, 2, None, upstream_ref, branch_ref
    )
    feed_backward(
        upstream_ref,
        middle,
        (ln2_gain, ln2_shift, up_w, down_w),
        slope_ref,
        active_ref,
        normed_ref,
        branch_ref,
        grad_ref,
        down_acc,
        up_acc,
        up_shift_acc,
        grad_middle_ref,
        vector_out,
    )

    @pl.when(last_group())
    def _():
        feed_vectors(vector_out, up_shift_acc)
        pieces = [rows_of(down_acc)] + column_parts(up_acc, middle.shape[1])
        store_blocks(where, keep_ref, send_ref, pieces)


def attention_backward_kernel(
    lengths,
    grad_middle,
    qkv_ref,
    lse_ref,
    mixed_ref,
    out_w,
    grad_qkv_ref,
    out_acc,
    bias_ref,
    grad_mixed_ref,
):
    start_totals(out_acc)
    write_bias(lengths, pl.program_id(0), bias_ref)
    attention_gradients(
        grad_middle[...], out_w, bias_ref, qkv_ref, mixed_ref, lse_ref, grad_mixed_ref, grad_qkv_ref, out_acc
    )


def encoder_input_kernel(
    where,
    patch,
    grad_middle,
    grad_qkv_ref,
    ln1_gain,
    ln1_shift,
    qkv_w,
    out_sum,
    feed_vector,
    bridge_sum,
    grad_patch_ref,
    keep_ref,
    send_ref,
    vector_out,
    qkv_acc,
    normed_ref,
    total_ref,
    small_ref,
    *,
    latent,
):
    start_totals(qkv_acc, vector_out)
    projection_gradients(
        patch,
        grad_middle,
        ln1_gain,
        ln1_shift,
        qkv_w,
        grad_qkv_ref,
        qkv_acc,
        normed_ref,
        total_ref,
        vector_out,
        grad_patch_ref,
    )

    @pl.when(last_group())
    def _():
        spread_rows(small_ref, (vector_out, 2), (feed_vector, feed_vector.shape[0]), (bridge_sum, latent))
        pieces = [rows_of(out_sum)] + column_parts(qkv_acc, patch.shape[1])
        store_blocks(where, keep_ref, send_ref, pieces + [lambda block: small_ref[block]])


def store_blocks(where, keep_ref, send_ref, pieces, order="relative"):
    def step(index, carry):
        if order == "relative":
            chunk = jnp.bitwise_xor(index, where[1])
        elif order == "deep":
            chunk = jnp.bitwise_xor(index, where[1] & 3)
        else:
            chunk = 4 * jnp.bitwise_xor(index & 3, where[1] >> 2) + (index >> 2)
        for side, ref in ((0, keep_ref), (1, send_ref)):
            block = 2 * chunk + jnp.bitwise_xor(where[0], side)
            offset = 0
            for piece in pieces:
                values = piece(block)
                count = values.shape[0]
                ref[index, offset : offset + count, :] = low(values)
                offset += count
        return carry

    lax.fori_loop(0, CHUNKS, step, 0)


def rows_of(ref, part=None):
    count = ref.shape[0] // (2 * CHUNKS)

    def piece(block):
        place = pl.ds(pl.multiple_of(block * count, count), count)
        if part is None:
            return ref[place, :]
        return ref[place, part]

    return piece


def column_parts(ref, width):
    return [rows_of(ref, slice(start, start + width)) for start in range(0, ref.shape[1], width)]


def codebook_rows(where, book_ref, per_owner, owners):
    def piece(block):
        side = jnp.bitwise_xor(block & 1, where[0])
        chunk = jnp.bitwise_xor(block >> 1, where[1])
        near = 4 * (chunk & 3) + (chunk >> 2)
        rows = []
        for high in range(owners // CHUNKS):
            far = jnp.bitwise_xor(high, where[2]) if owners > CHUNKS else 0
            owner = side * owners + far * CHUNKS + near
            rows.append(book_ref[pl.ds(pl.multiple_of(owner * per_owner, per_owner), per_owner), :])
        joined = jnp.concatenate(rows, axis=0) if len(rows) > 1 else rows[0]
        count = joined.shape[0] // 4
        return jnp.concatenate([joined[part * count : (part + 1) * count] for part in range(4)], axis=1)

    return piece


def spread_rows(target, *sources):
    target[...] = jnp.zeros_like(target)
    rows = [(ref, row) for ref, count in sources for row in range(count)]
    each = -(-len(rows) // target.shape[0])
    for number, (ref, row) in enumerate(rows):
        block, place = number // each, number % each
        target[block, place : place + 1, :] = ref[row : row + 1, :]


class Token:
    def __init__(self, shape, dtype):
        self.shape, self.dtype = shape, dtype

    def struct(self, groups):
        return jax.ShapeDtypeStruct((groups,) + self.shape, self.dtype)


    def spec(self):
        tail = (0,) * len(self.shape)
        return pl.BlockSpec((None,) + self.shape, lambda group: (group,) + tail)


class Parked(Token):
    def struct(self, groups):
        return pltpu.HBM((groups,) + self.shape, self.dtype)


class Whole:
    def __init__(self, shape, dtype):
        self.shape, self.dtype = shape, dtype

    def struct(self, groups):
        return jax.ShapeDtypeStruct(self.shape, self.dtype)

    def spec(self):
        zeros = (0,) * len(self.shape)
        return pl.BlockSpec(self.shape, lambda group: zeros, pipeline_mode=pl.Buffered(1))


class ParkedWhole(Whole):
    def struct(self, groups):
        return pltpu.HBM(self.shape, self.dtype)


class Loaded:
    def __init__(self, where, side, own, other, held, semaphore):
        self.shape = held.shape
        self.copies = [pltpu.make_async_copy(source, held, semaphore) for source in (own, other)]
        self.where, self.side, self.held, self.waited = where, side, held, False

    def start(self):
        @pl.when(self.where[0] == self.side)
        def _():
            self.copies[0].start()

        @pl.when(self.where[0] != self.side)
        def _():
            self.copies[1].start()

    def __getitem__(self, place):
        if not self.waited:
            self.waited = True

            @pl.when(pl.program_id(0) == 0)
            def _():
                self.copies[0].wait()

        return self.held[place]


def run_groups(
    kernel, name, groups, scalars, tokens, wholes, outs, scratch, flops, vmem, where=None, side=None
):
    in_place = pl.BlockSpec(memory_space=pltpu.HBM)
    pairs = [member for member in wholes if isinstance(member, tuple)]
    if pairs:
        scalars = [where] + list(scalars)
    specs = [pl.BlockSpec(memory_space=pltpu.SMEM)] * len(scalars)
    specs += [Token(array.shape[1:], array.dtype).spec() for array in tokens]
    given = list(scalars) + list(tokens)
    for member in wholes:
        if isinstance(member, tuple):
            specs += [in_place] * 2
            given += [in_hbm(member[0]), member[1]]
        else:
            specs.append(Whole(member.shape, member.dtype).spec())
            given.append(member)
    held = [pltpu.VMEM(own.shape, own.dtype) for own, _ in pairs]
    semaphores = [pltpu.SemaphoreType.DMA((len(pairs),))] if pairs else []

    def body(*refs):
        if not pairs:
            return kernel(*refs)
        place, refs = refs[0], list(refs[1:])
        semaphore, refs = refs[-1], refs[:-1]
        holders, refs = refs[len(refs) - len(pairs) :], refs[: len(refs) - len(pairs)]
        first = len(scalars) - 1 + len(tokens)
        arguments, rest = refs[:first], refs[first:]
        weights = []
        for member in wholes:
            if isinstance(member, tuple):
                number = len(weights)
                weights.append(
                    Loaded(place, side, rest[0], rest[1], holders[number], semaphore.at[number])
                )
                arguments.append(weights[-1])
                rest = rest[2:]
            else:
                arguments.append(rest[0])
                rest = rest[1:]

        @pl.when(pl.program_id(0) == 0)
        def _():
            for weight in weights:
                weight.start()

        return kernel(*arguments, *rest)

    return pl.pallas_call(
        body,
        grid=(groups,),
        in_specs=specs,
        out_specs=[out.spec() for out in outs],
        out_shape=[out.struct(groups) for out in outs],
        scratch_shapes=list(scratch) + held + semaphores,
        compiler_params=pltpu.CompilerParams(vmem_limit_bytes=vmem << 20),
        cost_estimate=pl.CostEstimate(flops=flops, bytes_accessed=0, transcendentals=0),
        name=name,
    )(*given)


def in_hbm(array):
    return pltpu.with_memory_space_constraint(array, pltpu.HBM)


def from_section(block):
    return lax.ppermute(block, "section", [(0, 1), (1, 0)])


def from_dp(block, mask):
    count = lax.axis_size("dp")
    return lax.ppermute(block, "dp", [(place, place ^ mask) for place in range(count)])


def from_dp_of(block, mask, side):
    count = lax.axis_size("dp")
    first = side * count
    route = [(first + place, first + (place ^ mask)) for place in range(count)]
    return lax.ppermute(block, ("section", "dp"), route)


def small_call(kernel, name, outs, *given):
    vmem = pl.BlockSpec(memory_space=pltpu.VMEM)
    size = sum(member.size * member.dtype.itemsize for member in given)
    return pl.pallas_call(
        kernel,
        in_specs=[vmem] * len(given),
        out_specs=[vmem] * len(outs),
        out_shape=[jax.ShapeDtypeStruct(shape, HALF) for shape in outs],
        compiler_params=pltpu.CompilerParams(vmem_limit_bytes=VMEM_BYTES),
        cost_estimate=pl.CostEstimate(flops=0, bytes_accessed=2 * size, transcendentals=0),
        name=name,
    )(*given)


def total_of(*values):
    total = values[0].astype(FULL)
    for value in values[1:]:
        total = total + value.astype(FULL)
    return low(total)


PLANE, DEPTH = (1, 2, 3), (4, 8, 12)


def groups_of(masks):
    count = lax.axis_size("dp")
    return [[place ^ mask for mask in (0,) + masks] for place in range(count) if place & masks[2] == 0]


def exchange(blocks, masks):
    return [blocks[0]] + [from_dp(block, mask) for block, mask in zip(blocks[1:], masks)]


def add_cores(name, batches):
    rows = sum(kept.shape[1] for kept, _ in batches)
    width = batches[0][0].shape[2]

    def kernel(*refs):
        outs = refs[-4:]
        for chunk in range(CHUNKS):
            start = 0
            for number in range(len(batches)):
                value = total_of(refs[2 * number][chunk], refs[2 * number + 1][chunk])
                outs[chunk % 4][chunk // 4, start : start + value.shape[0], :] = value
                start += value.shape[0]

    flat = [member for batch in batches for member in batch]
    return small_call(kernel, name + "_cores", [(CHUNKS // 4, rows, width)] * 4, *flat)


def exchange_whole(blocks, masks):
    return lax.all_to_all(
        blocks, "dp", split_axis=0, concat_axis=0, tiled=True, axis_index_groups=groups_of(masks)
    )


def split_cores(name, kept, got):
    half, width = kept.shape[1] // 2, kept.shape[2]

    def kernel(kept_ref, got_ref, *outs):
        for chunk in range(CHUNKS):
            deep, first, second = chunk // 4, chunk & 1, (chunk >> 1) & 1
            value = total_of(kept_ref[chunk], got_ref[chunk])
            outs[first][second, deep] = value[:half]
            outs[2 + second][first, deep] = value[half:]

    return small_call(kernel, name + "_cores", [(2, CHUNKS // 4, half, width)] * 4, kept, got)


def split_again(name, upper, lower):
    shape = upper[0].shape[1:]

    def kernel(*refs):
        for part in range(2):
            for side in range(2):
                refs[4 + 2 * part + side][...] = total_of(refs[2 * part][side], refs[2 * part + 1][side])

    return small_call(kernel, name + "_half", [shape] * 4, *upper, *lower)


def join_split(name, upper, lower, joined):
    half, rows = upper[0].shape[1], 2 * upper[0].shape[1]
    shape = (rows + joined.shape[1], joined.shape[2])

    def kernel(*refs):
        for place in range(4):
            out = refs[5 + place]
            out[:half, :] = total_of(refs[0][place], refs[1][place])
            out[half:rows, :] = total_of(refs[2][place], refs[3][place])
            out[rows:, :] = refs[4][place]

    return small_call(kernel, name + "_plane", [shape] * 4, *upper, *lower, joined)


def stack_plane(name, members):
    def kernel(*refs):
        for place in range(4):
            refs[-1][place] = total_of(*[ref[place] for ref in refs[:4]])

    return small_call(kernel, name + "_plane", [members[0].shape], *members)[0]


def add_stacked(name, members):
    def kernel(source, out):
        out[...] = total_of(*[source[place] for place in range(4)])

    return small_call(kernel, name + "_depth", [members.shape[1:]], members)[0]


def add_plane(name, members, joined=None, shared=None):
    rows = members[0].shape[1]
    middle = rows + (joined.shape[1] if joined is not None else 0)
    end = middle + (shared.shape[0] if shared is not None else 0)
    given = list(members) + [extra for extra in (joined, shared) if extra is not None]

    def kernel(*refs):
        for place in range(4):
            out = refs[-4 + place]
            out[:rows, :] = total_of(*[ref[place] for ref in refs[:4]])
            if middle > rows:
                out[rows:middle, :] = refs[4][place]
            if end > middle:
                out[middle:, :] = refs[len(given) - 1][...]

    return small_call(kernel, name + "_plane", [(end, members[0].shape[2])] * 4, *given)


def add_depth(name, members, rows=None):
    shape = (rows or members[0].shape[0], members[0].shape[1])

    def kernel(*refs):
        refs[-1][...] = total_of(*[ref[: shape[0], :] for ref in refs[:4]])

    return small_call(kernel, name + "_depth", [shape], *members)[0]


def add_far(chunk):
    bit = CHUNKS
    while bit < lax.axis_size("dp"):
        chunk = total_of(chunk, from_dp(chunk, bit))
        bit = 2 * bit
    return chunk


def gather_depth_for(chunk, side):
    own = jnp.stack([chunk, from_section(chunk)])
    return jnp.stack([own] + [from_dp_of(own, mask, side) for mask in DEPTH])


def gather_plane_for(deep, side):
    return [deep] + [from_dp_of(deep, mask, side) for mask in PLANE]


def join_cores(name, batches):
    rows = sum(kept.shape[1] for kept, _ in batches)
    width = batches[0][0].shape[2]

    def kernel(*refs):
        def step(chunk, carry):
            start = 0
            for number in range(len(batches)):
                value = total_of(refs[2 * number][chunk], refs[2 * number + 1][chunk])
                refs[-1][chunk, start : start + value.shape[0], :] = value
                start += value.shape[0]
            return carry

        lax.fori_loop(0, CHUNKS, step, 0, unroll=2)

    flat = [member for batch in batches for member in batch]
    return small_call(kernel, name + "_cores", [(CHUNKS, rows, width)], *flat)[0]


def scatter_group(blocks, masks):
    total = lax.psum_scatter(
        blocks.reshape(-1, blocks.shape[-1]),
        "dp",
        scatter_dimension=0,
        tiled=True,
        axis_index_groups=groups_of(masks),
    )
    return total.reshape(blocks.shape[1:])


def gather_group(block, masks):
    joined = lax.all_gather(
        block.reshape(-1, block.shape[-1]),
        "dp",
        axis=0,
        tiled=True,
        axis_index_groups=groups_of(masks),
    )
    return joined.reshape((4,) + block.shape)


def store_segments(outs, segments, block, piece, rows):
    for offset, size, target, column in segments:
        if offset < rows:
            place = pl.ds(pl.multiple_of(block * size, 16), size)
            values = piece[offset : offset + size, :]
            outs[target][place, column : column + values.shape[1]] = values.astype(FULL)


def unpack_kernel(feed_segments, attention_segments, segments, where, *refs):
    encoder, decoder, outs, small_out = refs[:4], refs[4:8], refs[8:-1], refs[-1]
    few = small_out.shape[1]
    rows = feed_segments[-1][0] + feed_segments[-1][1] + attention_segments[-1][0] + attention_segments[-1][1]
    attention_rows = rows - decoder[0].shape[2]

    @pl.when(where[0] == 0)
    def _():
        for flat in range(4):
            for side in range(2):
                block = 2 * jnp.bitwise_xor(flat, where[1] & 3) + side
                piece = encoder[flat].at[0, side]
                store_segments(outs, segments, block, piece, rows)
                small_out[block] = piece[rows : rows + 2 * few, :].astype(FULL)[:few]

    @pl.when(where[0] != 0)
    def _():
        for flat in range(4):
            for side in range(2):
                block = 2 * flat + jnp.bitwise_xor(where[0], side)
                piece = decoder[2 * side].at[flat, 0]
                store_segments(outs, feed_segments, block, piece, piece.shape[0])
                piece = decoder[2 * side + 1].at[flat, 0]
                store_segments(outs, attention_segments, block, piece, attention_rows)
                small_out[block] = piece[attention_rows : attention_rows + 2 * few, :].astype(FULL)[:few]


def after(value, *others):
    return lax.optimization_barrier((value, others))[0]


FEED = ["ln1_gain", "ln1_shift", "qkv_w", "out_w", "ln2_gain", "ln2_shift", "up_w", "up_shift", "down_w"]
ENDS = ["final_gain", "final_shift", "bridge"]


def picked(weights, names):
    return [weights[name] for name in names]


class Sizes:
    def __init__(self, width, hidden, groups, rows):
        self.groups, self.rows, self.width, self.hidden = groups, rows, width, hidden
        blocks = 2 * CHUNKS
        self.down_rows = self.hidden // blocks
        self.thin_rows = self.width // blocks
        self.up_parts = self.hidden // self.width
        self.feed_rows = self.down_rows + self.up_parts * self.thin_rows
        self.attention_rows = 4 * self.thin_rows
        self.small_rows = 16
        rows, width = self.rows, self.width
        self.qkv = Token((3 * PAIRS, rows, LANES), HALF)
        self.lse = Token((HEADS, rows), FULL)
        self.mixed = Token((PAIRS, rows, LANES), HALF)
        self.wide = Token((rows, width), FULL)
        self.wide_low = Token((rows, width), HALF)
        self.hidden_low = Token((rows, self.hidden), HALF)
        self.parked_qkv = Parked((3 * PAIRS, rows, LANES), HALF)
        self.parked_mixed = Parked((PAIRS, rows, LANES), HALF)
        self.parked_wide = Parked((rows, width), FULL)
        self.parked_hidden = Parked((rows, self.hidden), HALF)
        self.latent = Token((rows, LANES), FULL)
        self.latent_low = Token((rows, LANES), HALF)
        self.feed_blocks = Whole((CHUNKS, self.feed_rows, width), HALF)
        self.two_vectors = Whole((2, width), FULL)
        self.feed_vector = Whole((4 + self.up_parts, width), FULL)
        self.bridge = Whole((LANES, width), FULL)
        self.bias_scratch = pltpu.VMEM((rows, rows), FULL)
        self.lse_scratch = pltpu.VMEM((rows, LANES), FULL)
        self.wide_scratch = pltpu.VMEM((rows, width), FULL)
        self.low_scratch = pltpu.VMEM((rows, width), HALF)
        self.mixed_scratch = pltpu.VMEM((PAIRS, rows, LANES), HALF)
        self.qkv_scratch = pltpu.VMEM((3 * PAIRS, rows, LANES), HALF)
        self.hidden_scratch = pltpu.VMEM((rows, self.hidden), HALF)
        self.feed_sums = [
            pltpu.VMEM((self.hidden, width), FULL),
            pltpu.VMEM((width, self.hidden), FULL),
            pltpu.VMEM((1, self.hidden), FULL),
        ]
        self.qkv_sum = pltpu.VMEM((width, 3 * width), FULL)
        self.out_sum = pltpu.VMEM((width, width), FULL)
        self.small_sum = pltpu.VMEM((blocks, self.small_rows, width), FULL)

    def blocks(self, rows):
        return [Whole((CHUNKS, rows, self.width), HALF)] * 2


def encoder_mix(z, lengths, where, patch, weights):
    return run_groups(
        encoder_mix_kernel,
        "encoder_mix",
        z.groups,
        [lengths],
        [patch],
        picked(weights, FEED[:4]),
        [z.parked_qkv, z.lse, z.parked_mixed, z.wide],
        [z.bias_scratch, z.lse_scratch, z.low_scratch],
        10 << 30,
        24,
        where,
        0,
    )


def encoder_latent(z, where, middle, weights):
    return run_groups(
        encoder_latent_kernel,
        "encoder_latent",
        z.groups,
        [],
        [middle],
        picked(weights, FEED[4:] + ENDS),
        [z.parked_hidden, z.parked_hidden, z.parked_wide, z.latent],
        [z.low_scratch],
        12 << 30,
        30,
        where,
        0,
    )


def quantize(z, places, block, latent, pieces):
    count = z.groups * z.rows
    vmem = pl.BlockSpec(memory_space=pltpu.VMEM)
    rows = len(pieces) * pieces[0].shape[0]
    quant, book = pl.pallas_call(
        quant_kernel,
        in_specs=[pl.BlockSpec(memory_space=pltpu.SMEM), vmem, vmem]
        + [pl.BlockSpec(memory_space=pl.ANY)] * len(pieces),
        out_specs=[vmem, vmem],
        out_shape=[
            jax.ShapeDtypeStruct((count, LANES), HALF),
            jax.ShapeDtypeStruct((rows, LANES), FULL),
        ],
        scratch_shapes=[
            pltpu.VMEM((rows, LANES), FULL),
            pltpu.VMEM((count, LANES), FULL),
            pltpu.VMEM((count, LANES), FULL),
            pltpu.SemaphoreType.DMA((len(pieces),)),
        ]
        + [pltpu.VMEM((rows, LANES), FULL)] * 3,
        compiler_params=pltpu.CompilerParams(vmem_limit_bytes=VMEM_BYTES),
        cost_estimate=pl.CostEstimate(flops=8 << 30, bytes_accessed=0, transcendentals=0),
        name="quantize",
    )(places, block.reshape(count, 1), latent.reshape(count, LANES), *pieces)
    return quant.reshape(z.groups, z.rows, LANES), book


def decoder_mix(z, lengths, where, quant, weights):
    return run_groups(
        decoder_mix_kernel,
        "decoder_mix",
        z.groups,
        [lengths],
        [quant],
        picked(weights, FEED[:4] + ENDS[2:]),
        [z.parked_qkv, z.lse, z.parked_mixed, z.wide],
        [z.bias_scratch, z.lse_scratch, z.low_scratch, z.wide_scratch],
        10 << 30,
        26,
        where,
        1,
    )


def decoder_feed(z, where, middle, cotangent, weights):
    return run_groups(
        decoder_feed_kernel,
        "decoder_feed_both",
        z.groups,
        [where],
        [middle, cotangent],
        picked(weights, FEED[4:] + ENDS[:2]),
        [z.wide_low, z.parked_wide, z.feed_blocks, z.feed_blocks, z.feed_vector],
        [z.hidden_scratch, z.hidden_scratch, z.low_scratch, z.low_scratch, z.wide_scratch, z.wide_scratch]
        + z.feed_sums,
        28 << 30,
        36,
        where,
        1,
    )


def decoder_input(z, where, quant, grad_middle, grad_qkv, sums, weights, book, book_rows, latent, owners, per_owner):
    return run_groups(
        functools.partial(decoder_input_kernel, owners=owners, per_owner=per_owner, latent=latent),
        "decoder_input_backward",
        z.groups,
        [where],
        [quant, grad_middle, in_hbm(grad_qkv)],
        picked(weights, FEED[:3] + ENDS[2:]) + [book, in_hbm(sums[0]), sums[1]],
        [z.latent_low]
        + z.blocks(z.attention_rows + z.small_rows + book_rows)
        + [z.two_vectors, z.bridge],
        [z.qkv_sum, z.low_scratch, z.wide_scratch, z.wide_scratch, z.low_scratch, z.small_sum],
        8 << 30,
        28,
        where,
        1,
    )


def encoder_feed(z, where, grad_quant, middle, result, slope, active, weights):
    return run_groups(
        encoder_feed_kernel,
        "encoder_feed_backward",
        z.groups,
        [where],
        [grad_quant, middle, in_hbm(result), in_hbm(slope), in_hbm(active)],
        picked(weights, FEED[4:7] + FEED[8:] + ENDS),
        [z.parked_wide, z.feed_blocks, z.feed_blocks, z.feed_vector, z.bridge],
        [z.low_scratch, z.low_scratch, z.wide_scratch, z.wide_scratch] + z.feed_sums,
        20 << 30,
        36,
        where,
        0,
    )


def attention_gradient(z, name, side, lengths, where, grad_middle, saved, weights):
    return run_groups(
        attention_backward_kernel,
        name,
        z.groups,
        [lengths],
        [in_hbm(grad_middle), saved[0], saved[1], in_hbm(saved[2])],
        picked(weights, ["out_w"]),
        [z.parked_qkv, ParkedWhole((z.width, z.width), FULL)],
        [z.bias_scratch, z.mixed_scratch],
        20 << 30,
        26,
        where,
        side,
    )


def encoder_input(z, where, patch, grad_middle, grad_qkv, sums, weights, latent):
    return run_groups(
        functools.partial(encoder_input_kernel, latent=latent),
        "encoder_input_backward",
        z.groups,
        [where],
        [in_hbm(patch), in_hbm(grad_middle), in_hbm(grad_qkv)],
        picked(weights, FEED[:3]) + [in_hbm(sums[0])] + sums[1:],
        [z.wide_low] + z.blocks(z.attention_rows + z.small_rows) + [z.two_vectors],
        [z.qkv_sum, z.low_scratch, z.wide_scratch, z.small_sum],
        8 << 30,
        24,
        where,
        0,
    )


def on_device(
    section_in,
    ln1_gain,
    ln1_shift,
    qkv_weight,
    out_weight,
    ln2_gain,
    ln2_shift,
    up_weight,
    up_shift,
    down_weight,
    final_gain,
    final_shift,
    bridge_weight,
    codebook,
    codes,
    doc_lengths,
):
    section = lax.axis_index("section")
    encoder_side = section == 0
    micro = doc_lengths.shape[0]
    groups = micro // 2
    rows = section_in.shape[1] // micro
    width = section_in.shape[2]
    hidden_width = up_weight.shape[2]
    latent_width = bridge_weight.shape[1]
    per_device = codebook.shape[1]

    count = lax.axis_size("dp")
    dp = lax.axis_index("dp")
    where = jnp.stack([section, dp & (CHUNKS - 1), dp >> (CHUNKS.bit_length() - 1)]).astype(jnp.int32)

    inverse = lax.rsqrt(jnp.sum(codebook * codebook, axis=0, keepdims=True) + EPS)
    unit_codes = codebook * inverse
    quarter = per_device // 4
    packed = (
        unit_codes.reshape(latent_width, 4, quarter).transpose(2, 1, 0).reshape(quarter, 4 * latent_width)
    )
    deep_table = [packed] + [from_dp(packed, mask) for mask in DEPTH]

    vectors = jnp.concatenate(
        [ln1_gain, ln1_shift, ln2_gain, ln2_shift, final_gain, final_shift]
        + [up_shift.reshape(-1, width), bridge_weight[0].astype(FULL)],
        axis=0,
    )
    qkv_w, out_w, up_w, down_w = qkv_weight[0], out_weight[0], up_weight[0], down_weight[0]
    halves = section_in[0].reshape(2, groups, rows, width)
    other_halves = from_section(section_in[0]).reshape(halves.shape)
    other_vectors, other_qkv, other_out = from_section(vectors), from_section(qkv_w), from_section(out_w)
    patch = jnp.where(encoder_side, halves[0], other_halves[1])
    cotangent = jnp.where(encoder_side, other_halves[0], halves[1])
    lengths = lax.dynamic_slice_in_dim(doc_lengths, section * groups, groups, 0)
    own_codes = lax.dynamic_slice_in_dim(codes, section * groups * rows, groups * rows, 0)
    owner, within = own_codes // per_device, own_codes % per_device
    apart = (owner % count) ^ dp
    place = ((owner // count) ^ section) * count + (apart & -CHUNKS) + 4 * (apart & 3) + ((apart >> 2) & 3)
    places = place * quarter + within % quarter
    code_block = within // quarter
    deep_table, patch, cotangent, other_vectors, other_qkv, other_out = lax.optimization_barrier(
        (deep_table, patch, cotangent, other_vectors, other_qkv, other_out)
    )
    hidden_rows = hidden_width // width

    def vectors_of(vector):
        return dict(
            ln1_gain=vector[0:1],
            ln1_shift=vector[1:2],
            qkv_w=(qkv_w, other_qkv),
            out_w=(out_w, other_out),
            ln2_gain=vector[2:3],
            ln2_shift=vector[3:4],
            up_shift=vector[6 : 6 + hidden_rows].reshape(1, hidden_width),
            final_gain=vector[4:5],
            final_shift=vector[5:6],
            bridge=jnp.pad(low(vector[6 + hidden_rows :]), ((0, LANES - latent_width), (0, 0))),
        )

    encoder = vectors_of(jnp.where(encoder_side, vectors, other_vectors))
    decoder = vectors_of(jnp.where(encoder_side, other_vectors, vectors))
    z = Sizes(width, hidden_width, groups, rows)
    deep_table = jnp.concatenate(deep_table, axis=0)
    table = [deep_table] + [from_dp(deep_table, mask) for mask in PLANE]
    other_up, other_down = from_section(up_w), from_section(down_w)
    encoded = encoder_mix(z, lengths, where, patch, encoder)
    table, other_up, other_down, encoded = lax.optimization_barrier((table, other_up, other_down, encoded))
    qkv_e, lse_e, mixed_e, middle_e = encoded
    encoder.update(up_w=(up_w, other_up), down_w=(down_w, other_down))
    decoder.update(up_w=(up_w, other_up), down_w=(down_w, other_down))
    bit = CHUNKS
    while bit < count:
        table = table + [from_dp(piece, bit) for piece in table]
        bit = 2 * bit
    table = table + [from_section(piece) for piece in table]
    encoded = encoder_latent(z, where, middle_e, encoder)
    table, encoded = lax.optimization_barrier((table, encoded))
    slope_e, active_e, result_e, latent = encoded
    quant, book = quantize(z, places, code_block, latent, table)
    feed_rows, attention_rows = z.feed_rows, z.attention_rows
    book_rows = 4 * latent_width * (lax.axis_size("dp") // CHUNKS) * quarter // width
    qkv_d, lse_d, mixed_d, middle = decoder_mix(z, lengths, where, quant, decoder)
    final, middle_d, keep_1, send_1, vectors_1 = decoder_feed(z, where, middle, cotangent, decoder)
    got_1 = from_section(send_1)
    decoder_mixed = attention_gradient(
        z, "decoder_attention_backward", 1, lengths, where, middle_d, (qkv_d, lse_d, mixed_d), decoder
    )
    got_1, decoder_mixed = lax.optimization_barrier((got_1, decoder_mixed))
    grad_qkv_d, out_sum_d = decoder_mixed
    plane_1 = add_cores("decoder_feed", [(keep_1, got_1)])
    moved_1 = exchange(plane_1, PLANE)
    grad_quant, keep_2, send_2, vectors_2, bridge_d = decoder_input(
        z,
        where,
        quant,
        middle_d,
        after(grad_qkv_d, plane_1[0]),
        [out_sum_d, vectors_1],
        decoder,
        book,
        book_rows,
        latent_width,
        lax.axis_size("dp"),
        quarter,
    )
    got_2 = from_section(send_2)
    middle_grad, keep_3, send_3, vectors_3, bridge_e = encoder_feed(
        z, where, grad_quant, middle_e, result_e, slope_e, active_e, encoder
    )
    moved_1, got_2, middle_grad, keep_3, send_3, vectors_3, bridge_e = lax.optimization_barrier(
        (moved_1, got_2, middle_grad, keep_3, send_3, vectors_3, bridge_e)
    )
    got_3 = from_section(send_3)
    depth_1 = stack_plane("decoder_feed", moved_1)
    joined_2 = join_cores("decoder_attention", [(keep_2, got_2)])
    depth_2 = scatter_group(joined_2.reshape((4, CHUNKS // 4) + joined_2.shape[1:]), PLANE)
    upper, upper_sent, lower, lower_sent = split_cores("encoder_feed", keep_3, got_3)

    middle_grad = after(middle_grad, upper, joined_2, depth_1)
    upper_got, lower_got = from_dp(upper_sent, 1), from_dp(lower_sent, 2)
    deep_1 = exchange_whole(depth_1, DEPTH)
    grad_qkv, out_sum = attention_gradient(
        z, "encoder_attention_backward", 0, lengths, where, middle_grad, (qkv_e, lse_e, mixed_e), encoder
    )
    upper_got, lower_got, deep_1, grad_qkv, out_sum = lax.optimization_barrier(
        (upper_got, lower_got, deep_1, grad_qkv, out_sum)
    )
    upper, upper_sent, lower, lower_sent = split_again("encoder_feed", (upper, upper_got), (lower, lower_got))
    upper_got, lower_got = from_dp(upper_sent, 2), from_dp(lower_sent, 1)
    chunk_1 = add_far(add_stacked("decoder_feed", deep_1))
    near_1 = exchange_whole(jnp.broadcast_to(chunk_1[None], (4,) + chunk_1.shape), DEPTH)
    grad_patch, keep_4, send_4, _ = encoder_input(
        z,
        where,
        patch,
        middle_grad,
        after(grad_qkv, chunk_1, upper),
        [out_sum, vectors_3, bridge_e],
        encoder,
        latent_width,
    )
    upper_got, lower_got, near_1, depth_2, grad_patch, keep_4, send_4 = lax.optimization_barrier(
        (upper_got, lower_got, near_1, depth_2, grad_patch, keep_4, send_4)
    )
    half_1 = gather_group(near_1, PLANE)

    got_4 = from_section(send_4)
    depth_3 = join_split("encoder_feed", (upper, upper_got), (lower, lower_got), depth_2)
    deep_3 = exchange(depth_3, DEPTH)
    plane_4 = add_cores("encoder_attention", [(keep_4, got_4)])
    moved_4 = exchange(plane_4, PLANE)
    deep_3, moved_4 = lax.optimization_barrier((deep_3, moved_4))
    chunk_3 = add_far(add_depth("encoder_feed", deep_3))
    used_rows = attention_rows + z.small_rows
    depth_4 = add_plane("encoder_attention", moved_4, shared=chunk_3[feed_rows : feed_rows + used_rows])
    deep_4 = lax.optimization_barrier(exchange(depth_4, DEPTH))
    chunk_4 = add_far(add_depth("encoder_attention", deep_4, used_rows))
    grad_patch = after(grad_patch, chunk_4)
    sent = jnp.where(encoder_side, final, grad_patch)
    kept = jnp.where(encoder_side, grad_patch, final)
    chunk_e = jnp.concatenate([chunk_3[:feed_rows], chunk_4], axis=0)
    deep_e = gather_depth_for(chunk_e, 0)
    near_2 = jnp.stack([piece[used_rows:] for piece in deep_4])
    half_1, near_2 = lax.optimization_barrier((half_1, near_2))
    half_2 = gather_group(near_2, PLANE)
    deep_e = lax.optimization_barrier(deep_e)
    got = from_section(sent)
    book_sum = chunk_3[feed_rows + attention_rows + z.small_rows :].astype(FULL)
    book_sum = book_sum.reshape(book_rows, 4, LANES).transpose(1, 0, 2).reshape(-1, quarter, LANES)
    book_own = lax.dynamic_index_in_dim(book_sum, lax.axis_index("dp") // CHUNKS, 0, keepdims=False)
    book_grad = (
        book_own.reshape(quarter, 4, latent_width).transpose(2, 1, 0).reshape(latent_width, per_device)
    )
    book_grad = inverse * (
        book_grad - unit_codes * jnp.sum(unit_codes * book_grad, axis=0, keepdims=True)
    )

    section_out = jnp.where(
        encoder_side, jnp.concatenate([kept, got], axis=0), jnp.concatenate([got, kept], axis=0)
    ).reshape(1, micro * rows, width)
    gathered = gather_plane_for(deep_e, 0)
    halves_d = [half_1, half_2]
    halves_d = halves_d + [lax.ppermute(half, "section", [(0, 1)]) for half in halves_d]

    feed_segments = [(0, z.down_rows, 0, 0)] + [
        (z.down_rows + part * z.thin_rows, z.thin_rows, 1, part * width) for part in range(z.up_parts)
    ]
    attention_segments = [(0, z.thin_rows, 3, 0)] + [
        ((part + 1) * z.thin_rows, z.thin_rows, 2, part * width) for part in range(3)
    ]
    segments = feed_segments + [
        (feed_rows + offset, size, target, column) for offset, size, target, column in attention_segments
    ]
    gathered, section_out, book_grad = lax.optimization_barrier((gathered, section_out, book_grad))
    given = gathered + list(halves_d)
    vmem = pl.BlockSpec(memory_space=pltpu.VMEM)
    shapes = [(hidden_width, width), (width, hidden_width), (width, 3 * width), (width, width)]
    shapes.append((2 * CHUNKS, z.small_rows // 2, width))

    def part_of(shape):
        rest = (0,) * (len(shape) - 1)
        return pl.BlockSpec((shape[0] // 4,) + shape[1:], lambda depth, place: (depth,) + rest)

    def near(depth, place, side):
        return jnp.where(place[0] == side, jnp.bitwise_xor(depth, place[1] >> 2), 0)

    def same(depth, place, side):
        return jnp.where(place[0] == side, depth, 0)

    def deep_part(array):
        return pl.BlockSpec((1,) + array.shape[1:], lambda depth, place: (near(depth, place, 0), 0, 0, 0))

    def half_part(array, index):
        shape = (array.shape[0], 1) + array.shape[2:]
        return pl.BlockSpec(shape, lambda depth, place: (0, index(depth, place, 1), 0, 0))

    in_specs = [deep_part(piece) for piece in given[:4]]
    in_specs += [half_part(half, index) for half, index in zip(given[4:], (same, near, same, near))]
    down_total, up_total, qkv_total, out_total, small = pl.pallas_call(
        functools.partial(unpack_kernel, feed_segments, attention_segments, segments),
        grid_spec=pltpu.PrefetchScalarGridSpec(
            num_scalar_prefetch=1,
            grid=(4,),
            in_specs=in_specs,
            out_specs=[part_of(shape) for shape in shapes],
        ),
        out_shape=[jax.ShapeDtypeStruct(shape, FULL) for shape in shapes],
        compiler_params=pltpu.CompilerParams(vmem_limit_bytes=30 << 20),
        name="unpack",
    )(where, *given)

    small_count = 2 + 4 + z.up_parts + latent_width
    small = small[:, : -(-small_count // (2 * CHUNKS))].reshape(-1, width)

    first_vector = 2
    hidden_vector = first_vector + 4
    return (
        section_out,
        small[0:1],
        small[1:2],
        qkv_total[None],
        out_total[None],
        small[2:3],
        small[3:4],
        up_total[None],
        small[hidden_vector : hidden_vector + z.up_parts].reshape(1, hidden_width),
        down_total[None],
        small[4:5],
        small[5:6],
        small[hidden_vector + z.up_parts : hidden_vector + z.up_parts + latent_width][None],
        book_grad,
    )


def solution(mesh):
    placed = (
        P("section", "dp", None),
        P("section", None),
        P("section", None),
        P("section", None, None),
        P("section", None, None),
        P("section", None),
        P("section", None),
        P("section", None, None),
        P("section", None),
        P("section", None, None),
        P("section", None),
        P("section", None),
        P("section", None, None),
        P(None, ("section", "dp")),
        P("dp"),
        P("dp", None),
    )
    return jax.shard_map(
        on_device,
        mesh=mesh,
        in_specs=placed,
        out_specs=(
            P("section", "dp", None),
            P("section", None),
            P("section", None),
            P("section", None, None),
            P("section", None, None),
            P("section", None),
            P("section", None),
            P("section", None, None),
            P("section", None),
            P("section", None, None),
            P("section", None),
            P("section", None),
            P("section", None, None),
            P(None, ("section", "dp")),
        ),
        check_vma=False,
    )
```
